128 devices in a mesh: tm: 8 (over y, core), row: 8 (over z_lo, x), col: 2 (over z_hi).
Axes of the slice: x: 4, y: 4, z: 4 (z_hi: 2, z_lo: 2; z = z_hi * 2 + z_lo), core: 2. Of those that a mesh axis runs over, the one named last changes fastest.
Arguments:
- paths: bfloat16 [8, 1024, 6144], P('tm', 'row', 'col'), may hold values from -18 to 18
- prev_drift: bfloat16 [8, 1024, 6144], P('tm', 'row', 'col'), may hold values from -6 to 6
- boundary: bfloat16 [2, 1024, 6144], P(None, 'row', 'col'), may hold values from -6 to 6
- step_scale: float32 [8], P('tm'), may hold values from 0.3 to 3
- time_ids: int32 [8], P('tm'), may hold values from 0 to 63
- mod_table: bfloat16 [64, 2, 6144], P(None, None, 'col'), may hold values from -1.796875 to 1.796875
- w_qkv: bfloat16 [6144, 3, 3072], P('col', None, 'row'), may hold values from -2 to 2
- output_weight: bfloat16 [3072, 6144], P('row', 'col'), may hold values from -0.109375 to 0.109375
Outputs:
- grad_w_qkv: float32 [6144, 3, 3072], P(('col', 'tm'), None, 'row')
- grad_w_out: float32 [3072, 6144], P('row', ('col', 'tm'))
The draws below stay inside these ranges and needn't reach their ends.
All inputs are finite; a program needn't handle non-finite values.
Results may differ from the reference program's by a relative error of at most 0.013.
Values may be sent and summed in bfloat16 or wider, within the bound.
A program may use at most 128 MiB of HBM per device.

```python
import math
import jax
import jax.numpy as jnp
from jax import lax

D = 6144
H = 24
HEAD_DIM = 128
L = 1024
NT = 64
STEPS_DEV = 1
HW = 3072
TIMES = 8
N_TM = 8
N_ROW = 8


def draw_w_qkv(key, part):
    values = jax.random.normal(jax.random.fold_in(key, 11), (D, 3, HW), jnp.float32) * D ** (-0.5)
    values = jnp.clip(values, -6.0 * D ** (-0.5), 6.0 * D ** (-0.5))
    return values.astype(jnp.bfloat16)


def draw_paths(key, part):
    position = jnp.arange(D).astype(jnp.float32) / (D - 1)
    values = jnp.clip(jax.random.normal(jax.random.fold_in(key, 23), (TIMES, L, D), jnp.float32), -4.0, 4.0)
    feature_scale = jnp.exp(position * 1.386294)
    return (values * feature_scale).astype(jnp.bfloat16)


def plant(entries, own_key, least, high):
    spot = [jax.random.randint(jax.random.fold_in(own_key, axis), (), 0, length) for axis, length in enumerate(entries.shape)]
    main_axis = entries.shape.index(max(entries.shape))
    beside = spot[:main_axis] + [(spot[main_axis] + 1) % entries.shape[main_axis]] + spot[main_axis + 1:]
    return entries.at[tuple(spot)].set(least).at[tuple(beside)].set(high)


def block_scale(rng, extent, pieces, low, high):
    level, own = 1.0, jax.random.fold_in(rng, 6)
    for dim, parts in pieces:
        steps = jnp.exp(jax.random.uniform(jax.random.fold_in(own, dim), (parts,), jnp.float32, low / len(pieces), high / len(pieces)))
        level = level * jnp.repeat(steps, extent[dim] // parts).reshape([-1 if axis == dim else 1 for axis in range(len(extent))])
    return level


def scatter_about(key, shape, deviation, most, shards=(), kind=jnp.bfloat16):
    values = jax.random.normal(key, shape, jnp.float32) * deviation
    if len(shards) > 0:
        values = block_scale(key, shape, shards, -0.22, 0.18) * values
    return jnp.clip(values, min=-most, max=most).astype(kind)


def setup_inputs(seed: int = 0) -> dict:
    key_of = jax.random.split(jax.random.key(seed), 9)
    paths = draw_paths(jax.random.fold_in(key_of[8], 71), 0)
    prev_drift = scatter_about(key_of[1], (TIMES, L, D), 1.0, 6.0, ((0, 8), (1, 8), (2, 2)))
    boundary = scatter_about(key_of[2], (2, L, D), 1.0, 6.0, ((1, 8), (2, 2)))
    step_scale = jnp.clip(jnp.exp(math.log(3.0) - 2.3025851 * jax.random.uniform(key_of[3], (TIMES,), jnp.float32) ** block_scale(key_of[3], (TIMES,), ((0, 8),), -0.2, 0.2)), 0.3, 3.0)
    time_ids = plant(jax.random.randint(key_of[4], (TIMES,), 0, NT), jax.random.fold_in(key_of[4], 1), 0, NT - 1).astype(jnp.int32)
    mod_table = scatter_about(key_of[5], (NT, 2, D), 0.3, 1.796875, ((2, 2),))
    w_qkv = draw_w_qkv(jax.random.fold_in(key_of[8], 71), 0)
    output_weight = scatter_about(key_of[7], (HW, D), HW ** -0.5, 0.109375, ((0, 8), (1, 2)))
    return dict(paths=paths, prev_drift=prev_drift, boundary=boundary, step_scale=step_scale, time_ids=time_ids, mod_table=mod_table, w_qkv=w_qkv, output_weight=output_weight)


norm_eps = 1e-06

def attend_head(operands):
    query_rows, key_rows, value_rows = operands
    scores = jnp.dot(query_rows, key_rows.T, preferred_element_type=jnp.float32) * HEAD_DIM ** (-0.5)
    weights = jax.nn.softmax(scores, axis=-1)
    weights_low = weights.astype(jnp.bfloat16)
    mixed_rows = jnp.dot(weights_low, value_rows, preferred_element_type=jnp.float32).astype(jnp.bfloat16)
    return (mixed_rows, weights)

def head_grads(operands):
    query_rows, key_rows, value_rows, weights, upstream = operands
    weights_low = weights.astype(jnp.bfloat16)
    grad_value = jnp.dot(weights_low.T, upstream, preferred_element_type=jnp.float32).astype(jnp.bfloat16)
    grad_weights = jnp.dot(upstream, value_rows.T, preferred_element_type=jnp.float32)
    inner_sum = lax.optimization_barrier(jnp.sum(grad_weights * weights, axis=-1, keepdims=True))
    grad_scores = (weights * (grad_weights - inner_sum) * HEAD_DIM ** (-0.5)).astype(jnp.bfloat16)
    grad_query = jnp.dot(grad_scores, key_rows, preferred_element_type=jnp.float32).astype(jnp.bfloat16)
    grad_key = jnp.dot(grad_scores.T, query_rows, preferred_element_type=jnp.float32).astype(jnp.bfloat16)
    return (grad_query, grad_key, grad_value)

def step_grads(state, prev_state, drift_before, drift_now, scale_now, time_now, mod_table, w_qkv, output_weight):
    target = prev_state.astype(jnp.float32) + scale_now * (drift_before.astype(jnp.float32) - drift_now.astype(jnp.float32))
    onehot = (jnp.arange(NT) == time_now).astype(jnp.float32)
    modulation = jnp.dot(onehot, mod_table.reshape(NT, 2 * D).astype(jnp.float32), precision=lax.Precision.HIGHEST).reshape(2, D)
    state_f = state.astype(jnp.float32)
    mean_sq = lax.optimization_barrier(jnp.mean(state_f * state_f, axis=-1, keepdims=True))
    normed = (state_f * lax.rsqrt(mean_sq + norm_eps) * (1.0 + modulation[0]) + modulation[1]).astype(jnp.bfloat16)
    projected = jnp.dot(normed, w_qkv.reshape(D, 3 * HW), preferred_element_type=jnp.float32).astype(jnp.bfloat16)
    heads_first = jnp.transpose(projected.reshape(L, 3, H, HEAD_DIM), (1, 2, 0, 3))
    mixed_heads, weights = lax.map(attend_head, (heads_first[0], heads_first[1], heads_first[2]))
    mixed_rows = jnp.transpose(mixed_heads, (1, 0, 2)).reshape(L, HW)
    blocks_left = mixed_rows.reshape(L, N_ROW, HW // N_ROW).astype(jnp.float32)
    blocks_right = output_weight.reshape(N_ROW, HW // N_ROW, D).astype(jnp.float32)
    row_parts = jnp.einsum('lrh,rhd->rld', blocks_left, blocks_right)
    rounded_parts = lax.optimization_barrier(row_parts.astype(jnp.bfloat16))
    mix_out = lax.optimization_barrier(jnp.sum(rounded_parts.astype(jnp.float32), axis=0))
    output = state_f + mix_out
    upstream = ((output - target) * L ** (-0.5)).astype(jnp.bfloat16)
    output_gradient = jnp.dot(mixed_rows.T, upstream, preferred_element_type=jnp.float32)
    grad_mixed = jnp.dot(upstream, output_weight.T, preferred_element_type=jnp.float32).astype(jnp.bfloat16)
    grad_heads = jnp.transpose(grad_mixed.reshape(L, H, HEAD_DIM), (1, 0, 2))
    grad_query, grad_key, grad_value = lax.map(head_grads, (heads_first[0], heads_first[1], heads_first[2], weights, grad_heads))
    query_key_value_gradient = jnp.transpose(jnp.stack([grad_query, grad_key, grad_value]), (2, 0, 1, 3)).reshape(L, 3 * HW)
    input_gradient = jnp.dot(normed.T, query_key_value_gradient, preferred_element_type=jnp.float32).reshape(D, 3, HW)
    return (input_gradient, output_gradient)

def reference(paths, prev_drift, boundary, step_scale, time_ids, mod_table, w_qkv, output_weight):
    prev_states = jnp.concatenate([boundary[0:1], paths[:-1]], axis=0)
    prev_drifts = jnp.concatenate([boundary[1:2], prev_drift[:-1]], axis=0)

    def group_body(carry_pair, group_index):
        total_in, total_out = carry_pair
        group_in = jnp.zeros((D, 3, HW), jnp.float32)
        group_out = jnp.zeros((HW, D), jnp.float32)
        for inner_step in range(STEPS_DEV):
            step_index = group_index * STEPS_DEV + inner_step
            term_in, term_out = step_grads(paths[step_index], prev_states[step_index], prev_drifts[step_index], prev_drift[step_index], step_scale[step_index], time_ids[step_index], mod_table, w_qkv, output_weight)
            group_in = group_in + term_in
            group_out = group_out + term_out
        total_in = total_in + lax.optimization_barrier(group_in.astype(jnp.bfloat16)).astype(jnp.float32)
        total_out = total_out + lax.optimization_barrier(group_out.astype(jnp.bfloat16)).astype(jnp.float32)
        return ((total_in, total_out), None)
    start_pair = (jnp.zeros((D, 3, HW), jnp.float32), jnp.zeros((HW, D), jnp.float32))
    final_pair, unused = lax.scan(group_body, start_pair, jnp.arange(N_TM))
    return (final_pair[0], final_pair[1])
```

```python
import jax
import jax.numpy as jnp
from jax import lax
from jax.experimental import pallas as pl
from jax.experimental.pallas import tpu as pltpu
from jax.sharding import PartitionSpec as P

D = 6144
HEAD_DIM = 128
SCALE = HEAD_DIM**-0.5
MESH = pl.DeviceIdType.MESH
VMEM_LIMIT = 60 * 1024 * 1024

norm_eps = 1e-06

BF16 = jnp.bfloat16
F32 = jnp.float32


class Place:
    def __init__(self):
        self.t = lax.axis_index("tm")
        self.r = lax.axis_index("row")
        self.c = lax.axis_index("col")
        x = lax.rem(self.r, 4)
        base = self.r - x
        other = lax.rem(base + 4, 8)
        self.left = base + lax.rem(x + 3, 4)
        self.right = base + lax.rem(x + 1, 4)
        self.far = base + lax.rem(x + 2, 4)
        self.z = other + x
        self.zleft = other + lax.rem(x + 3, 4)
        self.zright = other + lax.rem(x + 1, 4)
        self.zfar = other + lax.rem(x + 2, 4)

    def row(self, r):
        return (self.t, r, self.c)

    def col(self):
        return (self.t, self.r, 1 - self.c)


def greet(signalled, awaited):
    barrier = pltpu.get_barrier_semaphore()
    for device in signalled:
        pl.semaphore_signal(barrier, inc=1, device_id=device, device_id_type=MESH)
    pl.semaphore_wait(barrier, awaited)


def remote(src, dst, send_sem, recv_sem, device):
    return pltpu.make_async_remote_copy(
        src_ref=src,
        dst_ref=dst,
        send_sem=send_sem,
        recv_sem=recv_sem,
        device_id=device,
        device_id_type=MESH,
    )


class Gather:
    def __init__(self, place, buf, send_sems, recv_sems, far_over_z):
        p = place
        low, high, full = pl.ds(0, 64), pl.ds(64, 64), pl.ds(0, 128)
        plan = [
            (p.r, p.left, full, p.right),
            (p.r, p.right, full, p.left),
            (p.r, p.z, full, p.z),
            (p.left, p.far, low, p.right),
            (p.right, p.far, high, p.left),
            (p.z, p.zleft, full, p.right),
            (p.z, p.zright, full, p.left),
        ]
        if far_over_z:
            plan += [(p.far, p.zfar, full, p.z)]
        else:
            plan += [(p.zleft, p.zfar, low, p.right), (p.zright, p.zfar, high, p.left)]
        self.out, self.into = [], []
        for i, (sent, received, rows, target) in enumerate(plan):
            device = p.row(target)
            a, b = buf.at[sent, rows], buf.at[received, rows]
            self.out.append(remote(a, a, send_sems.at[i], recv_sems.at[i], device))
            self.into.append(remote(b, b, send_sems.at[i], recv_sems.at[i], device))

    def send(self, *which):
        for i in which:
            self.out[i].start()

    def arrived(self, *which):
        for i in which:
            self.into[i].wait_recv()

    def finish(self):
        for copy in self.out:
            copy.wait_send()


def gather_steps(place, gather, far_over_z, visit):
    p = place
    gather.send(0, 1, 2)
    visit(0, p.r)
    gather.arrived(0)
    gather.send(3)
    gather.arrived(1)
    gather.send(4)
    gather.arrived(2)
    gather.send(5, 6)
    visit(1, p.left)
    visit(2, p.right)
    visit(3, p.z)
    gather.arrived(3, 4)
    if far_over_z:
        gather.send(7)
    visit(4, p.far)
    gather.arrived(5)
    if not far_over_z:
        gather.send(7)
    gather.arrived(6)
    if not far_over_z:
        gather.send(8)
    visit(5, p.zleft)
    visit(6, p.zright)
    if far_over_z:
        gather.arrived(7)
    else:
        gather.arrived(7, 8)
    visit(7, p.zfar)


def order_of(p):
    return [p.r, p.left, p.right, p.z, p.far, p.zleft, p.zright, p.zfar]


def project_kernel(
    x_ref, mod_ref, w_hbm, paths_hbm, drift_hbm,
    qkv_ref, full_ref, state_hbm, moved_hbm,
    w_ref, sq_out, sq_in, part, out_part, in_part,
    w_sems, sq_sems, send_sems, recv_sems, col_send, col_recv, tm_send, tm_recv,
):
    p = Place()
    weight_copies = [
        pltpu.make_async_copy(w_hbm.at[j], w_ref.at[j], w_sems.at[j]) for j in range(3)
    ]
    for copy in weight_copies:
        copy.start()
    after = (lax.rem(p.t + 1, 8), p.r, p.c)
    before = (lax.rem(p.t + 7, 8), p.r, p.c)
    greet([p.row(p.right), p.row(p.left), p.row(p.z), p.col(), before], 5)
    squares = jnp.zeros((128, 1), F32)
    for i in range(4):
        piece = x_ref[:, i * 768 : (i + 1) * 768].astype(F32)
        squares = squares + jnp.sum(piece * piece, axis=-1, keepdims=True)
    sq_out[...] = jnp.broadcast_to(squares, (128, 128))
    swap = remote(sq_out, sq_in, sq_sems.at[0], sq_sems.at[1], p.col())
    swap.start()
    swap.wait()
    total = sq_out[:, :1] + sq_in[:, :1]
    scale = lax.rsqrt(total / D + norm_eps)
    for i in range(4):
        cols = slice(i * 768, (i + 1) * 768)
        piece = x_ref[:, cols].astype(F32)
        full_ref[p.r, :, cols] = (
            piece * scale * (1.0 + mod_ref[0:1, cols]) + mod_ref[1:2, cols]
        ).astype(BF16)

    gather = Gather(p, full_ref, send_sems, recv_sems, False)
    col_copies = []
    moves = [
        remote(paths_hbm, state_hbm, tm_send.at[0], tm_recv.at[0], after),
        remote(drift_hbm, moved_hbm, tm_send.at[1], tm_recv.at[1], after),
    ]

    def visit(k, owner):
        if k == 0:
            for move in moves:
                move.start()
            for copy in weight_copies:
                copy.wait()

        @pl.loop(0, 3)
        def _(j):
            term = jnp.dot(full_ref[owner], w_ref[j], preferred_element_type=F32)
            part[k, j] = term
            out_part[k, j] = term.astype(BF16)

        copy = remote(out_part.at[k], in_part.at[k], col_send.at[k], col_recv.at[k], p.col())
        copy.start()
        col_copies.append(copy)

    gather_steps(p, gather, False, visit)
    for k, owner in enumerate(order_of(p)):
        col_copies[k].wait_recv()
        for j in range(3):
            qkv_ref[j, owner] = (part[k, j] + in_part[k, j].astype(F32)).astype(BF16)
    for copy in col_copies:
        copy.wait_send()
    for move in moves:
        move.wait()
    gather.finish()


def project(x, mod, w, paths, drift):
    vmem = pl.BlockSpec(memory_space=pltpu.VMEM)
    hbm = pl.BlockSpec(memory_space=pl.ANY)
    dma = pltpu.SemaphoreType.DMA
    return pl.pallas_call(
        project_kernel,
        out_shape=(
            jax.ShapeDtypeStruct((3, 8, 128, 384), BF16),
            jax.ShapeDtypeStruct((8, 128, 3072), BF16),
            jax.ShapeDtypeStruct((128, 3072), BF16),
            jax.ShapeDtypeStruct((128, 3072), BF16),
        ),
        in_specs=[vmem, vmem, hbm, hbm, hbm],
        out_specs=(vmem, vmem, hbm, hbm),
        scratch_shapes=[
            pltpu.VMEM((3, 3072, 384), BF16),
            pltpu.VMEM((128, 128), F32),
            pltpu.VMEM((128, 128), F32),
            pltpu.VMEM((8, 3, 128, 384), F32),
            pltpu.VMEM((8, 3, 128, 384), BF16),
            pltpu.VMEM((8, 3, 128, 384), BF16),
            dma((3,)),
            dma((2,)),
            dma((9,)),
            dma((9,)),
            dma((8,)),
            dma((8,)),
            dma((2,)),
            dma((2,)),
        ],
        name="project",
        cost_estimate=pl.CostEstimate(
            flops=2 * 1024 * 3072 * 1152, bytes_accessed=20_000_000, transcendentals=0
        ),
        compiler_params=pltpu.CompilerParams(
            collective_id=1, has_side_effects=True, vmem_limit_bytes=VMEM_LIMIT
        ),
    )(x, mod, w, paths, drift)


def attend_kernel(
    qkv_ref, w_ref, base_ref,
    grads_ref, up_ref, mixed_ref,
    probs, outbox, inbox, half_in, gm_part, gm_out, gm_in, key_acc, value_acc,
    rs_send, rs_recv, send_sems, recv_sems, col_send, col_recv,
):
    p = Place()
    greet([p.row(p.right), p.row(p.left), p.row(p.z), p.col()], 4)

    def keys(h):
        return qkv_ref[1, :, :, h * 128 : (h + 1) * 128].reshape(1024, 128)

    def values(h):
        return qkv_ref[2, :, :, h * 128 : (h + 1) * 128].reshape(1024, 128)

    def attend(owner):
        for h in range(3):
            cols = slice(h * 128, (h + 1) * 128)
            scores = (
                lax.dot_general(
                    qkv_ref[0, owner, :, cols],
                    keys(h),
                    (((1,), (1,)), ((), ())),
                    preferred_element_type=F32,
                )
                * SCALE
            )
            top = jnp.max(scores, axis=-1, keepdims=True)
            weights = jnp.exp(scores - top)
            weights = weights * (1.0 / jnp.sum(weights, axis=-1, keepdims=True))
            probs[h, owner] = weights
            mixed_ref[owner, :, cols] = jnp.dot(
                weights.astype(BF16), values(h), preferred_element_type=F32
            ).astype(BF16)

    def out_rows(owner, lo, n, extra, put):
        @pl.loop(0, 4)
        def _(i):
            cols = pl.ds(pl.multiple_of(i * 768, 768), 768)
            term = jnp.dot(
                mixed_ref[owner, lo : lo + n, :], w_ref[:, cols], preferred_element_type=F32
            )
            for ref in extra:
                term = term + ref[:, cols].astype(F32)
            put(cols, term)

    def to_slot(slot, lo, n):
        def put(cols, term):
            outbox[slot, lo : lo + n, cols] = term.astype(BF16)

        return put

    low, high = pl.ds(0, 64), pl.ds(64, 64)
    messages = [
        (outbox.at[0], inbox.at[0], p.z),
        (outbox.at[1], inbox.at[1], p.left),
        (outbox.at[2], inbox.at[2], p.right),
        (outbox.at[3, low], half_in.at[0], p.left),
        (outbox.at[3, high], half_in.at[1], p.right),
        (outbox.at[4], inbox.at[3], p.left),
        (outbox.at[5], inbox.at[4], p.right),
        (outbox.at[6], inbox.at[5], p.z),
    ]
    copies = [
        remote(src, dst, rs_send.at[i], rs_recv.at[i], p.row(target))
        for i, (src, dst, target) in enumerate(messages)
    ]
    for slot, owner in enumerate([p.zfar, p.zleft, p.zright]):
        attend(owner)
        out_rows(owner, 0, 128, [], to_slot(slot, 0, 128))
        copies[slot].start()

    @pl.loop(0, 5)
    def _(i):
        owner = jnp.where(
            i == 0,
            p.far,
            jnp.where(i == 1, p.left, jnp.where(i == 2, p.right, jnp.where(i == 3, p.z, p.r))),
        )
        attend(owner)

    copies[0].wait_recv()
    out_rows(p.far, 0, 128, [inbox.at[0]], to_slot(3, 0, 128))
    copies[3].start()
    copies[4].start()
    copies[1].wait_recv()
    copies[2].wait_recv()
    out_rows(p.z, 0, 128, [inbox.at[1], inbox.at[2]], to_slot(6, 0, 128))
    copies[7].start()
    out_rows(p.left, 64, 64, [], to_slot(4, 64, 64))
    out_rows(p.right, 0, 64, [], to_slot(5, 0, 64))
    copies[3].wait_recv()
    out_rows(p.left, 0, 64, [half_in.at[0]], to_slot(4, 0, 64))
    copies[5].start()
    copies[4].wait_recv()
    out_rows(p.right, 64, 64, [half_in.at[1]], to_slot(5, 64, 64))
    copies[6].start()
    key_acc[...] = jnp.zeros_like(key_acc)
    value_acc[...] = jnp.zeros_like(value_acc)
    copies[5].wait_recv()
    copies[6].wait_recv()
    copies[7].wait_recv()

    def to_up(cols, term):
        up_ref[p.r, :, cols] = ((base_ref[:, cols] + term) * (1024**-0.5)).astype(BF16)

    out_rows(p.r, 0, 128, [inbox.at[3], inbox.at[4], inbox.at[5]], to_up)

    gather = Gather(p, up_ref, send_sems, recv_sems, True)
    col_copies = []
    waiting = []

    def backward(k, owner):
        col_copies[k].wait_recv()
        grad = (gm_part[k] + gm_in[k].astype(F32)).astype(BF16)
        tokens = pl.ds(pl.multiple_of(owner * 128, 128), 128)
        for h in range(3):
            cols = slice(h * 128, (h + 1) * 128)
            head_grad = grad[:, cols]
            weights = probs[h, owner]
            value_acc[h] += jnp.dot(
                head_grad.T, weights.astype(BF16), preferred_element_type=F32
            )
            grad_weights = lax.dot_general(
                head_grad, values(h), (((1,), (1,)), ((), ())), preferred_element_type=F32
            )
            inner = jnp.sum(grad_weights * weights, axis=-1, keepdims=True)
            grad_scores = (weights * (grad_weights - inner) * SCALE).astype(BF16)
            query_grad = jnp.dot(grad_scores, keys(h), preferred_element_type=F32)
            grads_ref[0, cols, tokens] = query_grad.T.astype(BF16)
            key_acc[h] += jnp.dot(
                qkv_ref[0, owner, :, cols].T, grad_scores, preferred_element_type=F32
            )

    def visit(k, owner):
        term = lax.dot_general(
            up_ref[owner], w_ref[...], (((1,), (1,)), ((), ())), preferred_element_type=F32
        )
        gm_part[k] = term
        gm_out[k] = term.astype(BF16)
        copy = remote(gm_out.at[k], gm_in.at[k], col_send.at[k], col_recv.at[k], p.col())
        copy.start()
        col_copies.append(copy)
        if waiting:
            backward(*waiting.pop())
        waiting.append((k, owner))

    gather_steps(p, gather, True, visit)
    backward(*waiting.pop())
    for h in range(3):
        cols = slice(h * 128, (h + 1) * 128)
        grads_ref[1, cols, :] = key_acc[h].astype(BF16)
        grads_ref[2, cols, :] = value_acc[h].astype(BF16)
    for copy in copies + col_copies:
        copy.wait_send()
    gather.finish()


def attend(qkv, w, base):
    vmem = pl.BlockSpec(memory_space=pltpu.VMEM)
    dma = pltpu.SemaphoreType.DMA
    return pl.pallas_call(
        attend_kernel,
        out_shape=(
            jax.ShapeDtypeStruct((3, 384, 1024), BF16),
            jax.ShapeDtypeStruct((8, 128, 3072), BF16),
            jax.ShapeDtypeStruct((8, 128, 384), BF16),
        ),
        in_specs=[vmem] * 3,
        out_specs=(vmem,) * 3,
        scratch_shapes=[
            pltpu.VMEM((3, 8, 128, 1024), F32),
            pltpu.VMEM((7, 128, 3072), BF16),
            pltpu.VMEM((6, 128, 3072), BF16),
            pltpu.VMEM((2, 64, 3072), BF16),
            pltpu.VMEM((8, 128, 384), F32),
            pltpu.VMEM((8, 128, 384), BF16),
            pltpu.VMEM((8, 128, 384), BF16),
            pltpu.VMEM((3, 128, 1024), F32),
            pltpu.VMEM((3, 128, 1024), F32),
            dma((8,)),
            dma((8,)),
            dma((8,)),
            dma((8,)),
            dma((8,)),
            dma((8,)),
        ],
        name="attend",
        cost_estimate=pl.CostEstimate(
            flops=10_000_000_000, bytes_accessed=15_000_000, transcendentals=3 * 1024 * 1024
        ),
        compiler_params=pltpu.CompilerParams(
            collective_id=2, has_side_effects=True, vmem_limit_bytes=VMEM_LIMIT
        ),
    )(qkv, w, base)


def body(paths, prev_drift, boundary, step_scale, time_ids, mod_table, w_qkv, output_weight):
    modulation = lax.dynamic_index_in_dim(mod_table, time_ids[0], 0, keepdims=False).astype(F32)
    w = jnp.transpose(w_qkv, (1, 0, 2))
    qkv, normed, moved_state, moved_drift = project(
        paths[0], modulation, w, paths[0], prev_drift[0]
    )
    at_start = lax.axis_index("tm") == 0
    prev_state = jnp.where(at_start, boundary[0], moved_state).astype(F32)
    prev_shift = jnp.where(at_start, boundary[1], moved_drift).astype(F32)
    target = prev_state + step_scale[0] * (prev_shift - prev_drift[0].astype(F32))
    base = paths[0].astype(F32) - target
    grads, upstream, mixed = attend(qkv, output_weight, base)
    grads = grads.reshape(1152, 1024)
    normed = normed.reshape(1024, 3072)
    output_gradient = lax.dot_general(
        mixed.reshape(1024, 384),
        upstream.reshape(1024, 3072),
        (((0,), (0,)), ((), ())),
        preferred_element_type=F32,
    )
    input_gradient = jnp.dot(grads, normed, preferred_element_type=F32)
    grad_in_sum = lax.psum_scatter(
        input_gradient.astype(BF16), "tm", scatter_dimension=1, tiled=True
    ).astype(F32)
    grad_in_sum = jnp.transpose(grad_in_sum.reshape(3, 384, 384), (2, 0, 1))
    grad_out_sum = lax.psum_scatter(
        output_gradient.astype(BF16), "tm", scatter_dimension=1, tiled=True
    ).astype(F32)
    return (grad_in_sum, grad_out_sum)


def solution(mesh):
    placed = (
        P("tm", "row", "col"),
        P("tm", "row", "col"),
        P(None, "row", "col"),
        P("tm"),
        P("tm"),
        P(None, None, "col"),
        P("col", None, "row"),
        P("row", "col"),
    )
    return jax.shard_map(
        body,
        mesh=mesh,
        in_specs=placed,
        out_specs=(P(("col", "tm"), None, "row"), P("row", ("col", "tm"))),
        check_vma=False,
    )
```

```python
import jax
import jax.numpy as jnp
from jax import lax
from jax.experimental import pallas as pl
from jax.experimental.pallas import tpu as pltpu
from jax.sharding import PartitionSpec as P

D = 6144
HEAD_DIM = 128
SCALE = HEAD_DIM**-0.5
MESH = pl.DeviceIdType.MESH
VMEM_LIMIT = 60 * 1024 * 1024

norm_eps = 1e-06

BF16 = jnp.bfloat16
F32 = jnp.float32


class Place:
    def __init__(self):
        self.t = lax.axis_index("tm")
        self.r = lax.axis_index("row")
        self.c = lax.axis_index("col")
        x = lax.rem(self.r, 4)
        base = self.r - x
        other = lax.rem(base + 4, 8)
        self.left = base + lax.rem(x + 3, 4)
        self.right = base + lax.rem(x + 1, 4)
        self.far = base + lax.rem(x + 2, 4)
        self.z = other + x
        self.zleft = other + lax.rem(x + 3, 4)
        self.zright = other + lax.rem(x + 1, 4)
        self.zfar = other + lax.rem(x + 2, 4)

    def row(self, r):
        return (self.t, r, self.c)

    def col(self):
        return (self.t, self.r, 1 - self.c)


def greet(signalled, awaited):
    barrier = pltpu.get_barrier_semaphore()
    for device in signalled:
        pl.semaphore_signal(barrier, inc=1, device_id=device, device_id_type=MESH)
    pl.semaphore_wait(barrier, awaited)


def remote(src, dst, send_sem, recv_sem, device):
    return pltpu.make_async_remote_copy(
        src_ref=src,
        dst_ref=dst,
        send_sem=send_sem,
        recv_sem=recv_sem,
        device_id=device,
        device_id_type=MESH,
    )


class Gather:
    def __init__(self, place, buf, send_sems, recv_sems, far_over_z):
        p = place
        low, high, full = pl.ds(0, 64), pl.ds(64, 64), pl.ds(0, 128)
        plan = [
            (p.r, p.left, full, p.right),
            (p.r, p.right, full, p.left),
            (p.r, p.z, full, p.z),
            (p.left, p.far, low, p.right),
            (p.right, p.far, high, p.left),
            (p.z, p.zleft, full, p.right),
            (p.z, p.zright, full, p.left),
        ]
        if far_over_z:
            plan += [(p.far, p.zfar, full, p.z)]
        else:
            plan += [(p.zleft, p.zfar, low, p.right), (p.zright, p.zfar, high, p.left)]
        self.out, self.into = [], []
        for i, (sent, received, rows, target) in enumerate(plan):
            device = p.row(target)
            a, b = buf.at[sent, rows], buf.at[received, rows]
            self.out.append(remote(a, a, send_sems.at[i], recv_sems.at[i], device))
            self.into.append(remote(b, b, send_sems.at[i], recv_sems.at[i], device))

    def send(self, *which):
        for i in which:
            self.out[i].start()

    def arrived(self, *which):
        for i in which:
            self.into[i].wait_recv()

    def finish(self):
        for copy in self.out:
            copy.wait_send()


def gather_steps(place, gather, far_over_z, visit):
    p = place
    gather.send(0, 1, 2)
    visit(0, p.r)
    gather.arrived(0)
    gather.send(3)
    gather.arrived(1)
    gather.send(4)
    gather.arrived(2)
    gather.send(5, 6)
    visit(1, p.left)
    visit(2, p.right)
    visit(3, p.z)
    gather.arrived(3, 4)
    if far_over_z:
        gather.send(7)
    visit(4, p.far)
    gather.arrived(5)
    if not far_over_z:
        gather.send(7)
    gather.arrived(6)
    if not far_over_z:
        gather.send(8)
    visit(5, p.zleft)
    visit(6, p.zright)
    if far_over_z:
        gather.arrived(7)
    else:
        gather.arrived(7, 8)
    visit(7, p.zfar)


def order_of(p):
    return [p.r, p.left, p.right, p.z, p.far, p.zleft, p.zright, p.zfar]


def project_kernel(
    x_ref, mod_ref, w_hbm, paths_hbm, drift_hbm,
    qkv_ref, full_ref, state_hbm, moved_hbm,
    w_ref, sq_out, sq_in, part, out_part, in_part,
    w_sems, sq_sems, send_sems, recv_sems, col_send, col_recv, tm_send, tm_recv,
):
    p = Place()
    weight_copies = [
        pltpu.make_async_copy(w_hbm.at[j], w_ref.at[j], w_sems.at[j]) for j in range(3)
    ]
    for copy in weight_copies:
        copy.start()
    after = (lax.rem(p.t + 1, 8), p.r, p.c)
    before = (lax.rem(p.t + 7, 8), p.r, p.c)
    greet([p.row(p.right), p.row(p.left), p.row(p.z), p.col(), before], 5)
    squares = jnp.zeros((128, 1), F32)
    for i in range(4):
        piece = x_ref[:, i * 768 : (i + 1) * 768].astype(F32)
        squares = squares + jnp.sum(piece * piece, axis=-1, keepdims=True)
    sq_out[...] = jnp.broadcast_to(squares, (128, 128))
    swap = remote(sq_out, sq_in, sq_sems.at[0], sq_sems.at[1], p.col())
    swap.start()
    swap.wait()
    total = sq_out[:, :1] + sq_in[:, :1]
    scale = lax.rsqrt(total / D + norm_eps)
    for i in range(4):
        cols = slice(i * 768, (i + 1) * 768)
        piece = x_ref[:, cols].astype(F32)
        full_ref[p.r, :, cols] = (
            piece * scale * (1.0 + mod_ref[0:1, cols]) + mod_ref[1:2, cols]
        ).astype(BF16)

    gather = Gather(p, full_ref, send_sems, recv_sems, False)
    col_copies = []
    moves = [
        remote(paths_hbm, state_hbm, tm_send.at[0], tm_recv.at[0], after),
        remote(drift_hbm, moved_hbm, tm_send.at[1], tm_recv.at[1], after),
    ]

    def visit(k, owner):
        if k == 0:
            for move in moves:
                move.start()
            for copy in weight_copies:
                copy.wait()

        @pl.loop(0, 3)
        def _(j):
            term = jnp.dot(full_ref[owner], w_ref[j], preferred_element_type=F32)
            part[k, j] = term
            out_part[k, j] = term.astype(BF16)

        copy = remote(out_part.at[k], in_part.at[k], col_send.at[k], col_recv.at[k], p.col())
        copy.start()
        col_copies.append(copy)

    gather_steps(p, gather, False, visit)
    for k, owner in enumerate(order_of(p)):
        col_copies[k].wait_recv()
        for j in range(3):
            qkv_ref[j, owner] = (part[k, j] + in_part[k, j].astype(F32)).astype(BF16)
    for copy in col_copies:
        copy.wait_send()
    for move in moves:
        move.wait()
    gather.finish()


def project(x, mod, w, paths, drift):
    vmem = pl.BlockSpec(memory_space=pltpu.VMEM)
    hbm = pl.BlockSpec(memory_space=pl.ANY)
    dma = pltpu.SemaphoreType.DMA
    return pl.pallas_call(
        project_kernel,
        out_shape=(
            jax.ShapeDtypeStruct((3, 8, 128, 384), BF16),
            jax.ShapeDtypeStruct((8, 128, 3072), BF16),
            jax.ShapeDtypeStruct((128, 3072), BF16),
            jax.ShapeDtypeStruct((128, 3072), BF16),
        ),
        in_specs=[vmem, vmem, hbm, hbm, hbm],
        out_specs=(vmem, vmem, hbm, hbm),
        scratch_shapes=[
            pltpu.VMEM((3, 3072, 384), BF16),
            pltpu.VMEM((128, 128), F32),
            pltpu.VMEM((128, 128), F32),
            pltpu.VMEM((8, 3, 128, 384), F32),
            pltpu.VMEM((8, 3, 128, 384), BF16),
            pltpu.VMEM((8, 3, 128, 384), BF16),
            dma((3,)),
            dma((2,)),
            dma((9,)),
            dma((9,)),
            dma((8,)),
            dma((8,)),
            dma((2,)),
            dma((2,)),
        ],
        name="project",
        cost_estimate=pl.CostEstimate(
            flops=2 * 1024 * 3072 * 1152, bytes_accessed=20_000_000, transcendentals=0
        ),
        compiler_params=pltpu.CompilerParams(
            collective_id=1, has_side_effects=True, vmem_limit_bytes=VMEM_LIMIT
        ),
    )(x, mod, w, paths, drift)


def attend_kernel(
    qkv_ref, w_ref, base_ref,
    grads_ref, up_ref, mixed_ref,
    probs, outbox, inbox, half_in, gm_part, gm_out, gm_in, key_acc, value_acc,
    rs_send, rs_recv, send_sems, recv_sems, col_send, col_recv,
):
    p = Place()
    greet([p.row(p.right), p.row(p.left), p.row(p.z), p.col()], 4)

    def keys(h):
        return qkv_ref[1, :, :, h * 128 : (h + 1) * 128].reshape(1024, 128)

    def values(h):
        return qkv_ref[2, :, :, h * 128 : (h + 1) * 128].reshape(1024, 128)

    def attend(owner):
        for h in range(3):
            cols = slice(h * 128, (h + 1) * 128)
            scores = (
                lax.dot_general(
                    qkv_ref[0, owner, :, cols],
                    keys(h),
                    (((1,), (1,)), ((), ())),
                    preferred_element_type=F32,
                )
                * SCALE
            )
            top = jnp.max(scores, axis=-1, keepdims=True)
            weights = jnp.exp(scores - top)
            weights = weights * (1.0 / jnp.sum(weights, axis=-1, keepdims=True))
            probs[h, owner] = weights
            mixed_ref[owner, :, cols] = jnp.dot(
                weights.astype(BF16), values(h), preferred_element_type=F32
            ).astype(BF16)

    def out_rows(owner, lo, n, extra, put):
        @pl.loop(0, 4)
        def _(i):
            cols = pl.ds(pl.multiple_of(i * 768, 768), 768)
            term = jnp.dot(
                mixed_ref[owner, lo : lo + n, :], w_ref[:, cols], preferred_element_type=F32
            )
            for ref in extra:
                term = term + ref[:, cols].astype(F32)
            put(cols, term)

    def to_slot(slot, lo, n):
        def put(cols, term):
            outbox[slot, lo : lo + n, cols] = term.astype(BF16)

        return put

    low, high = pl.ds(0, 64), pl.ds(64, 64)
    messages = [
        (outbox.at[0], inbox.at[0], p.z),
        (outbox.at[1], inbox.at[1], p.left),
        (outbox.at[2], inbox.at[2], p.right),
        (outbox.at[3, low], half_in.at[0], p.left),
        (outbox.at[3, high], half_in.at[1], p.right),
        (outbox.at[4], inbox.at[3], p.left),
        (outbox.at[5], inbox.at[4], p.right),
        (outbox.at[6], inbox.at[5], p.z),
    ]
    copies = [
        remote(src, dst, rs_send.at[i], rs_recv.at[i], p.row(target))
        for i, (src, dst, target) in enumerate(messages)
    ]
    for slot, owner in enumerate([p.zfar, p.zleft, p.zright]):
        attend(owner)
        out_rows(owner, 0, 128, [], to_slot(slot, 0, 128))
        copies[slot].start()

    @pl.loop(0, 5)
    def _(i):
        owner = jnp.where(
            i == 0,
            p.far,
            jnp.where(i == 1, p.left, jnp.where(i == 2, p.right, jnp.where(i == 3, p.z, p.r))),
        )
        attend(owner)

    copies[0].wait_recv()
    out_rows(p.far, 0, 128, [inbox.at[0]], to_slot(3, 0, 128))
    copies[3].start()
    copies[4].start()
    copies[1].wait_recv()
    copies[2].wait_recv()
    out_rows(p.z, 0, 128, [inbox.at[1], inbox.at[2]], to_slot(6, 0, 128))
    copies[7].start()
    out_rows(p.left, 64, 64, [], to_slot(4, 64, 64))
    out_rows(p.right, 0, 64, [], to_slot(5, 0, 64))
    copies[3].wait_recv()
    out_rows(p.left, 0, 64, [half_in.at[0]], to_slot(4, 0, 64))
    copies[5].start()
    copies[4].wait_recv()
    out_rows(p.right, 64, 64, [half_in.at[1]], to_slot(5, 64, 64))
    copies[6].start()
    key_acc[...] = jnp.zeros_like(key_acc)
    value_acc[...] = jnp.zeros_like(value_acc)
    copies[5].wait_recv()
    copies[6].wait_recv()
    copies[7].wait_recv()

    def to_up(cols, term):
        up_ref[p.r, :, cols] = ((base_ref[:, cols] + term) * (1024**-0.5)).astype(BF16)

    out_rows(p.r, 0, 128, [inbox.at[3], inbox.at[4], inbox.at[5]], to_up)

    gather = Gather(p, up_ref, send_sems, recv_sems, True)
    col_copies = []
    waiting = []

    def backward(k, owner):
        col_copies[k].wait_recv()
        grad = (gm_part[k] + gm_in[k].astype(F32)).astype(BF16)
        tokens = pl.ds(pl.multiple_of(owner * 128, 128), 128)
        for h in range(3):
            cols = slice(h * 128, (h + 1) * 128)
            head_grad = grad[:, cols]
            weights = probs[h, owner]
            value_acc[h] += jnp.dot(
                head_grad.T, weights.astype(BF16), preferred_element_type=F32
            )
            grad_weights = lax.dot_general(
                head_grad, values(h), (((1,), (1,)), ((), ())), preferred_element_type=F32
            )
            inner = jnp.sum(grad_weights * weights, axis=-1, keepdims=True)
            grad_scores = (weights * (grad_weights - inner) * SCALE).astype(BF16)
            query_grad = jnp.dot(grad_scores, keys(h), preferred_element_type=F32)
            grads_ref[0, cols, tokens] = query_grad.T.astype(BF16)
            key_acc[h] += jnp.dot(
                qkv_ref[0, owner, :, cols].T, grad_scores, preferred_element_type=F32
            )

    def visit(k, owner):
        term = lax.dot_general(
            up_ref[owner], w_ref[...], (((1,), (1,)), ((), ())), preferred_element_type=F32
        )
        gm_part[k] = term
        gm_out[k] = term.astype(BF16)
        copy = remote(gm_out.at[k], gm_in.at[k], col_send.at[k], col_recv.at[k], p.col())
        copy.start()
        col_copies.append(copy)
        if waiting:
            backward(*waiting.pop())
        waiting.append((k, owner))

    gather_steps(p, gather, True, visit)
    backward(*waiting.pop())
    for h in range(3):
        cols = slice(h * 128, (h + 1) * 128)
        grads_ref[1, cols, :] = key_acc[h].astype(BF16)
        grads_ref[2, cols, :] = value_acc[h].astype(BF16)
    for copy in copies + col_copies:
        copy.wait_send()
    gather.finish()


def attend(qkv, w, base):
    vmem = pl.BlockSpec(memory_space=pltpu.VMEM)
    dma = pltpu.SemaphoreType.DMA
    return pl.pallas_call(
        attend_kernel,
        out_shape=(
            jax.ShapeDtypeStruct((3, 384, 1024), BF16),
            jax.ShapeDtypeStruct((8, 128, 3072), BF16),
            jax.ShapeDtypeStruct((8, 128, 384), BF16),
        ),
        in_specs=[vmem] * 3,
        out_specs=(vmem,) * 3,
        scratch_shapes=[
            pltpu.VMEM((3, 8, 128, 1024), F32),
            pltpu.VMEM((7, 128, 3072), BF16),
            pltpu.VMEM((6, 128, 3072), BF16),
            pltpu.VMEM((2, 64, 3072), BF16),
            pltpu.VMEM((8, 128, 384), F32),
            pltpu.VMEM((8, 128, 384), BF16),
            pltpu.VMEM((8, 128, 384), BF16),
            pltpu.VMEM((3, 128, 1024), F32),
            pltpu.VMEM((3, 128, 1024), F32),
            dma((8,)),
            dma((8,)),
            dma((8,)),
            dma((8,)),
            dma((8,)),
            dma((8,)),
        ],
        name="attend",
        cost_estimate=pl.CostEstimate(
            flops=10_000_000_000, bytes_accessed=15_000_000, transcendentals=3 * 1024 * 1024
        ),
        compiler_params=pltpu.CompilerParams(
            collective_id=2, has_side_effects=True, vmem_limit_bytes=VMEM_LIMIT
        ),
    )(qkv, w, base)


def reduce_kernel(
    grads_ref, mixed_ref, normed_hbm, up_hbm,
    in_ref, out_ref,
    mixed_t, normed, up, core_out, core_in, y_out, y_in, left_low, right_high, own,
    normed_sems, up_sems, core_send, core_recv, y_send, y_recv,
):
    p = Place()
    core = lax.rem(p.t, 2)
    y = p.t // 2
    peers = [lax.rem(y + by, 4) for by in (2, 3, 1, 0)]
    theirs = [2 * peer + 1 - core for peer in peers]
    mine = [2 * peer + core for peer in peers]
    order = [
        theirs[0], theirs[1], mine[0], theirs[2], mine[1], theirs[3], mine[2], mine[3],
    ]
    loads = []
    for k, owner in enumerate(order):
        cols = pl.ds(pl.multiple_of(owner * 384, 384), 384)
        loads.append(
            (
                pltpu.make_async_copy(normed_hbm.at[:, :, cols], normed.at[k], normed_sems.at[k]),
                pltpu.make_async_copy(up_hbm.at[:, :, cols], up.at[k], up_sems.at[k]),
            )
        )
        for copy in loads[-1]:
            copy.start()
    partner = (2 * y + 1 - core, p.r, p.c)
    to_left = (2 * peers[1] + core, p.r, p.c)
    to_right = (2 * peers[2] + core, p.r, p.c)
    greet([partner, to_left, to_right], 3)
    mixed_t[...] = mixed_ref[...].reshape(1024, 384).T

    def chunk(k, put):
        for copy in loads[k]:
            copy.wait()

        @pl.loop(0, 3)
        def _(j):
            put(
                j,
                jnp.dot(
                    grads_ref[j], normed[k].reshape(1024, 384), preferred_element_type=F32
                ),
            )

        put(3, jnp.dot(mixed_t[...], up[k].reshape(1024, 384), preferred_element_type=F32))

    core_copies = [
        remote(core_out.at[i], core_in.at[i], core_send.at[i], core_recv.at[i], partner)
        for i in range(4)
    ]
    low, high = pl.ds(0, 2), pl.ds(2, 2)
    messages = [
        (y_out.at[0, low], to_left),
        (y_out.at[0, high], to_right),
        (y_out.at[1, high], to_left),
        (y_out.at[2, low], to_right),
        (y_out.at[1, low], to_left),
        (y_out.at[2, high], to_right),
    ]
    y_copies = [
        remote(src, y_in.at[i], y_send.at[i], y_recv.at[i], device)
        for i, (src, device) in enumerate(messages)
    ]

    def for_partner(k, i):
        def put(j, term):
            core_out[i, j] = term.astype(BF16)

        chunk(k, put)
        core_copies[i].start()

    def for_far(j, term):
        y_out[0, j] = (term + core_in[0, j].astype(F32)).astype(BF16)

    def for_left(j, term):
        total = term + core_in[1, j].astype(F32)
        y_out[1, j] = total.astype(BF16)
        left_low[j] = total

    def for_right(j, term):
        total = term + core_in[2, j].astype(F32)
        y_out[2, j] = total.astype(BF16)
        right_high[j] = total

    def for_own(j, term):
        own[j] = term + core_in[3, j].astype(F32)

    for_partner(0, 0)
    for_partner(1, 1)
    core_copies[0].wait_recv()
    chunk(2, for_far)
    y_copies[0].start()
    y_copies[1].start()
    for_partner(3, 2)
    core_copies[1].wait_recv()
    chunk(4, for_left)
    y_copies[2].start()
    for_partner(5, 3)
    core_copies[2].wait_recv()
    chunk(6, for_right)
    y_copies[3].start()
    core_copies[3].wait_recv()
    chunk(7, for_own)
    y_copies[0].wait_recv()
    for j in (0, 1):
        y_out[1, j] = (left_low[j] + y_in[0, j].astype(F32)).astype(BF16)
    y_copies[4].start()
    y_copies[1].wait_recv()
    for j in (2, 3):
        y_out[2, j] = (right_high[j] + y_in[1, j - 2].astype(F32)).astype(BF16)
    y_copies[5].start()
    y_copies[2].wait_recv()
    y_copies[3].wait_recv()
    for j in (0, 1):
        own[j] += y_in[3, j].astype(F32)
        own[j + 2] += y_in[2, j].astype(F32)
    y_copies[4].wait_recv()
    for j in (0, 1):
        in_ref[j] = own[j] + y_in[4, j].astype(F32)
    y_copies[5].wait_recv()
    in_ref[2] = own[2] + y_in[5, 0].astype(F32)
    out_ref[...] = own[3] + y_in[5, 1].astype(F32)
    for copy in core_copies + y_copies:
        copy.wait_send()


def reduce(grads, mixed, normed, up):
    vmem = pl.BlockSpec(memory_space=pltpu.VMEM)
    hbm = pl.BlockSpec(memory_space=pl.ANY)
    dma = pltpu.SemaphoreType.DMA
    return pl.pallas_call(
        reduce_kernel,
        out_shape=(
            jax.ShapeDtypeStruct((3, 384, 384), F32),
            jax.ShapeDtypeStruct((384, 384), F32),
        ),
        in_specs=[vmem, vmem, hbm, hbm],
        out_specs=(vmem, vmem),
        scratch_shapes=[
            pltpu.VMEM((384, 1024), BF16),
            pltpu.VMEM((8, 8, 128, 384), BF16),
            pltpu.VMEM((8, 8, 128, 384), BF16),
            pltpu.VMEM((4, 4, 384, 384), BF16),
            pltpu.VMEM((4, 4, 384, 384), BF16),
            pltpu.VMEM((3, 4, 384, 384), BF16),
            pltpu.VMEM((6, 2, 384, 384), BF16),
            pltpu.VMEM((4, 384, 384), F32),
            pltpu.VMEM((4, 384, 384), F32),
            pltpu.VMEM((4, 384, 384), F32),
            dma((8,)),
            dma((8,)),
            dma((4,)),
            dma((4,)),
            dma((6,)),
            dma((6,)),
        ],
        name="reduce",
        cost_estimate=pl.CostEstimate(
            flops=2 * 1024 * 3072 * 1536, bytes_accessed=20_000_000, transcendentals=0
        ),
        compiler_params=pltpu.CompilerParams(
            collective_id=3, has_side_effects=True, vmem_limit_bytes=VMEM_LIMIT
        ),
    )(grads, mixed, normed, up)


def body(paths, prev_drift, boundary, step_scale, time_ids, mod_table, w_qkv, output_weight):
    modulation = lax.dynamic_index_in_dim(mod_table, time_ids[0], 0, keepdims=False).astype(F32)
    w = jnp.transpose(w_qkv, (1, 0, 2))
    qkv, normed, moved_state, moved_drift = project(
        paths[0], modulation, w, paths[0], prev_drift[0]
    )
    at_start = lax.axis_index("tm") == 0
    prev_state = jnp.where(at_start, boundary[0], moved_state).astype(F32)
    prev_shift = jnp.where(at_start, boundary[1], moved_drift).astype(F32)
    target = prev_state + step_scale[0] * (prev_shift - prev_drift[0].astype(F32))
    base = paths[0].astype(F32) - target
    grads, upstream, mixed = attend(qkv, output_weight, base)
    grad_in_sum, grad_out_sum = reduce(grads, mixed, normed, upstream)
    grad_in_sum = jnp.transpose(grad_in_sum, (2, 0, 1))
    return (grad_in_sum, grad_out_sum)


def solution(mesh):
    placed = (
        P("tm", "row", "col"),
        P("tm", "row", "col"),
        P(None, "row", "col"),
        P("tm"),
        P("tm"),
        P(None, None, "col"),
        P("col", None, "row"),
        P("row", "col"),
    )
    return jax.shard_map(
        body,
        mesh=mesh,
        in_specs=placed,
        out_specs=(P(("col", "tm"), None, "row"), P("row", ("col", "tm"))),
        check_vma=False,
    )
```

```python
import jax
import jax.numpy as jnp
from jax import lax
from jax.experimental import pallas as pl
from jax.experimental.pallas import tpu as pltpu
from jax.sharding import PartitionSpec as P

D = 6144
HEAD_DIM = 128
SCALE = HEAD_DIM**-0.5
MESH = pl.DeviceIdType.MESH
VMEM_LIMIT = 60 * 1024 * 1024

norm_eps = 1e-06

BF16 = jnp.bfloat16
F32 = jnp.float32
HALVES = (pl.ds(0, 1536), pl.ds(1536, 1536))


class Place:
    def __init__(self):
        self.t = lax.axis_index("tm")
        self.r = lax.axis_index("row")
        self.c = lax.axis_index("col")
        x = lax.rem(self.r, 4)
        base = self.r - x
        other = lax.rem(base + 4, 8)
        self.left = base + lax.rem(x + 3, 4)
        self.right = base + lax.rem(x + 1, 4)
        self.far = base + lax.rem(x + 2, 4)
        self.z = other + x
        self.zleft = other + lax.rem(x + 3, 4)
        self.zright = other + lax.rem(x + 1, 4)
        self.zfar = other + lax.rem(x + 2, 4)

    def row(self, r):
        return (self.t, r, self.c)

    def col(self):
        return (self.t, self.r, 1 - self.c)


def greet(signalled, awaited):
    barrier = pltpu.get_barrier_semaphore()
    for device in signalled:
        pl.semaphore_signal(barrier, inc=1, device_id=device, device_id_type=MESH)
    pl.semaphore_wait(barrier, awaited)


def remote(src, dst, send_sem, recv_sem, device):
    return pltpu.make_async_remote_copy(
        src_ref=src,
        dst_ref=dst,
        send_sem=send_sem,
        recv_sem=recv_sem,
        device_id=device,
        device_id_type=MESH,
    )


class Gather:
    def __init__(self, place, buf, send_sems, recv_sems, over_z):
        p = place
        self.over_z = over_z
        low, high, full = pl.ds(0, 64), pl.ds(64, 64), pl.ds(0, 128)
        plan = [
            (p.r, p.left, full, p.right),
            (p.r, p.right, full, p.left),
            (p.r, p.z, full, p.z),
            (p.left, p.far, low, p.right),
            (p.right, p.far, high, p.left),
            (p.z, p.zleft, full, p.right),
            (p.z, p.zright, full, p.left),
            (p.zleft, p.zfar, low, p.right),
            (p.zright, p.zfar, high, p.left),
            (p.far, p.zfar, full, p.z),
        ]
        self.out, self.into, self.started = {}, {}, []
        for c in (0, 1):
            for m, (sent, received, rows, target) in enumerate(plan):
                i = 10 * c + m
                device = p.row(target)
                a, b = buf.at[sent, rows, HALVES[c]], buf.at[received, rows, HALVES[c]]
                self.out[m, c] = remote(a, a, send_sems.at[i], recv_sems.at[i], device)
                self.into[m, c] = remote(b, b, send_sems.at[i], recv_sems.at[i], device)

    def send(self, c, *which):
        for m in which:
            self.out[m, c].start()
            self.started.append(self.out[m, c])

    def arrived(self, c, *which):
        for m in which:
            self.into[m, c].wait_recv()

    def finish(self):
        for copy in self.started:
            copy.wait_send()

    def run(self, place, visit):
        p = place
        visit(0, p.r)
        for c in (0, 1):
            self.arrived(c, 0)
            self.send(c, 3)
            self.arrived(c, 1)
            self.send(c, 4)
            self.arrived(c, 2)
            self.send(c, 5, 6)
        visit(1, p.left)
        visit(2, p.right)
        for c in (0, 1):
            self.arrived(c, 3, 4)
            if c in self.over_z:
                self.send(c, 9)
        visit(3, p.z)
        visit(4, p.far)
        for c in (0, 1):
            self.arrived(c, 5)
            if c not in self.over_z:
                self.send(c, 7)
            self.arrived(c, 6)
            if c not in self.over_z:
                self.send(c, 8)
        visit(5, p.zleft)
        visit(6, p.zright)
        for c in (0, 1):
            if c in self.over_z:
                self.arrived(c, 9)
            else:
                self.arrived(c, 7, 8)
        visit(7, p.zfar)


def attend_kernel(
    scale_ref, x_ref, drift_ref, mod_ref, w_hbm, wo_ref, paths_hbm, drift_hbm, bound_hbm,
    grads_ref, mixed_ref, normed_hbm, up_hbm,
    w_ref, full_ref, up_ref, moved, sq_out, sq_in, part, out_part, in_part,
    probs, outbox, in_half, in_full, gm_in, key_acc, value_acc,
    w_sems, sq_sems, n_send, n_recv, u_send, u_recv, kv_send, kv_recv, q_send, q_recv,
    tm_send, tm_recv, b_sems, rs_send, rs_recv, gm_send, gm_recv, store_sems, up_sems,
):
    p = Place()
    weight_copies = [
        pltpu.make_async_copy(w_hbm.at[j], w_ref.at[j], w_sems.at[j]) for j in range(3)
    ]
    for copy in weight_copies:
        copy.start()
    after = (lax.rem(p.t + 1, 8), p.r, p.c)
    before = (lax.rem(p.t + 7, 8), p.r, p.c)
    greet([p.row(p.right), p.row(p.left), p.row(p.z), p.col(), before], 5)

    squares = jnp.zeros((128, 1), F32)
    for i in range(4):
        piece = x_ref[:, i * 768 : (i + 1) * 768].astype(F32)
        squares = squares + jnp.sum(piece * piece, axis=-1, keepdims=True)
    sq_out[...] = jnp.broadcast_to(squares, (128, 128))
    swap = remote(sq_out, sq_in, sq_sems.at[0], sq_sems.at[1], p.col())
    swap.start()
    swap.wait()
    total = sq_out[:, :1] + sq_in[:, :1]
    scale = lax.rsqrt(total / D + norm_eps)
    gather = Gather(p, full_ref, n_send, n_recv, ())
    for i in range(4):
        cols = slice(i * 768, (i + 1) * 768)
        piece = x_ref[:, cols].astype(F32)
        full_ref[p.r, :, cols] = (
            piece * scale * (1.0 + mod_ref[0:1, cols]) + mod_ref[1:2, cols]
        ).astype(BF16)
        if i % 2 == 1:
            gather.send(i // 2, 0, 1, 2)

    moves = [
        remote(paths_hbm, moved.at[0], tm_send.at[0], tm_recv.at[0], after),
        remote(drift_hbm, moved.at[1], tm_send.at[1], tm_recv.at[1], after),
    ]
    bounds = [pltpu.make_async_copy(bound_hbm.at[i], moved.at[i], b_sems.at[i]) for i in (0, 1)]

    @pl.when(p.t < 7)
    def _():
        for move in moves:
            move.start()

    @pl.when(p.t == 0)
    def _():
        for copy in bounds:
            copy.start()

    kv_copies, q_copies = [], []

    def project(k, owner):
        if k == 0:
            for copy in weight_copies:
                copy.wait()

        @pl.loop(0, 3)
        def _(j):
            term = jnp.dot(full_ref[owner], w_ref[j], preferred_element_type=F32)
            part[k, j] = term
            out_part[k, j] = term.astype(BF16)

        pair = pl.ds(1, 2)
        copy = remote(
            out_part.at[k, pair], in_part.at[k, pair], kv_send.at[k], kv_recv.at[k], p.col()
        )
        copy.start()
        kv_copies.append(copy)
        q_copies.append(
            remote(out_part.at[k, 0], in_part.at[k, 0], q_send.at[k], q_recv.at[k], p.col())
        )

    gather.run(p, project)
    query_order = [7, 5, 6, 4, 1, 2, 3, 0]
    for k in query_order:
        q_copies[k].start()
    owners = [p.r, p.left, p.right, p.z, p.far, p.zleft, p.zright, p.zfar]
    store = pltpu.make_async_copy(full_ref, normed_hbm, store_sems.at[0])
    store.start()


    def rows_of(owner):
        return pl.ds(pl.multiple_of(owner * 128, 128), 128)

    def join(k, j):
        w_ref[j, rows_of(owners[k])] = (part[k, j] + in_part[k, j].astype(F32)).astype(BF16)

    for k in range(8):
        kv_copies[k].wait_recv()
        join(k, 1)
        join(k, 2)

    def keys(h):
        return w_ref[1, :1024, h * 128 : (h + 1) * 128]

    def values(h):
        return w_ref[2, :1024, h * 128 : (h + 1) * 128]

    def attend(owner):
        for h in range(3):
            cols = slice(h * 128, (h + 1) * 128)
            scores = (
                lax.dot_general(
                    w_ref[0, rows_of(owner), cols],
                    keys(h),
                    (((1,), (1,)), ((), ())),
                    preferred_element_type=F32,
                )
                * SCALE
            )
            top = jnp.max(scores, axis=-1, keepdims=True)
            weights = jnp.exp(scores - top)
            weights = weights * (1.0 / jnp.sum(weights, axis=-1, keepdims=True))
            weights_low = weights.astype(BF16)
            probs[h, owner] = weights_low
            mixed_ref[owner, :, cols] = jnp.dot(
                weights_low, values(h), preferred_element_type=F32
            ).astype(BF16)

    def ready(k):
        q_copies[k].wait_recv()
        join(k, 0)

    def out_rows(owner, c, lo, n, extra, put):
        @pl.loop(0, 2)
        def _(i):
            near = pl.ds(pl.multiple_of(i * 768, 768), 768)
            cols = pl.ds(pl.multiple_of(c * 1536 + i * 768, 768), 768)
            term = jnp.dot(
                mixed_ref[owner, lo : lo + n, :], wo_ref[:, cols], preferred_element_type=F32
            )
            for ref in extra:
                term = term + ref[:, near].astype(F32)
            put(cols, term)

    low, high, full = pl.ds(0, 64), pl.ds(64, 64), pl.ds(0, 128)
    plan = {
        "zfar low": (0, low, p.left, 0),
        "zfar high": (0, high, p.right, 1),
        "far low": (3, low, p.left, 2),
        "far high": (3, high, p.right, 3),
        "zfar": (0, full, p.z, 0),
        "zleft": (1, full, p.left, 1),
        "zright": (2, full, p.right, 2),
        "left": (4, full, p.left, 3),
        "right": (5, full, p.right, 4),
        "z": (6, full, p.z, 5),
    }
    copies, landed, started = {}, {}, []
    for c in (0, 1):
        for m, (name, (slot, rows, target, place)) in enumerate(plan.items()):
            i = 10 * c + m
            landed[name, c] = in_half.at[c, place] if m < 4 else in_full.at[c, place]
            copies[name, c] = remote(
                outbox.at[slot, rows, HALVES[c]],
                landed[name, c],
                rs_send.at[i],
                rs_recv.at[i],
                p.row(target),
            )

    def send(name, c):
        copies[name, c].start()
        started.append(copies[name, c])

    def arrived(*names_and_halves):
        for name, c in names_and_halves:
            copies[name, c].wait_recv()

    def to_slot(slot, lo, n):
        def put(cols, term):
            outbox[slot, lo : lo + n, cols] = term.astype(BF16)

        return put

    def share(slot, owner, c, lo=0, n=128, extra=()):
        out_rows(owner, c, lo, n, [landed[name, c] for name in extra], to_slot(slot, lo, n))

    ready(7)
    attend(p.zfar)
    share(0, p.zfar, 0)
    send("zfar low", 0)
    send("zfar high", 0)
    share(0, p.zfar, 1)
    send("zfar", 1)
    ready(5)
    attend(p.zleft)
    share(1, p.zleft, 1)
    send("zleft", 1)
    ready(6)
    attend(p.zright)
    share(2, p.zright, 1)
    send("zright", 1)
    share(1, p.zleft, 0, 64, 64)
    share(2, p.zright, 0, 0, 64)
    arrived(("zfar low", 0))
    share(1, p.zleft, 0, 0, 64, ["zfar low"])
    send("zleft", 0)
    arrived(("zfar high", 0))
    share(2, p.zright, 0, 64, 64, ["zfar high"])
    send("zright", 0)
    ready(4)
    attend(p.far)
    share(3, p.far, 0)
    send("far low", 0)
    send("far high", 0)
    for k in (1, 2, 3, 0):
        ready(k)

    @pl.loop(0, 4)
    def _(i):
        attend(
            jnp.where(
                i == 0, p.left, jnp.where(i == 1, p.right, jnp.where(i == 2, p.z, p.r))
            )
        )

    arrived(("zfar", 1))
    share(3, p.far, 1, extra=["zfar"])
    send("far low", 1)
    send("far high", 1)
    for c in (1, 0):
        arrived(("zleft", c), ("zright", c))
        share(6, p.z, c, extra=["zleft", "zright"])
        send("z", c)
    for c in (0, 1):
        share(4, p.left, c, 64, 64)
        share(5, p.right, c, 0, 64)
        arrived(("far low", c))
        share(4, p.left, c, 0, 64, ["far low"])
        send("left", c)
        arrived(("far high", c))
        share(5, p.right, c, 64, 64, ["far high"])
        send("right", c)

    @pl.when(p.t > 0)
    def _():
        for move in moves:
            move.wait_recv()

    @pl.when(p.t == 0)
    def _():
        for copy in bounds:
            copy.wait()

    key_acc[...] = jnp.zeros_like(key_acc)
    value_acc[...] = jnp.zeros_like(value_acc)

    def to_up(cols, term):
        target = moved[0, :, cols].astype(F32) + scale_ref[0] * (
            moved[1, :, cols].astype(F32) - drift_ref[:, cols].astype(F32)
        )
        rest = x_ref[:, cols].astype(F32) - target
        up_ref[p.r, :, cols] = ((rest + term) * (1024**-0.5)).astype(BF16)

    gather_up = Gather(p, up_ref, u_send, u_recv, (1,))
    for c in (0, 1):
        names = ["left", "right", "z"]
        arrived(*[(name, c) for name in names])
        out_rows(p.r, c, 0, 128, [landed[name, c] for name in names], to_up)
        gather_up.send(c, 0, 1, 2)

    gm_copies, stores, waiting = [], [], []

    def backward(k, owner):
        gm_copies[k].wait_recv()
        grad = (part[k, 0] + gm_in[k].astype(F32)).astype(BF16)
        tokens = rows_of(owner)
        for h in range(3):
            cols = slice(h * 128, (h + 1) * 128)
            head_grad = grad[:, cols]
            weights_low = probs[h, owner]
            weights = weights_low.astype(F32)
            value_acc[h] += jnp.dot(head_grad.T, weights_low, preferred_element_type=F32)
            grad_weights = lax.dot_general(
                head_grad, values(h), (((1,), (1,)), ((), ())), preferred_element_type=F32
            )
            inner = jnp.sum(grad_weights * weights, axis=-1, keepdims=True)
            grad_scores = (weights * (grad_weights - inner) * SCALE).astype(BF16)
            query_grad = jnp.dot(grad_scores, keys(h), preferred_element_type=F32)
            grads_ref[0, cols, tokens] = query_grad.T.astype(BF16)
            key_acc[h] += jnp.dot(
                w_ref[0, rows_of(owner), cols].T, grad_scores, preferred_element_type=F32
            )

    def visit(k, owner):
        term = lax.dot_general(
            up_ref[owner], wo_ref[...], (((1,), (1,)), ((), ())), preferred_element_type=F32
        )
        part[k, 0] = term
        kv_copies[k].wait_send()
        out_part[k, 1] = term.astype(BF16)
        copy = remote(out_part.at[k, 1], gm_in.at[k], gm_send.at[k], gm_recv.at[k], p.col())
        copy.start()
        gm_copies.append(copy)
        stores.append(pltpu.make_async_copy(up_ref.at[owner], up_hbm.at[owner], up_sems.at[k]))
        stores[-1].start()
        if waiting:
            backward(*waiting.pop())
        waiting.append((k, owner))

    gather_up.run(p, visit)
    backward(*waiting.pop())
    for h in range(3):
        cols = slice(h * 128, (h + 1) * 128)
        grads_ref[1, cols, :] = key_acc[h].astype(BF16)
        grads_ref[2, cols, :] = value_acc[h].astype(BF16)
    for copy in q_copies + started + gm_copies:
        copy.wait_send()
    gather.finish()
    gather_up.finish()

    @pl.when(p.t < 7)
    def _():
        for move in moves:
            move.wait_send()

    store.wait()
    for copy in stores:
        copy.wait()


def attend(scale, x, drift, mod, w, wo, bound):
    vmem = pl.BlockSpec(memory_space=pltpu.VMEM)
    smem = pl.BlockSpec(memory_space=pltpu.SMEM)
    hbm = pl.BlockSpec(memory_space=pl.ANY)
    dma = pltpu.SemaphoreType.DMA
    return pl.pallas_call(
        attend_kernel,
        out_shape=(
            jax.ShapeDtypeStruct((3, 384, 1024), BF16),
            jax.ShapeDtypeStruct((8, 128, 384), BF16),
            jax.ShapeDtypeStruct((8, 128, 3072), BF16),
            jax.ShapeDtypeStruct((8, 128, 3072), BF16),
        ),
        in_specs=[smem, vmem, vmem, vmem, hbm, vmem, hbm, hbm, hbm],
        out_specs=(vmem, vmem, hbm, hbm),
        scratch_shapes=[
            pltpu.VMEM((3, 3072, 384), BF16),
            pltpu.VMEM((8, 128, 3072), BF16),
            pltpu.VMEM((8, 128, 3072), BF16),
            pltpu.VMEM((2, 128, 3072), BF16),
            pltpu.VMEM((128, 128), F32),
            pltpu.VMEM((128, 128), F32),
            pltpu.VMEM((8, 3, 128, 384), F32),
            pltpu.VMEM((8, 3, 128, 384), BF16),
            pltpu.VMEM((8, 3, 128, 384), BF16),
            pltpu.VMEM((3, 8, 128, 1024), BF16),
            pltpu.VMEM((7, 128, 3072), BF16),
            pltpu.VMEM((2, 4, 64, 1536), BF16),
            pltpu.VMEM((2, 6, 128, 1536), BF16),
            pltpu.VMEM((8, 128, 384), BF16),
            pltpu.VMEM((3, 128, 1024), F32),
            pltpu.VMEM((3, 128, 1024), F32),
            dma((3,)),
            dma((2,)),
            dma((20,)),
            dma((20,)),
            dma((20,)),
            dma((20,)),
            dma((8,)),
            dma((8,)),
            dma((8,)),
            dma((8,)),
            dma((2,)),
            dma((2,)),
            dma((2,)),
            dma((20,)),
            dma((20,)),
            dma((8,)),
            dma((8,)),
            dma((1,)),
            dma((8,)),
        ],
        name="attend",
        cost_estimate=pl.CostEstimate(
            flops=20_000_000_000, bytes_accessed=30_000_000, transcendentals=3 * 1024 * 1024
        ),
        compiler_params=pltpu.CompilerParams(
            collective_id=2, has_side_effects=True, vmem_limit_bytes=62 * 1024 * 1024
        ),
    )(scale, x, drift, mod, w, wo, x, drift, bound)


def reduce_kernel(
    grads_ref, mixed_ref, normed_hbm, up_hbm,
    in_ref, out_ref,
    mixed_t, normed, up, core_out, core_in, y_out, y_in, left_low, right_high, own,
    normed_sems, up_sems, core_send, core_recv, y_send, y_recv,
):
    p = Place()
    core = lax.rem(p.t, 2)
    y = p.t // 2
    peers = [lax.rem(y + by, 4) for by in (2, 3, 1, 0)]
    theirs = [2 * peer + 1 - core for peer in peers]
    mine = [2 * peer + core for peer in peers]
    order = [
        theirs[0], theirs[1], mine[0], theirs[2], mine[1], theirs[3], mine[2], mine[3],
    ]
    loads = []
    for k, owner in enumerate(order):
        cols = pl.ds(pl.multiple_of(owner * 384, 384), 384)
        loads.append(
            (
                pltpu.make_async_copy(normed_hbm.at[:, :, cols], normed.at[k], normed_sems.at[k]),
                pltpu.make_async_copy(up_hbm.at[:, :, cols], up.at[k], up_sems.at[k]),
            )
        )
        for copy in loads[-1]:
            copy.start()
    partner = (2 * y + 1 - core, p.r, p.c)
    to_left = (2 * peers[1] + core, p.r, p.c)
    to_right = (2 * peers[2] + core, p.r, p.c)
    greet([partner, to_left, to_right], 3)
    mixed_t[...] = mixed_ref[...].reshape(1024, 384).T

    def chunk(k, put):
        for copy in loads[k]:
            copy.wait()

        @pl.loop(0, 3)
        def _(j):
            put(
                j,
                jnp.dot(
                    grads_ref[j], normed[k].reshape(1024, 384), preferred_element_type=F32
                ),
            )

        put(3, jnp.dot(mixed_t[...], up[k].reshape(1024, 384), preferred_element_type=F32))

    core_copies = [
        remote(core_out.at[i], core_in.at[i], core_send.at[i], core_recv.at[i], partner)
        for i in range(4)
    ]
    low, high = pl.ds(0, 2), pl.ds(2, 2)
    messages = [
        (y_out.at[0, low], to_left),
        (y_out.at[0, high], to_right),
        (y_out.at[1, high], to_left),
        (y_out.at[2, low], to_right),
        (y_out.at[1, low], to_left),
        (y_out.at[2, high], to_right),
    ]
    y_copies = [
        remote(src, y_in.at[i], y_send.at[i], y_recv.at[i], device)
        for i, (src, device) in enumerate(messages)
    ]

    def for_partner(k, i):
        def put(j, term):
            core_out[i, j] = term.astype(BF16)

        chunk(k, put)
        core_copies[i].start()

    def for_far(j, term):
        y_out[0, j] = (term + core_in[0, j].astype(F32)).astype(BF16)

    def for_left(j, term):
        total = term + core_in[1, j].astype(F32)
        y_out[1, j] = total.astype(BF16)
        left_low[j] = total

    def for_right(j, term):
        total = term + core_in[2, j].astype(F32)
        y_out[2, j] = total.astype(BF16)
        right_high[j] = total

    def for_own(j, term):
        own[j] = term + core_in[3, j].astype(F32)

    for_partner(0, 0)
    for_partner(1, 1)
    core_copies[0].wait_recv()
    chunk(2, for_far)
    y_copies[0].start()
    y_copies[1].start()
    for_partner(3, 2)
    core_copies[1].wait_recv()
    chunk(4, for_left)
    y_copies[2].start()
    for_partner(5, 3)
    core_copies[2].wait_recv()
    chunk(6, for_right)
    y_copies[3].start()
    core_copies[3].wait_recv()
    chunk(7, for_own)
    y_copies[0].wait_recv()
    for j in (0, 1):
        y_out[1, j] = (left_low[j] + y_in[0, j].astype(F32)).astype(BF16)
    y_copies[4].start()
    y_copies[1].wait_recv()
    for j in (2, 3):
        y_out[2, j] = (right_high[j] + y_in[1, j - 2].astype(F32)).astype(BF16)
    y_copies[5].start()
    y_copies[2].wait_recv()
    y_copies[3].wait_recv()
    for j in (0, 1):
        own[j] += y_in[3, j].astype(F32)
        own[j + 2] += y_in[2, j].astype(F32)
    y_copies[4].wait_recv()
    for j in (0, 1):
        in_ref[j] = own[j] + y_in[4, j].astype(F32)
    y_copies[5].wait_recv()
    in_ref[2] = own[2] + y_in[5, 0].astype(F32)
    out_ref[...] = own[3] + y_in[5, 1].astype(F32)
    for copy in core_copies + y_copies:
        copy.wait_send()


def reduce(grads, mixed, normed, up):
    vmem = pl.BlockSpec(memory_space=pltpu.VMEM)
    hbm = pl.BlockSpec(memory_space=pl.ANY)
    dma = pltpu.SemaphoreType.DMA
    return pl.pallas_call(
        reduce_kernel,
        out_shape=(
            jax.ShapeDtypeStruct((3, 384, 384), F32),
            jax.ShapeDtypeStruct((384, 384), F32),
        ),
        in_specs=[vmem, vmem, hbm, hbm],
        out_specs=(vmem, vmem),
        scratch_shapes=[
            pltpu.VMEM((384, 1024), BF16),
            pltpu.VMEM((8, 8, 128, 384), BF16),
            pltpu.VMEM((8, 8, 128, 384), BF16),
            pltpu.VMEM((4, 4, 384, 384), BF16),
            pltpu.VMEM((4, 4, 384, 384), BF16),
            pltpu.VMEM((3, 4, 384, 384), BF16),
            pltpu.VMEM((6, 2, 384, 384), BF16),
            pltpu.VMEM((4, 384, 384), F32),
            pltpu.VMEM((4, 384, 384), F32),
            pltpu.VMEM((4, 384, 384), F32),
            dma((8,)),
            dma((8,)),
            dma((4,)),
            dma((4,)),
            dma((6,)),
            dma((6,)),
        ],
        name="reduce",
        cost_estimate=pl.CostEstimate(
            flops=2 * 1024 * 3072 * 1536, bytes_accessed=20_000_000, transcendentals=0
        ),
        compiler_params=pltpu.CompilerParams(
            collective_id=3, has_side_effects=True, vmem_limit_bytes=VMEM_LIMIT
        ),
    )(grads, mixed, normed, up)


def body(paths, prev_drift, boundary, step_scale, time_ids, mod_table, w_qkv, output_weight):
    modulation = lax.dynamic_index_in_dim(mod_table, time_ids[0], 0, keepdims=False).astype(F32)
    w = jnp.transpose(w_qkv, (1, 0, 2))
    grads, mixed, normed, upstream = attend(
        step_scale, paths[0], prev_drift[0], modulation, w, output_weight, boundary
    )
    grad_in_sum, grad_out_sum = reduce(grads, mixed, normed, upstream)
    grad_in_sum = jnp.transpose(grad_in_sum, (2, 0, 1))
    return (grad_in_sum, grad_out_sum)


def solution(mesh):
    placed = (
        P("tm", "row", "col"),
        P("tm", "row", "col"),
        P(None, "row", "col"),
        P("tm"),
        P("tm"),
        P(None, None, "col"),
        P("col", None, "row"),
        P("row", "col"),
    )
    return jax.shard_map(
        body,
        mesh=mesh,
        in_specs=placed,
        out_specs=(P(("col", "tm"), None, "row"), P("row", ("col", "tm"))),
        check_vma=False,
    )
```

```python
import jax
import jax.numpy as jnp
from jax import lax
from jax.experimental import pallas as pl
from jax.experimental.pallas import tpu as pltpu
from jax.sharding import PartitionSpec as P

D = 6144
HEAD_DIM = 128
SCALE = HEAD_DIM**-0.5
MESH = pl.DeviceIdType.MESH
VMEM_LIMIT = 60 * 1024 * 1024

norm_eps = 1e-06

BF16 = jnp.bfloat16
F32 = jnp.float32
HALVES = (pl.ds(0, 1536), pl.ds(1536, 1536))


class Place:
    def __init__(self):
        self.t = lax.axis_index("tm")
        self.r = lax.axis_index("row")
        self.c = lax.axis_index("col")
        x = lax.rem(self.r, 4)
        base = self.r - x
        other = lax.rem(base + 4, 8)
        self.left = base + lax.rem(x + 3, 4)
        self.right = base + lax.rem(x + 1, 4)
        self.far = base + lax.rem(x + 2, 4)
        self.z = other + x
        self.zleft = other + lax.rem(x + 3, 4)
        self.zright = other + lax.rem(x + 1, 4)
        self.zfar = other + lax.rem(x + 2, 4)

    def row(self, r):
        return (self.t, r, self.c)

    def col(self):
        return (self.t, self.r, 1 - self.c)


def greet(signalled, awaited):
    barrier = pltpu.get_barrier_semaphore()
    for device in signalled:
        pl.semaphore_signal(barrier, inc=1, device_id=device, device_id_type=MESH)
    pl.semaphore_wait(barrier, awaited)


def remote(src, dst, send_sem, recv_sem, device):
    return pltpu.make_async_remote_copy(
        src_ref=src,
        dst_ref=dst,
        send_sem=send_sem,
        recv_sem=recv_sem,
        device_id=device,
        device_id_type=MESH,
    )


class Gather:
    def __init__(self, place, buf, send_sems, recv_sems, over_z):
        p = place
        self.over_z = over_z
        low, high, full = pl.ds(0, 64), pl.ds(64, 64), pl.ds(0, 128)
        plan = [
            (p.r, p.left, full, p.right),
            (p.r, p.right, full, p.left),
            (p.r, p.z, full, p.z),
            (p.left, p.far, low, p.right),
            (p.right, p.far, high, p.left),
            (p.z, p.zleft, full, p.right),
            (p.z, p.zright, full, p.left),
            (p.zleft, p.zfar, low, p.right),
            (p.zright, p.zfar, high, p.left),
            (p.far, p.zfar, full, p.z),
        ]
        self.out, self.into, self.started = {}, {}, []
        for c in (0, 1):
            for m, (sent, received, rows, target) in enumerate(plan):
                i = 10 * c + m
                device = p.row(target)
                a, b = buf.at[sent, rows, HALVES[c]], buf.at[received, rows, HALVES[c]]
                self.out[m, c] = remote(a, a, send_sems.at[i], recv_sems.at[i], device)
                self.into[m, c] = remote(b, b, send_sems.at[i], recv_sems.at[i], device)

    def send(self, c, *which):
        for m in which:
            self.out[m, c].start()
            self.started.append(self.out[m, c])

    def arrived(self, c, *which):
        for m in which:
            self.into[m, c].wait_recv()

    def finish(self):
        for copy in self.started:
            copy.wait_send()

    def run(self, place, visit, spare=None):
        p = place
        visit(0, p.r)
        for c in (0, 1):
            self.arrived(c, 0)
            self.send(c, 3)
            self.arrived(c, 1)
            self.send(c, 4)
            self.arrived(c, 2)
            self.send(c, 5, 6)
        visit(1, p.left)
        visit(2, p.right)
        for c in (0, 1):
            self.arrived(c, 3, 4)
            if c in self.over_z:
                self.send(c, 9)
        visit(3, p.z)
        visit(4, p.far)
        for c in (0, 1):
            self.arrived(c, 5)
            if c not in self.over_z:
                self.send(c, 7)
            self.arrived(c, 6)
            if c not in self.over_z:
                self.send(c, 8)
        visit(5, p.zleft)
        visit(6, p.zright)
        if spare is not None:
            spare()
        for c in (0, 1):
            if c in self.over_z:
                self.arrived(c, 9)
            else:
                self.arrived(c, 7, 8)
        visit(7, p.zfar)


def attend_kernel(
    scale_ref, x_ref, mod_ref, w_hbm, wo_hbm, paths_hbm, drift_hbm, bound_hbm,
    grads_ref, mixed_ref, normed_hbm, up_hbm,
    w_ref, wo_ref, drift_ref, full_ref, up_ref, moved, sq_out, sq_in, part, out_part, in_part,
    probs, outbox, in_half, in_full, gm_in, key_acc, value_acc,
    w_sems, late_sems, sq_sems, n_send, n_recv, u_send, u_recv, kv_send, kv_recv, q_send, q_recv,
    tm_send, tm_recv, b_sems, rs_send, rs_recv, gm_send, gm_recv, store_sems, up_sems,
):
    p = Place()
    weight_copies = [
        pltpu.make_async_copy(w_hbm.at[j], w_ref.at[j], w_sems.at[j]) for j in range(3)
    ]
    late_copies = [
        pltpu.make_async_copy(wo_hbm, wo_ref, late_sems.at[0]),
        pltpu.make_async_copy(drift_hbm, drift_ref, late_sems.at[1]),
    ]
    for copy in weight_copies + late_copies:
        copy.start()
    after = (lax.rem(p.t + 1, 8), p.r, p.c)
    before = (lax.rem(p.t + 7, 8), p.r, p.c)
    greet([p.row(p.right), p.row(p.left), p.row(p.z), p.col(), before], 5)

    squares = jnp.zeros((128, 1), F32)
    for i in range(4):
        piece = x_ref[:, i * 768 : (i + 1) * 768].astype(F32)
        squares = squares + jnp.sum(piece * piece, axis=-1, keepdims=True)
    sq_out[...] = jnp.broadcast_to(squares, (128, 128))
    swap = remote(sq_out, sq_in, sq_sems.at[0], sq_sems.at[1], p.col())
    swap.start()
    swap.wait()
    total = sq_out[:, :1] + sq_in[:, :1]
    scale = lax.rsqrt(total / D + norm_eps)
    gather = Gather(p, full_ref, n_send, n_recv, ())
    for i in range(4):
        cols = slice(i * 768, (i + 1) * 768)
        piece = x_ref[:, cols].astype(F32)
        full_ref[p.r, :, cols] = (
            piece * scale * (1.0 + mod_ref[0:1, cols]) + mod_ref[1:2, cols]
        ).astype(BF16)
        if i % 2 == 1:
            gather.send(i // 2, 0, 1, 2)

    moves = [
        remote(paths_hbm, moved.at[0], tm_send.at[0], tm_recv.at[0], after),
        remote(drift_hbm, moved.at[1], tm_send.at[1], tm_recv.at[1], after),
    ]
    bounds = [pltpu.make_async_copy(bound_hbm.at[i], moved.at[i], b_sems.at[i]) for i in (0, 1)]

    @pl.when(p.t < 7)
    def _():
        for move in moves:
            move.start()

    @pl.when(p.t == 0)
    def _():
        for copy in bounds:
            copy.start()

    kv_copies, q_copies = [], []

    def project(k, owner):
        if k == 0:
            for copy in weight_copies:
                copy.wait()

        def product(j):
            term = jnp.dot(full_ref[owner], w_ref[j], preferred_element_type=F32)
            part[k, j] = term
            out_part[k, j] = term.astype(BF16)

        @pl.loop(1, 3)
        def _(j):
            product(j)

        pair = pl.ds(1, 2)
        copy = remote(
            out_part.at[k, pair], in_part.at[k, pair], kv_send.at[k], kv_recv.at[k], p.col()
        )
        copy.start()
        kv_copies.append(copy)
        product(0)
        q_copies.append(
            remote(out_part.at[k, 0], in_part.at[k, 0], q_send.at[k], q_recv.at[k], p.col())
        )

    owners = [p.r, p.left, p.right, p.z, p.far, p.zleft, p.zright, p.zfar]

    def rows_of(owner):
        return pl.ds(pl.multiple_of(owner * 128, 128), 128)

    def join_early():
        for copy in late_copies:
            copy.wait()
        for k in range(5):
            kv_copies[k].wait_recv()
            for j in (1, 2):
                part[k, j] += in_part[k, j].astype(F32)

    gather.run(p, project, join_early)
    query_order = [7, 5, 6, 4, 1, 2, 3, 0]
    for k in query_order:
        q_copies[k].start()
    store = pltpu.make_async_copy(full_ref, normed_hbm, store_sems.at[0])
    store.start()


    def join(k, j):
        w_ref[j, rows_of(owners[k])] = (part[k, j] + in_part[k, j].astype(F32)).astype(BF16)

    for k in range(5):
        for j in (1, 2):
            w_ref[j, rows_of(owners[k])] = part[k, j].astype(BF16)
    for k in (5, 6, 7):
        kv_copies[k].wait_recv()
        join(k, 1)
        join(k, 2)

    def keys(h):
        return w_ref[1, :1024, h * 128 : (h + 1) * 128]

    def values(h):
        return w_ref[2, :1024, h * 128 : (h + 1) * 128]

    def attend(owner):
        for h in range(3):
            cols = slice(h * 128, (h + 1) * 128)
            scores = (
                lax.dot_general(
                    w_ref[0, rows_of(owner), cols],
                    keys(h),
                    (((1,), (1,)), ((), ())),
                    preferred_element_type=F32,
                )
                * SCALE
            )
            top = jnp.max(scores, axis=-1, keepdims=True)
            weights = jnp.exp(scores - top)
            weights = weights * (1.0 / jnp.sum(weights, axis=-1, keepdims=True))
            weights_low = weights.astype(BF16)
            probs[h, owner] = weights_low
            mixed_ref[owner, :, cols] = jnp.dot(
                weights_low, values(h), preferred_element_type=F32
            ).astype(BF16)

    def ready(k):
        q_copies[k].wait_recv()
        join(k, 0)

    def out_rows(owner, c, lo, n, extra, put):
        @pl.loop(0, 2)
        def _(i):
            near = pl.ds(pl.multiple_of(i * 768, 768), 768)
            cols = pl.ds(pl.multiple_of(c * 1536 + i * 768, 768), 768)
            term = jnp.dot(
                mixed_ref[owner, lo : lo + n, :], wo_ref[:, cols], preferred_element_type=F32
            )
            for ref in extra:
                term = term + ref[:, near].astype(F32)
            put(cols, term)

    low, high, full = pl.ds(0, 64), pl.ds(64, 64), pl.ds(0, 128)
    plan = {
        "zfar low": (0, low, p.left, 0),
        "zfar high": (0, high, p.right, 1),
        "far low": (3, low, p.left, 2),
        "far high": (3, high, p.right, 3),
        "zfar": (0, full, p.z, 0),
        "zleft": (1, full, p.left, 1),
        "zright": (2, full, p.right, 2),
        "left": (4, full, p.left, 3),
        "right": (5, full, p.right, 4),
        "z": (6, full, p.z, 5),
    }
    copies, landed, started = {}, {}, []
    for c in (0, 1):
        for m, (name, (slot, rows, target, place)) in enumerate(plan.items()):
            i = 10 * c + m
            landed[name, c] = in_half.at[c, place] if m < 4 else in_full.at[c, place]
            copies[name, c] = remote(
                outbox.at[slot, rows, HALVES[c]],
                landed[name, c],
                rs_send.at[i],
                rs_recv.at[i],
                p.row(target),
            )

    def send(name, c):
        copies[name, c].start()
        started.append(copies[name, c])

    def arrived(*names_and_halves):
        for name, c in names_and_halves:
            copies[name, c].wait_recv()

    def to_slot(slot, lo, n):
        def put(cols, term):
            outbox[slot, lo : lo + n, cols] = term.astype(BF16)

        return put

    def share(slot, owner, c, lo=0, n=128, extra=()):
        out_rows(owner, c, lo, n, [landed[name, c] for name in extra], to_slot(slot, lo, n))

    ready(7)
    attend(p.zfar)
    share(0, p.zfar, 0)
    send("zfar low", 0)
    send("zfar high", 0)
    share(0, p.zfar, 1)
    send("zfar", 1)
    ready(5)
    attend(p.zleft)
    share(1, p.zleft, 1)
    send("zleft", 1)
    ready(6)
    attend(p.zright)
    share(2, p.zright, 1)
    send("zright", 1)
    share(1, p.zleft, 0, 64, 64)
    share(2, p.zright, 0, 0, 64)
    arrived(("zfar low", 0))
    share(1, p.zleft, 0, 0, 64, ["zfar low"])
    send("zleft", 0)
    arrived(("zfar high", 0))
    share(2, p.zright, 0, 64, 64, ["zfar high"])
    send("zright", 0)
    ready(4)
    attend(p.far)
    share(3, p.far, 0)
    send("far low", 0)
    send("far high", 0)
    for k in (1, 2, 3, 0):
        ready(k)

    @pl.loop(0, 4)
    def _(i):
        attend(
            jnp.where(
                i == 0, p.left, jnp.where(i == 1, p.right, jnp.where(i == 2, p.z, p.r))
            )
        )

    arrived(("zfar", 1))
    share(3, p.far, 1, extra=["zfar"])
    send("far low", 1)
    send("far high", 1)
    for c in (1, 0):
        arrived(("zleft", c), ("zright", c))
        share(6, p.z, c, extra=["zleft", "zright"])
        send("z", c)
    for c in (0, 1):
        share(4, p.left, c, 64, 64)
        share(5, p.right, c, 0, 64)
        arrived(("far low", c))
        share(4, p.left, c, 0, 64, ["far low"])
        send("left", c)
        arrived(("far high", c))
        share(5, p.right, c, 64, 64, ["far high"])
        send("right", c)

    @pl.when(p.t > 0)
    def _():
        for move in moves:
            move.wait_recv()

    @pl.when(p.t == 0)
    def _():
        for copy in bounds:
            copy.wait()

    key_acc[...] = jnp.zeros_like(key_acc)
    value_acc[...] = jnp.zeros_like(value_acc)

    def to_up(cols, term):
        target = moved[0, :, cols].astype(F32) + scale_ref[0] * (
            moved[1, :, cols].astype(F32) - drift_ref[:, cols].astype(F32)
        )
        rest = x_ref[:, cols].astype(F32) - target
        up_ref[p.r, :, cols] = ((rest + term) * (1024**-0.5)).astype(BF16)

    gather_up = Gather(p, up_ref, u_send, u_recv, (1,))
    for c in (0, 1):
        names = ["left", "right", "z"]
        arrived(*[(name, c) for name in names])
        out_rows(p.r, c, 0, 128, [landed[name, c] for name in names], to_up)
        gather_up.send(c, 0, 1, 2)

    gm_copies, stores, waiting = [], [], []

    def backward(k, owner):
        gm_copies[k].wait_recv()
        grad = (part[k, 0] + gm_in[k].astype(F32)).astype(BF16)
        tokens = rows_of(owner)
        for h in range(3):
            cols = slice(h * 128, (h + 1) * 128)
            head_grad = grad[:, cols]
            weights_low = probs[h, owner]
            weights = weights_low.astype(F32)
            value_acc[h] += jnp.dot(head_grad.T, weights_low, preferred_element_type=F32)
            grad_weights = lax.dot_general(
                head_grad, values(h), (((1,), (1,)), ((), ())), preferred_element_type=F32
            )
            inner = jnp.sum(grad_weights * weights, axis=-1, keepdims=True)
            grad_scores = (weights * (grad_weights - inner) * SCALE).astype(BF16)
            query_grad = jnp.dot(grad_scores, keys(h), preferred_element_type=F32)
            grads_ref[0, cols, tokens] = query_grad.T.astype(BF16)
            key_acc[h] += jnp.dot(
                w_ref[0, rows_of(owner), cols].T, grad_scores, preferred_element_type=F32
            )

    def visit(k, owner):
        term = lax.dot_general(
            up_ref[owner], wo_ref[...], (((1,), (1,)), ((), ())), preferred_element_type=F32
        )
        part[k, 0] = term
        kv_copies[k].wait_send()
        out_part[k, 1] = term.astype(BF16)
        copy = remote(out_part.at[k, 1], gm_in.at[k], gm_send.at[k], gm_recv.at[k], p.col())
        copy.start()
        gm_copies.append(copy)
        stores.append(pltpu.make_async_copy(up_ref.at[owner], up_hbm.at[owner], up_sems.at[k]))
        stores[-1].start()
        if waiting:
            backward(*waiting.pop())
        waiting.append((k, owner))

    gather_up.run(p, visit)
    backward(*waiting.pop())
    for h in range(3):
        cols = slice(h * 128, (h + 1) * 128)
        grads_ref[1, cols, :] = key_acc[h].astype(BF16)
        grads_ref[2, cols, :] = value_acc[h].astype(BF16)
    for copy in q_copies + started + gm_copies:
        copy.wait_send()
    gather.finish()
    gather_up.finish()

    @pl.when(p.t < 7)
    def _():
        for move in moves:
            move.wait_send()

    store.wait()
    for copy in stores:
        copy.wait()


def attend(scale, x, drift, mod, w, wo, bound):
    vmem = pl.BlockSpec(memory_space=pltpu.VMEM)
    smem = pl.BlockSpec(memory_space=pltpu.SMEM)
    hbm = pl.BlockSpec(memory_space=pl.ANY)
    dma = pltpu.SemaphoreType.DMA
    return pl.pallas_call(
        attend_kernel,
        out_shape=(
            jax.ShapeDtypeStruct((3, 384, 1024), BF16),
            jax.ShapeDtypeStruct((8, 128, 384), BF16),
            jax.ShapeDtypeStruct((8, 128, 3072), BF16),
            jax.ShapeDtypeStruct((8, 128, 3072), BF16),
        ),
        in_specs=[smem, vmem, vmem, hbm, hbm, hbm, hbm, hbm],
        out_specs=(vmem, vmem, hbm, hbm),
        scratch_shapes=[
            pltpu.VMEM((3, 3072, 384), BF16),
            pltpu.VMEM((384, 3072), BF16),
            pltpu.VMEM((128, 3072), BF16),
            pltpu.VMEM((8, 128, 3072), BF16),
            pltpu.VMEM((8, 128, 3072), BF16),
            pltpu.VMEM((2, 128, 3072), BF16),
            pltpu.VMEM((128, 128), F32),
            pltpu.VMEM((128, 128), F32),
            pltpu.VMEM((8, 3, 128, 384), F32),
            pltpu.VMEM((8, 3, 128, 384), BF16),
            pltpu.VMEM((8, 3, 128, 384), BF16),
            pltpu.VMEM((3, 8, 128, 1024), BF16),
            pltpu.VMEM((7, 128, 3072), BF16),
            pltpu.VMEM((2, 4, 64, 1536), BF16),
            pltpu.VMEM((2, 6, 128, 1536), BF16),
            pltpu.VMEM((8, 128, 384), BF16),
            pltpu.VMEM((3, 128, 1024), F32),
            pltpu.VMEM((3, 128, 1024), F32),
            dma((3,)),
            dma((2,)),
            dma((2,)),
            dma((20,)),
            dma((20,)),
            dma((20,)),
            dma((20,)),
            dma((8,)),
            dma((8,)),
            dma((8,)),
            dma((8,)),
            dma((2,)),
            dma((2,)),
            dma((2,)),
            dma((20,)),
            dma((20,)),
            dma((8,)),
            dma((8,)),
            dma((1,)),
            dma((8,)),
        ],
        name="attend",
        cost_estimate=pl.CostEstimate(
            flops=20_000_000_000, bytes_accessed=30_000_000, transcendentals=3 * 1024 * 1024
        ),
        compiler_params=pltpu.CompilerParams(
            collective_id=2, has_side_effects=True, vmem_limit_bytes=62 * 1024 * 1024
        ),
    )(scale, x, mod, w, wo, x, drift, bound)


def reduce_kernel(
    grads_ref, mixed_ref, normed_hbm, up_hbm,
    in_ref, out_ref,
    mixed_t, normed, up, core_out, core_in, y_out, y_in, own,
    normed_sems, up_sems, core_send, core_recv, y_send, y_recv,
):
    p = Place()
    core = lax.rem(p.t, 2)
    y = p.t // 2
    peers = [lax.rem(y + by, 4) for by in (2, 3, 1, 0)]
    owners = [2 * peer + 1 - core for peer in peers] + [2 * peer + core for peer in peers]
    loads = {}
    for k in (0, 4, 1, 2, 5, 6, 3, 7):
        cols = pl.ds(pl.multiple_of(owners[k] * 384, 384), 384)
        loads[k] = [
            pltpu.make_async_copy(normed_hbm.at[:, :, cols], normed.at[k], normed_sems.at[k]),
            pltpu.make_async_copy(up_hbm.at[:, :, cols], up.at[k], up_sems.at[k]),
        ]
        for copy in loads[k]:
            copy.start()
    partner = (2 * y + 1 - core, p.r, p.c)
    to_left = (2 * peers[1] + core, p.r, p.c)
    to_right = (2 * peers[2] + core, p.r, p.c)
    greet([partner, to_left, to_right], 3)

    def unit(k, g):
        for copy in loads.pop(k, ()):
            copy.wait()
        left = grads_ref[g] if g < 3 else mixed_t[...]
        right = normed[k] if g < 3 else up[k]
        term = jnp.dot(left, right.reshape(1024, 384), preferred_element_type=F32)
        return term.reshape(3, 128, 384)

    core_copies = {}
    for i in range(4):
        for g in range(4):
            n = 4 * i + g
            core_copies[i, g] = remote(
                core_out.at[n], core_in.at[n], core_send.at[n], core_recv.at[n], partner
            )
    y_copies = {}
    for i in range(3):
        for g in range(4):
            n = 4 * i + g
            leftward = g < 2 if i == 0 else i == 1
            y_copies[i, g] = remote(
                y_out.at[n], y_in.at[n], y_send.at[n], y_recv.at[n],
                to_left if leftward else to_right,
            )

    def for_partner(i, *groups):
        for g in groups:
            core_out[4 * i + g] = unit(i, g).astype(BF16)
            core_copies[i, g].start()

    def summed(i, g):
        term = unit(4 + i, g)
        core_copies[i, g].wait_recv()
        return term + core_in[4 * i + g].astype(F32)

    def onward(i, g):
        total = summed(i, g)
        if (i, g) in ((1, 0), (1, 1), (2, 2), (2, 3)):
            y_copies[0, g].wait_recv()
            total = total + y_in[g].astype(F32)
        y_out[4 * i + g] = total.astype(BF16)
        y_copies[i, g].start()

    for_partner(0, 0, 2)
    onward(0, 0)
    onward(0, 2)
    mixed_t[...] = mixed_ref[...].reshape(1024, 384).T
    for_partner(0, 1, 3)
    onward(0, 1)
    onward(0, 3)
    for low in (0, 1):
        for_partner(1, 2 + low)
        for_partner(2, low)
        onward(1, 2 + low)
        onward(2, low)
    for low in (0, 1):
        for_partner(1, low)
        for_partner(2, 2 + low)
    for_partner(3, 0, 1, 2, 3)
    for low in (0, 1):
        onward(1, low)
        onward(2, 2 + low)
    for g in range(4):
        own[g] = summed(3, g)
    for g in range(4):
        y_copies[1, g].wait_recv()
        y_copies[2, g].wait_recv()
        total = own[g] + y_in[4 + g].astype(F32) + y_in[8 + g].astype(F32)
        if g < 3:
            in_ref[g] = total
        else:
            out_ref[...] = total
    for copy in list(core_copies.values()) + list(y_copies.values()):
        copy.wait_send()


def reduce(grads, mixed, normed, up):
    vmem = pl.BlockSpec(memory_space=pltpu.VMEM)
    hbm = pl.BlockSpec(memory_space=pl.ANY)
    dma = pltpu.SemaphoreType.DMA
    return pl.pallas_call(
        reduce_kernel,
        out_shape=(
            jax.ShapeDtypeStruct((3, 3, 128, 384), F32),
            jax.ShapeDtypeStruct((3, 128, 384), F32),
        ),
        in_specs=[vmem, vmem, hbm, hbm],
        out_specs=(vmem, vmem),
        scratch_shapes=[
            pltpu.VMEM((384, 1024), BF16),
            pltpu.VMEM((8, 8, 128, 384), BF16),
            pltpu.VMEM((8, 8, 128, 384), BF16),
            pltpu.VMEM((16, 3, 128, 384), BF16),
            pltpu.VMEM((16, 3, 128, 384), BF16),
            pltpu.VMEM((12, 3, 128, 384), BF16),
            pltpu.VMEM((12, 3, 128, 384), BF16),
            pltpu.VMEM((4, 3, 128, 384), F32),
            dma((8,)),
            dma((8,)),
            dma((16,)),
            dma((16,)),
            dma((12,)),
            dma((12,)),
        ],
        name="reduce",
        cost_estimate=pl.CostEstimate(
            flops=2 * 1024 * 3072 * 1536, bytes_accessed=20_000_000, transcendentals=0
        ),
        compiler_params=pltpu.CompilerParams(
            collective_id=3, has_side_effects=True, vmem_limit_bytes=VMEM_LIMIT
        ),
    )(grads, mixed, normed, up)


def body(paths, prev_drift, boundary, step_scale, time_ids, mod_table, w_qkv, output_weight):
    modulation = lax.dynamic_index_in_dim(mod_table, time_ids[0], 0, keepdims=False).astype(F32)
    w = jnp.transpose(w_qkv, (1, 0, 2))
    grads, mixed, normed, upstream = attend(
        step_scale, paths[0], prev_drift[0], modulation, w, output_weight, boundary
    )
    grad_in_sum, grad_out_sum = reduce(grads, mixed, normed, upstream)
    grad_in_sum = jnp.transpose(grad_in_sum.reshape(3, 384, 384), (2, 0, 1))
    grad_out_sum = grad_out_sum.reshape(384, 384)
    return (grad_in_sum, grad_out_sum)


def solution(mesh):
    placed = (
        P("tm", "row", "col"),
        P("tm", "row", "col"),
        P(None, "row", "col"),
        P("tm"),
        P("tm"),
        P(None, None, "col"),
        P("col", None, "row"),
        P("row", "col"),
    )
    return jax.shard_map(
        body,
        mesh=mesh,
        in_specs=placed,
        out_specs=(P(("col", "tm"), None, "row"), P("row", ("col", "tm"))),
        check_vma=False,
    )
```

```python
import jax
import jax.numpy as jnp
from jax import lax
from jax.experimental import pallas as pl
from jax.experimental.pallas import tpu as pltpu
from jax.sharding import PartitionSpec as P

D = 6144
HEAD_DIM = 128
SCALE = HEAD_DIM**-0.5
MESH = pl.DeviceIdType.MESH
VMEM_LIMIT = 63 * 1024 * 1024

norm_eps = 1e-06

BF16 = jnp.bfloat16
F32 = jnp.float32
HALVES = (pl.ds(0, 1536), pl.ds(1536, 1536))


class Place:
    def __init__(self):
        self.t = lax.axis_index("tm")
        self.r = lax.axis_index("row")
        self.c = lax.axis_index("col")
        x = lax.rem(self.r, 4)
        base = self.r - x
        other = lax.rem(base + 4, 8)
        self.left = base + lax.rem(x + 3, 4)
        self.right = base + lax.rem(x + 1, 4)
        self.far = base + lax.rem(x + 2, 4)
        self.z = other + x
        self.zleft = other + lax.rem(x + 3, 4)
        self.zright = other + lax.rem(x + 1, 4)
        self.zfar = other + lax.rem(x + 2, 4)

    def row(self, r):
        return (self.t, r, self.c)

    def col(self):
        return (self.t, self.r, 1 - self.c)


def greet(signalled, awaited):
    barrier = pltpu.get_barrier_semaphore()
    for device in signalled:
        pl.semaphore_signal(barrier, inc=1, device_id=device, device_id_type=MESH)
    pl.semaphore_wait(barrier, awaited)


def remote(src, dst, send_sem, recv_sem, device):
    return pltpu.make_async_remote_copy(
        src_ref=src,
        dst_ref=dst,
        send_sem=send_sem,
        recv_sem=recv_sem,
        device_id=device,
        device_id_type=MESH,
    )


class Gather:
    def __init__(self, place, buf, send_sems, recv_sems, over_z):
        p = place
        self.over_z = over_z
        low, high, full = pl.ds(0, 64), pl.ds(64, 64), pl.ds(0, 128)
        plan = [
            (p.r, p.left, full, p.right),
            (p.r, p.right, full, p.left),
            (p.r, p.z, full, p.z),
            (p.left, p.far, low, p.right),
            (p.right, p.far, high, p.left),
            (p.z, p.zleft, full, p.right),
            (p.z, p.zright, full, p.left),
            (p.zleft, p.zfar, low, p.right),
            (p.zright, p.zfar, high, p.left),
            (p.far, p.zfar, full, p.z),
        ]
        self.out, self.into, self.started = {}, {}, []
        for c in (0, 1):
            for m, (sent, received, rows, target) in enumerate(plan):
                i = 10 * c + m
                device = p.row(target)
                a, b = buf.at[sent, rows, HALVES[c]], buf.at[received, rows, HALVES[c]]
                self.out[m, c] = remote(a, a, send_sems.at[i], recv_sems.at[i], device)
                self.into[m, c] = remote(b, b, send_sems.at[i], recv_sems.at[i], device)

    def send(self, c, *which):
        for m in which:
            self.out[m, c].start()
            self.started.append(self.out[m, c])

    def arrived(self, c, *which):
        for m in which:
            self.into[m, c].wait_recv()

    def finish(self):
        for copy in self.started:
            copy.wait_send()

    def run(self, place, visit, spare=None):
        p = place
        visit(0, p.r)
        for c in (0, 1):
            self.arrived(c, 0)
            self.send(c, 3)
            self.arrived(c, 1)
            self.send(c, 4)
            self.arrived(c, 2)
            self.send(c, 5, 6)
        visit(1, p.left)
        visit(2, p.right)
        for c in (0, 1):
            self.arrived(c, 3, 4)
            if c in self.over_z:
                self.send(c, 9)
        visit(3, p.z)
        visit(4, p.far)
        for c in (0, 1):
            self.arrived(c, 5)
            if c not in self.over_z:
                self.send(c, 7)
            self.arrived(c, 6)
            if c not in self.over_z:
                self.send(c, 8)
        visit(5, p.zleft)
        visit(6, p.zright)
        if spare is not None:
            spare()
        for c in (0, 1):
            if c in self.over_z:
                self.arrived(c, 9)
            else:
                self.arrived(c, 7, 8)
        visit(7, p.zfar)


def attend_kernel(
    scale_ref, x_ref, mod_ref, w_hbm, wo_hbm, paths_hbm, drift_hbm, bound_hbm,
    grad_in_hbm, grad_out_hbm,
    grads_ref, mixed_ref, mixed_t, w_ref, wo_ref, drift_ref, full_ref, up_ref, moved, part, out_part, in_part,
    probs, outbox, in_half, in_full, gm_in, key_acc, value_acc,
    w_sems, late_sems, sq_sems, n_send, n_recv, u_send, u_recv, kv_send, kv_recv, q_send, q_recv,
    tm_send, tm_recv, b_sems, rs_send, rs_recv, gm_send, gm_recv, core_send, core_recv, y_send, y_recv, end_sems,
    core_free, y_free,
):
    p = Place()
    weight_copies = [
        pltpu.make_async_copy(w_hbm.at[j], w_ref.at[j], w_sems.at[j]) for j in range(3)
    ]
    late_copies = [
        pltpu.make_async_copy(wo_hbm, wo_ref, late_sems.at[0]),
        pltpu.make_async_copy(drift_hbm, drift_ref, late_sems.at[1]),
    ]
    for copy in weight_copies + late_copies:
        copy.start()
    after = (lax.rem(p.t + 1, 8), p.r, p.c)
    before = (lax.rem(p.t + 7, 8), p.r, p.c)
    core = lax.rem(p.t, 2)
    y = p.t // 2
    peers = [lax.rem(y + by, 4) for by in (2, 3, 1, 0)]
    partner = (2 * y + 1 - core, p.r, p.c)
    to_left = (2 * peers[1] + core, p.r, p.c)
    to_right = (2 * peers[2] + core, p.r, p.c)
    row_peers = [p.row(p.right), p.row(p.left), p.row(p.z)]
    greet(row_peers + [p.col(), before, partner, to_left, to_right], 8)

    sq_out, sq_in = part.at[0, 0, :, pl.ds(0, 128)], part.at[7, 0, :, pl.ds(0, 128)]
    squares = jnp.zeros((128, 1), F32)
    for i in range(4):
        piece = x_ref[:, i * 768 : (i + 1) * 768].astype(F32)
        squares = squares + jnp.sum(piece * piece, axis=-1, keepdims=True)
    sq_out[...] = jnp.broadcast_to(squares, (128, 128))
    swap = remote(sq_out, sq_in, sq_sems.at[0], sq_sems.at[1], p.col())
    swap.start()
    swap.wait()
    total = sq_out[:, :1] + sq_in[:, :1]
    scale = lax.rsqrt(total / D + norm_eps)
    gather = Gather(p, full_ref, n_send, n_recv, ())
    for i in range(4):
        cols = slice(i * 768, (i + 1) * 768)
        piece = x_ref[:, cols].astype(F32)
        full_ref[p.r, :, cols] = (
            piece * scale * (1.0 + mod_ref[0:1, cols]) + mod_ref[1:2, cols]
        ).astype(BF16)
        if i % 2 == 1:
            gather.send(i // 2, 0, 1, 2)

    moves = [
        remote(paths_hbm, moved.at[0], tm_send.at[0], tm_recv.at[0], after),
        remote(drift_hbm, moved.at[1], tm_send.at[1], tm_recv.at[1], after),
    ]
    bounds = [pltpu.make_async_copy(bound_hbm.at[i], moved.at[i], b_sems.at[i]) for i in (0, 1)]

    @pl.when(p.t < 7)
    def _():
        for move in moves:
            move.start()

    @pl.when(p.t == 0)
    def _():
        for copy in bounds:
            copy.start()

    kv_copies, q_copies = [], []

    def project(k, owner):
        if k == 0:
            for copy in weight_copies:
                copy.wait()

        def product(j):
            term = jnp.dot(full_ref[owner], w_ref[j], preferred_element_type=F32)
            part[k, j] = term
            out_part[k, j] = term.astype(BF16)

        @pl.loop(1, 3)
        def _(j):
            product(j)

        pair = pl.ds(1, 2)
        copy = remote(
            out_part.at[k, pair], in_part.at[k, pair], kv_send.at[k], kv_recv.at[k], p.col()
        )
        copy.start()
        kv_copies.append(copy)
        product(0)
        q_copies.append(
            remote(out_part.at[k, 0], in_part.at[k, 0], q_send.at[k], q_recv.at[k], p.col())
        )

    owners = [p.r, p.left, p.right, p.z, p.far, p.zleft, p.zright, p.zfar]

    def rows_of(owner):
        return pl.ds(pl.multiple_of(owner * 128, 128), 128)

    def join_early():
        for copy in late_copies:
            copy.wait()
        for k in range(5):
            kv_copies[k].wait_recv()
            for j in (1, 2):
                part[k, j] += in_part[k, j].astype(F32)

    gather.run(p, project, join_early)
    query_order = [7, 5, 6, 4, 1, 2, 3, 0]
    for k in query_order:
        q_copies[k].start()


    def join(k, j):
        w_ref[j, rows_of(owners[k])] = (part[k, j] + in_part[k, j].astype(F32)).astype(BF16)

    for k in range(5):
        for j in (1, 2):
            w_ref[j, rows_of(owners[k])] = part[k, j].astype(BF16)
    for k in (5, 6, 7):
        kv_copies[k].wait_recv()
        join(k, 1)
        join(k, 2)

    def keys(h):
        return w_ref[1, :1024, h * 128 : (h + 1) * 128]

    def values(h):
        return w_ref[2, :1024, h * 128 : (h + 1) * 128]

    def attend(owner):
        for h in range(3):
            cols = slice(h * 128, (h + 1) * 128)
            scores = (
                lax.dot_general(
                    w_ref[0, rows_of(owner), cols],
                    keys(h),
                    (((1,), (1,)), ((), ())),
                    preferred_element_type=F32,
                )
                * SCALE
            )
            top = jnp.max(scores, axis=-1, keepdims=True)
            weights = jnp.exp(scores - top)
            weights = weights * (1.0 / jnp.sum(weights, axis=-1, keepdims=True))
            weights_low = weights.astype(BF16)
            probs[h, owner] = weights_low
            mixed_ref[owner, :, cols] = jnp.dot(
                weights_low, values(h), preferred_element_type=F32
            ).astype(BF16)

    def ready(k):
        q_copies[k].wait_recv()
        join(k, 0)

    def out_rows(owner, c, lo, n, extra, put):
        @pl.loop(0, 2)
        def _(i):
            near = pl.ds(pl.multiple_of(i * 768, 768), 768)
            cols = pl.ds(pl.multiple_of(c * 1536 + i * 768, 768), 768)
            term = jnp.dot(
                mixed_ref[owner, lo : lo + n, :], wo_ref[:, cols], preferred_element_type=F32
            )
            for ref in extra:
                term = term + ref[:, near].astype(F32)
            put(cols, term)

    low, high, full = pl.ds(0, 64), pl.ds(64, 64), pl.ds(0, 128)
    plan = {
        "zfar low": (0, low, p.left, 0),
        "zfar high": (0, high, p.right, 1),
        "far low": (3, low, p.left, 2),
        "far high": (3, high, p.right, 3),
        "zfar": (0, full, p.z, 0),
        "zleft": (1, full, p.left, 1),
        "zright": (2, full, p.right, 2),
        "left": (4, full, p.left, 3),
        "right": (5, full, p.right, 4),
        "z": (6, full, p.z, 5),
    }
    copies, landed, started = {}, {}, []
    for c in (0, 1):
        for m, (name, (slot, rows, target, place)) in enumerate(plan.items()):
            i = 10 * c + m
            landed[name, c] = in_half.at[c, place] if m < 4 else in_full.at[c, place]
            copies[name, c] = remote(
                outbox.at[slot, rows, HALVES[c]],
                landed[name, c],
                rs_send.at[i],
                rs_recv.at[i],
                p.row(target),
            )

    def send(name, c):
        copies[name, c].start()
        started.append(copies[name, c])

    def arrived(*names_and_halves):
        for name, c in names_and_halves:
            copies[name, c].wait_recv()

    def to_slot(slot, lo, n):
        def put(cols, term):
            outbox[slot, lo : lo + n, cols] = term.astype(BF16)

        return put

    def share(slot, owner, c, lo=0, n=128, extra=()):
        out_rows(owner, c, lo, n, [landed[name, c] for name in extra], to_slot(slot, lo, n))

    ready(7)
    attend(p.zfar)
    share(0, p.zfar, 0)
    send("zfar low", 0)
    send("zfar high", 0)
    share(0, p.zfar, 1)
    send("zfar", 1)
    ready(5)
    attend(p.zleft)
    share(1, p.zleft, 1)
    send("zleft", 1)
    ready(6)
    attend(p.zright)
    share(2, p.zright, 1)
    send("zright", 1)
    share(1, p.zleft, 0, 64, 64)
    share(2, p.zright, 0, 0, 64)
    arrived(("zfar low", 0))
    share(1, p.zleft, 0, 0, 64, ["zfar low"])
    send("zleft", 0)
    arrived(("zfar high", 0))
    share(2, p.zright, 0, 64, 64, ["zfar high"])
    send("zright", 0)
    ready(4)
    attend(p.far)
    share(3, p.far, 0)
    send("far low", 0)
    send("far high", 0)
    for k in (1, 2, 3, 0):
        ready(k)

    @pl.loop(0, 4)
    def _(i):
        attend(
            jnp.where(
                i == 0, p.left, jnp.where(i == 1, p.right, jnp.where(i == 2, p.z, p.r))
            )
        )

    arrived(("zfar", 1))
    share(3, p.far, 1, extra=["zfar"])
    send("far low", 1)
    send("far high", 1)
    for c in (1, 0):
        arrived(("zleft", c), ("zright", c))
        share(6, p.z, c, extra=["zleft", "zright"])
        send("z", c)
    for c in (0, 1):
        share(4, p.left, c, 64, 64)
        share(5, p.right, c, 0, 64)
        arrived(("far low", c))
        share(4, p.left, c, 0, 64, ["far low"])
        send("left", c)
        arrived(("far high", c))
        share(5, p.right, c, 64, 64, ["far high"])
        send("right", c)

    @pl.when(p.t > 0)
    def _():
        for move in moves:
            move.wait_recv()

    @pl.when(p.t == 0)
    def _():
        for copy in bounds:
            copy.wait()

    key_acc[...] = jnp.zeros_like(key_acc)
    value_acc[...] = jnp.zeros_like(value_acc)

    def to_up(cols, term):
        target = moved[0, :, cols].astype(F32) + scale_ref[0] * (
            moved[1, :, cols].astype(F32) - drift_ref[:, cols].astype(F32)
        )
        rest = x_ref[:, cols].astype(F32) - target
        up_ref[p.r, :, cols] = ((rest + term) * (1024**-0.5)).astype(BF16)

    gather_up = Gather(p, up_ref, u_send, u_recv, (1,))
    for c in (0, 1):
        names = ["left", "right", "z"]
        arrived(*[(name, c) for name in names])
        out_rows(p.r, c, 0, 128, [landed[name, c] for name in names], to_up)
        gather_up.send(c, 0, 1, 2)

    pl.semaphore_signal(core_free, inc=1, device_id=partner, device_id_type=MESH)
    pl.semaphore_signal(y_free, inc=1, device_id=to_left, device_id_type=MESH)
    pl.semaphore_signal(y_free, inc=1, device_id=to_right, device_id_type=MESH)
    for copy in started + q_copies + kv_copies:
        copy.wait_send()
    mixed_t[...] = mixed_ref[...].reshape(1024, 384).T

    gm_copies, waiting = [], []

    def backward(k, owner):
        gm_copies[k].wait_recv()
        grad = (part[k, 0] + gm_in[k].astype(F32)).astype(BF16)
        tokens = rows_of(owner)
        for h in range(3):
            cols = slice(h * 128, (h + 1) * 128)
            head_grad = grad[:, cols]
            weights_low = probs[h, owner]
            weights = weights_low.astype(F32)
            value_acc[h] += jnp.dot(head_grad.T, weights_low, preferred_element_type=F32)
            grad_weights = lax.dot_general(
                head_grad, values(h), (((1,), (1,)), ((), ())), preferred_element_type=F32
            )
            inner = jnp.sum(grad_weights * weights, axis=-1, keepdims=True)
            grad_scores = (weights * (grad_weights - inner) * SCALE).astype(BF16)
            query_grad = jnp.dot(grad_scores, keys(h), preferred_element_type=F32)
            grads_ref[0, cols, tokens] = query_grad.T.astype(BF16)
            key_acc[h] += jnp.dot(
                w_ref[0, rows_of(owner), cols].T, grad_scores, preferred_element_type=F32
            )

    def visit(k, owner):
        term = lax.dot_general(
            up_ref[owner], wo_ref[...], (((1,), (1,)), ((), ())), preferred_element_type=F32
        )
        part[k, 0] = term
        rows = pl.ds(1024 + 128 * k, 128)
        w_ref[0, rows] = term.astype(BF16)
        copy = remote(w_ref.at[0, rows], gm_in.at[k], gm_send.at[k], gm_recv.at[k], p.col())
        copy.start()
        gm_copies.append(copy)
        if waiting:
            backward(*waiting.pop())
        waiting.append((k, owner))

    chunks = [2 * peer + 1 - core for peer in peers] + [2 * peer + core for peer in peers]

    def unit(k, g):
        cols = pl.ds(pl.multiple_of(chunks[k] * 384, 384), 384)
        left = grads_ref[g] if g < 3 else mixed_t[...]
        right = full_ref[:, :, cols] if g < 3 else up_ref[:, :, cols]
        term = jnp.dot(left, right.reshape(1024, 384), preferred_element_type=F32)
        return term.reshape(3, 128, 384)

    core_out, core_in, core_copies = {}, {}, {}
    for i in range(4):
        for g in range(4):
            n = 4 * i + g
            slots = pl.ds(3 * (n // 8), 3)
            core_out[i, g] = outbox.at[slots, :, pl.ds(384 * (n % 8), 384)]
            core_in[i, g] = in_full.at[
                i // 2, pl.ds(3 * (i % 2), 3), :, pl.ds(384 * g, 384)
            ]
            core_copies[i, g] = remote(
                core_out[i, g], core_in[i, g], core_send.at[n], core_recv.at[n], partner
            )
    y_order = [
        (0, 3), (1, 3), (2, 3), (0, 0), (0, 1), (0, 2), (1, 0), (1, 1),
        (1, 2), (2, 0), (2, 1), (2, 2),
    ]
    y_out, y_in, y_copies = {}, {}, {}
    for n, (i, g) in enumerate(y_order):
        if n < 8:
            y_out[i, g], y_in[i, g] = out_part.at[n], in_part.at[n]
        else:
            rows = pl.ds(1024 + 384 * (n - 8), 384)
            y_out[i, g], y_in[i, g] = w_ref.at[1, rows], w_ref.at[2, rows]
        leftward = g < 2 if i == 0 else i == 1
        y_copies[i, g] = remote(
            y_out[i, g], y_in[i, g], y_send.at[n], y_recv.at[n],
            to_left if leftward else to_right,
        )

    def for_partner(i, *groups):
        for g in groups:
            core_out[i, g][...] = unit(i, g).astype(BF16)
            core_copies[i, g].start()

    def summed(i, g):
        term = unit(4 + i, g)
        core_copies[i, g].wait_recv()
        return term + core_in[i, g][...].astype(F32)

    def landed_unit(i, g):
        return y_in[i, g][...].reshape(3, 128, 384).astype(F32)

    def onward(i, g):
        total = summed(i, g)
        if (i, g) in ((1, 0), (1, 1), (2, 2), (2, 3)):
            y_copies[0, g].wait_recv()
            total = total + landed_unit(0, g)
        y_out[i, g][...] = total.reshape(y_out[i, g].shape).astype(BF16)
        y_copies[i, g].start()

    gather_up.run(p, visit)
    pl.semaphore_wait(core_free, 1)
    for_partner(0, 3)
    for_partner(1, 3)
    for_partner(2, 3)
    pl.semaphore_wait(y_free, 2)
    onward(0, 3)
    onward(1, 3)
    backward(*waiting.pop())
    for h in range(3):
        cols = slice(h * 128, (h + 1) * 128)
        grads_ref[1, cols, :] = key_acc[h].astype(BF16)
        grads_ref[2, cols, :] = value_acc[h].astype(BF16)
    for_partner(0, 0, 2)
    onward(0, 0)
    onward(0, 2)
    for_partner(0, 1)
    for_partner(2, 0)
    onward(0, 1)
    onward(2, 3)
    for_partner(1, 2)
    onward(2, 0)
    onward(1, 2)
    for_partner(2, 1)
    for_partner(1, 0, 1)
    onward(2, 1)
    for_partner(2, 2)
    for_partner(3, 3, 0, 1, 2)
    onward(1, 0)
    onward(2, 2)
    onward(1, 1)
    for g in (3, 2, 0, 1):
        part[g] = summed(3, g)
    ends = []
    for n, g in enumerate((3, 2, 0, 1)):
        y_copies[1, g].wait_recv()
        y_copies[2, g].wait_recv()
        part[g] += landed_unit(1, g) + landed_unit(2, g)
        target = grad_in_hbm.at[g] if g < 3 else grad_out_hbm
        ends.append(pltpu.make_async_copy(part.at[g], target, end_sems.at[n]))
        ends[-1].start()
    for copy in gm_copies + list(core_copies.values()) + list(y_copies.values()):
        copy.wait_send()
    gather.finish()
    gather_up.finish()

    @pl.when(p.t < 7)
    def _():
        for move in moves:
            move.wait_send()

    for copy in ends:
        copy.wait()


def attend(scale, x, drift, mod, w, wo, bound):
    vmem = pl.BlockSpec(memory_space=pltpu.VMEM)
    smem = pl.BlockSpec(memory_space=pltpu.SMEM)
    hbm = pl.BlockSpec(memory_space=pl.ANY)
    dma = pltpu.SemaphoreType.DMA
    return pl.pallas_call(
        attend_kernel,
        out_shape=(
            jax.ShapeDtypeStruct((3, 3, 128, 384), F32),
            jax.ShapeDtypeStruct((3, 128, 384), F32),
        ),
        in_specs=[smem, vmem, vmem, hbm, hbm, hbm, hbm, hbm],
        out_specs=(hbm, hbm),
        scratch_shapes=[
            pltpu.VMEM((3, 384, 1024), BF16),
            pltpu.VMEM((8, 128, 384), BF16),
            pltpu.VMEM((384, 1024), BF16),
            pltpu.VMEM((3, 3072, 384), BF16),
            pltpu.VMEM((384, 3072), BF16),
            pltpu.VMEM((128, 3072), BF16),
            pltpu.VMEM((8, 128, 3072), BF16),
            pltpu.VMEM((8, 128, 3072), BF16),
            pltpu.VMEM((2, 128, 3072), BF16),
            pltpu.VMEM((8, 3, 128, 384), F32),
            pltpu.VMEM((8, 3, 128, 384), BF16),
            pltpu.VMEM((8, 3, 128, 384), BF16),
            pltpu.VMEM((3, 8, 128, 1024), BF16),
            pltpu.VMEM((7, 128, 3072), BF16),
            pltpu.VMEM((2, 4, 64, 1536), BF16),
            pltpu.VMEM((2, 6, 128, 1536), BF16),
            pltpu.VMEM((8, 128, 384), BF16),
            pltpu.VMEM((3, 128, 1024), F32),
            pltpu.VMEM((3, 128, 1024), F32),
            dma((3,)),
            dma((2,)),
            dma((2,)),
            dma((20,)),
            dma((20,)),
            dma((20,)),
            dma((20,)),
            dma((8,)),
            dma((8,)),
            dma((8,)),
            dma((8,)),
            dma((2,)),
            dma((2,)),
            dma((2,)),
            dma((20,)),
            dma((20,)),
            dma((8,)),
            dma((8,)),
            dma((16,)),
            dma((16,)),
            dma((12,)),
            dma((12,)),
            dma((4,)),
            pltpu.SemaphoreType.REGULAR,
            pltpu.SemaphoreType.REGULAR,
        ],
        name="attend",
        cost_estimate=pl.CostEstimate(
            flops=30_000_000_000, bytes_accessed=30_000_000, transcendentals=3 * 1024 * 1024
        ),
        compiler_params=pltpu.CompilerParams(
            collective_id=2, has_side_effects=True, vmem_limit_bytes=VMEM_LIMIT
        ),
    )(scale, x, mod, w, wo, x, drift, bound)


def body(paths, prev_drift, boundary, step_scale, time_ids, mod_table, w_qkv, output_weight):
    modulation = lax.dynamic_index_in_dim(mod_table, time_ids[0], 0, keepdims=False).astype(F32)
    w = jnp.transpose(w_qkv, (1, 0, 2))
    grad_in_sum, grad_out_sum = attend(
        step_scale, paths[0], prev_drift[0], modulation, w, output_weight, boundary
    )
    grad_in_sum = jnp.transpose(grad_in_sum.reshape(3, 384, 384), (2, 0, 1))
    grad_out_sum = grad_out_sum.reshape(384, 384)
    return (grad_in_sum, grad_out_sum)


def solution(mesh):
    placed = (
        P("tm", "row", "col"),
        P("tm", "row", "col"),
        P(None, "row", "col"),
        P("tm"),
        P("tm"),
        P(None, None, "col"),
        P("col", None, "row"),
        P("row", "col"),
    )
    return jax.shard_map(
        body,
        mesh=mesh,
        in_specs=placed,
        out_specs=(P(("col", "tm"), None, "row"), P("row", ("col", "tm"))),
        check_vma=False,
    )
```

```python
import jax
import jax.numpy as jnp
from jax import lax
from jax.experimental import pallas as pl
from jax.experimental.pallas import tpu as pltpu
from jax.sharding import PartitionSpec as P

D = 6144
HEAD_DIM = 128
SCALE = HEAD_DIM**-0.5
MESH = pl.DeviceIdType.MESH
VMEM_LIMIT = 63 * 1024 * 1024

norm_eps = 1e-06

BF16 = jnp.bfloat16
F32 = jnp.float32
HALVES = (pl.ds(0, 1536), pl.ds(1536, 1536))


class Place:
    def __init__(self):
        self.t = lax.axis_index("tm")
        self.r = lax.axis_index("row")
        self.c = lax.axis_index("col")
        x = lax.rem(self.r, 4)
        base = self.r - x
        other = lax.rem(base + 4, 8)
        self.left = base + lax.rem(x + 3, 4)
        self.right = base + lax.rem(x + 1, 4)
        self.far = base + lax.rem(x + 2, 4)
        self.z = other + x
        self.zleft = other + lax.rem(x + 3, 4)
        self.zright = other + lax.rem(x + 1, 4)
        self.zfar = other + lax.rem(x + 2, 4)

    def row(self, r):
        return (self.t, r, self.c)

    def col(self):
        return (self.t, self.r, 1 - self.c)


def greet(signalled, awaited):
    barrier = pltpu.get_barrier_semaphore()
    for device in signalled:
        pl.semaphore_signal(barrier, inc=1, device_id=device, device_id_type=MESH)
    pl.semaphore_wait(barrier, awaited)


def remote(src, dst, send_sem, recv_sem, device):
    return pltpu.make_async_remote_copy(
        src_ref=src,
        dst_ref=dst,
        send_sem=send_sem,
        recv_sem=recv_sem,
        device_id=device,
        device_id_type=MESH,
    )


class Gather:
    def __init__(self, place, buf, send_sems, recv_sems, over_z):
        p = place
        self.over_z = over_z
        low, high, full = pl.ds(0, 64), pl.ds(64, 64), pl.ds(0, 128)
        plan = [
            (p.r, p.left, full, p.right),
            (p.r, p.right, full, p.left),
            (p.r, p.z, full, p.z),
            (p.left, p.far, low, p.right),
            (p.right, p.far, high, p.left),
            (p.z, p.zleft, full, p.right),
            (p.z, p.zright, full, p.left),
            (p.zleft, p.zfar, low, p.right),
            (p.zright, p.zfar, high, p.left),
            (p.far, p.zfar, full, p.z),
        ]
        self.out, self.into, self.started = {}, {}, []
        for c in (0, 1):
            for m, (sent, received, rows, target) in enumerate(plan):
                i = 10 * c + m
                device = p.row(target)
                a, b = buf.at[sent, rows, HALVES[c]], buf.at[received, rows, HALVES[c]]
                self.out[m, c] = remote(a, a, send_sems.at[i], recv_sems.at[i], device)
                self.into[m, c] = remote(b, b, send_sems.at[i], recv_sems.at[i], device)

    def send(self, c, *which):
        for m in which:
            self.out[m, c].start()
            self.started.append(self.out[m, c])

    def arrived(self, c, *which):
        for m in which:
            self.into[m, c].wait_recv()

    def finish(self):
        for copy in self.started:
            copy.wait_send()

    def run(self, place, visit, spare=None):
        p = place
        visit(0, p.r)
        for c in (0, 1):
            self.arrived(c, 0)
            self.send(c, 3)
            self.arrived(c, 1)
            self.send(c, 4)
            self.arrived(c, 2)
            self.send(c, 5, 6)
        visit(1, p.left)
        visit(2, p.right)
        for c in (0, 1):
            self.arrived(c, 3, 4)
            if c in self.over_z:
                self.send(c, 9)
        visit(3, p.z)
        visit(4, p.far)
        for c in (0, 1):
            self.arrived(c, 5)
            if c not in self.over_z:
                self.send(c, 7)
            self.arrived(c, 6)
            if c not in self.over_z:
                self.send(c, 8)
        visit(5, p.zleft)
        visit(6, p.zright)
        if spare is not None:
            spare()
        for c in (0, 1):
            if c in self.over_z:
                self.arrived(c, 9)
            else:
                self.arrived(c, 7, 8)
        visit(7, p.zfar)


def attend_kernel(
    scale_ref, time_ref, x_ref, table_ref, w_hbm, wo_hbm, paths_hbm, drift_hbm, bound_hbm,
    grad_in_hbm, grad_out_hbm,
    grads_ref, mixed_ref, mixed_t, w_ref, wo_ref, drift_ref, full_ref, up_ref, moved, part, out_part, in_part,
    probs, outbox, in_half, in_full, gm_in, key_acc, value_acc,
    w_sems, late_sems, sq_sems, n_send, n_recv, u_send, u_recv, kv_send, kv_recv, q_send, q_recv,
    tm_send, tm_recv, b_sems, rs_send, rs_recv, gm_send, gm_recv, core_send, core_recv, y_send, y_recv, end_sems,
    core_free, y_free,
):
    p = Place()
    weight_copies = [
        pltpu.make_async_copy(w_hbm.at[j], w_ref.at[j], w_sems.at[j]) for j in range(3)
    ]
    late_copies = [
        pltpu.make_async_copy(wo_hbm, wo_ref, late_sems.at[0]),
        pltpu.make_async_copy(drift_hbm, drift_ref, late_sems.at[1]),
    ]
    for copy in weight_copies + late_copies:
        copy.start()
    after = (lax.rem(p.t + 1, 8), p.r, p.c)
    before = (lax.rem(p.t + 7, 8), p.r, p.c)
    core = lax.rem(p.t, 2)
    y = p.t // 2
    peers = [lax.rem(y + by, 4) for by in (2, 3, 1, 0)]
    partner = (2 * y + 1 - core, p.r, p.c)
    to_left = (2 * peers[1] + core, p.r, p.c)
    to_right = (2 * peers[2] + core, p.r, p.c)
    row_peers = [p.row(p.right), p.row(p.left), p.row(p.z)]
    greet(row_peers + [p.col(), before, partner, to_left, to_right], 8)

    sq_out, sq_in = part.at[0, 0, :, pl.ds(0, 128)], part.at[7, 0, :, pl.ds(0, 128)]
    squares = jnp.zeros((128, 1), F32)
    for i in range(4):
        piece = x_ref[:, i * 768 : (i + 1) * 768].astype(F32)
        squares = squares + jnp.sum(piece * piece, axis=-1, keepdims=True)
    sq_out[...] = jnp.broadcast_to(squares, (128, 128))
    swap = remote(sq_out, sq_in, sq_sems.at[0], sq_sems.at[1], p.col())
    swap.start()
    swap.wait()
    total = sq_out[:, :1] + sq_in[:, :1]
    scale = lax.rsqrt(total / D + norm_eps)
    gather = Gather(p, full_ref, n_send, n_recv, ())
    modulation = table_ref[time_ref[0]].astype(F32)
    for i in range(4):
        cols = slice(i * 768, (i + 1) * 768)
        piece = x_ref[:, cols].astype(F32)
        full_ref[p.r, :, cols] = (
            piece * scale * (1.0 + modulation[0:1, cols]) + modulation[1:2, cols]
        ).astype(BF16)
        if i % 2 == 1:
            gather.send(i // 2, 0, 1, 2)

    moves = [
        remote(paths_hbm, moved.at[0], tm_send.at[0], tm_recv.at[0], after),
        remote(drift_hbm, moved.at[1], tm_send.at[1], tm_recv.at[1], after),
    ]
    bounds = [pltpu.make_async_copy(bound_hbm.at[i], moved.at[i], b_sems.at[i]) for i in (0, 1)]

    @pl.when(p.t < 7)
    def _():
        for move in moves:
            move.start()

    @pl.when(p.t == 0)
    def _():
        for copy in bounds:
            copy.start()

    kv_copies, q_copies = [], []

    def project(k, owner):
        if k == 0:
            for copy in weight_copies:
                copy.wait()

        def product(j):
            term = jnp.dot(full_ref[owner], w_ref[j], preferred_element_type=F32)
            part[k, j] = term
            out_part[k, j] = term.astype(BF16)

        @pl.loop(1, 3)
        def _(j):
            product(j)

        pair = pl.ds(1, 2)
        copy = remote(
            out_part.at[k, pair], in_part.at[k, pair], kv_send.at[k], kv_recv.at[k], p.col()
        )
        copy.start()
        kv_copies.append(copy)
        product(0)
        q_copies.append(
            remote(out_part.at[k, 0], in_part.at[k, 0], q_send.at[k], q_recv.at[k], p.col())
        )

    owners = [p.r, p.left, p.right, p.z, p.far, p.zleft, p.zright, p.zfar]

    def rows_of(owner):
        return pl.ds(pl.multiple_of(owner * 128, 128), 128)

    def join_early():
        for copy in late_copies:
            copy.wait()
        for k in range(5):
            kv_copies[k].wait_recv()
            for j in (1, 2):
                part[k, j] += in_part[k, j].astype(F32)

    gather.run(p, project, join_early)
    query_order = [7, 5, 6, 4, 1, 2, 3, 0]
    for k in query_order:
        q_copies[k].start()


    def join(k, j):
        w_ref[j, rows_of(owners[k])] = (part[k, j] + in_part[k, j].astype(F32)).astype(BF16)

    for k in range(5):
        for j in (1, 2):
            w_ref[j, rows_of(owners[k])] = part[k, j].astype(BF16)
    for k in (5, 6, 7):
        kv_copies[k].wait_recv()
        join(k, 1)
        join(k, 2)

    def keys(h):
        return w_ref[1, :1024, h * 128 : (h + 1) * 128]

    def values(h):
        return w_ref[2, :1024, h * 128 : (h + 1) * 128]

    def attend(owner):
        for h in range(3):
            cols = slice(h * 128, (h + 1) * 128)
            scores = (
                lax.dot_general(
                    w_ref[0, rows_of(owner), cols],
                    keys(h),
                    (((1,), (1,)), ((), ())),
                    preferred_element_type=F32,
                )
                * SCALE
            )
            top = jnp.max(scores, axis=-1, keepdims=True)
            weights = jnp.exp(scores - top)
            weights = weights * (1.0 / jnp.sum(weights, axis=-1, keepdims=True))
            weights_low = weights.astype(BF16)
            probs[h, owner] = weights_low
            mixed_ref[owner, :, cols] = jnp.dot(
                weights_low, values(h), preferred_element_type=F32
            ).astype(BF16)

    def ready(k):
        q_copies[k].wait_recv()
        join(k, 0)

    def out_rows(owner, c, lo, n, extra, put):
        @pl.loop(0, 2)
        def _(i):
            near = pl.ds(pl.multiple_of(i * 768, 768), 768)
            cols = pl.ds(pl.multiple_of(c * 1536 + i * 768, 768), 768)
            term = jnp.dot(
                mixed_ref[owner, lo : lo + n, :], wo_ref[:, cols], preferred_element_type=F32
            )
            for ref in extra:
                term = term + ref[:, near].astype(F32)
            put(cols, term)

    low, high, full = pl.ds(0, 64), pl.ds(64, 64), pl.ds(0, 128)
    plan = {
        "zfar low": (0, low, p.left, 0),
        "zfar high": (0, high, p.right, 1),
        "far low": (3, low, p.left, 2),
        "far high": (3, high, p.right, 3),
        "zfar": (0, full, p.z, 0),
        "zleft": (1, full, p.left, 1),
        "zright": (2, full, p.right, 2),
        "left": (4, full, p.left, 3),
        "right": (5, full, p.right, 4),
        "z": (6, full, p.z, 5),
    }
    copies, landed, started = {}, {}, []
    for c in (0, 1):
        for m, (name, (slot, rows, target, place)) in enumerate(plan.items()):
            i = 10 * c + m
            landed[name, c] = in_half.at[c, place] if m < 4 else in_full.at[c, place]
            copies[name, c] = remote(
                outbox.at[slot, rows, HALVES[c]],
                landed[name, c],
                rs_send.at[i],
                rs_recv.at[i],
                p.row(target),
            )

    def send(name, c):
        copies[name, c].start()
        started.append(copies[name, c])

    def arrived(*names_and_halves):
        for name, c in names_and_halves:
            copies[name, c].wait_recv()

    def to_slot(slot, lo, n):
        def put(cols, term):
            outbox[slot, lo : lo + n, cols] = term.astype(BF16)

        return put

    def share(slot, owner, c, lo=0, n=128, extra=()):
        out_rows(owner, c, lo, n, [landed[name, c] for name in extra], to_slot(slot, lo, n))

    ready(7)
    attend(p.zfar)
    share(0, p.zfar, 0)
    send("zfar low", 0)
    send("zfar high", 0)
    share(0, p.zfar, 1)
    send("zfar", 1)
    ready(5)
    attend(p.zleft)
    share(1, p.zleft, 1)
    send("zleft", 1)
    ready(6)
    attend(p.zright)
    share(2, p.zright, 1)
    send("zright", 1)
    share(1, p.zleft, 0, 64, 64)
    share(2, p.zright, 0, 0, 64)
    arrived(("zfar low", 0))
    share(1, p.zleft, 0, 0, 64, ["zfar low"])
    send("zleft", 0)
    arrived(("zfar high", 0))
    share(2, p.zright, 0, 64, 64, ["zfar high"])
    send("zright", 0)
    ready(4)
    attend(p.far)
    share(3, p.far, 0)
    send("far low", 0)
    send("far high", 0)
    for k in (1, 2, 3, 0):
        ready(k)

    @pl.loop(0, 4)
    def _(i):
        attend(
            jnp.where(
                i == 0, p.left, jnp.where(i == 1, p.right, jnp.where(i == 2, p.z, p.r))
            )
        )

    arrived(("zfar", 1))
    share(3, p.far, 1, extra=["zfar"])
    send("far low", 1)
    send("far high", 1)
    for c in (1, 0):
        arrived(("zleft", c), ("zright", c))
        share(6, p.z, c, extra=["zleft", "zright"])
        send("z", c)
    for c in (0, 1):
        share(4, p.left, c, 64, 64)
        share(5, p.right, c, 0, 64)
        arrived(("far low", c))
        share(4, p.left, c, 0, 64, ["far low"])
        send("left", c)
        arrived(("far high", c))
        share(5, p.right, c, 64, 64, ["far high"])
        send("right", c)

    @pl.when(p.t > 0)
    def _():
        for move in moves:
            move.wait_recv()

    @pl.when(p.t == 0)
    def _():
        for copy in bounds:
            copy.wait()

    key_acc[...] = jnp.zeros_like(key_acc)
    value_acc[...] = jnp.zeros_like(value_acc)

    def to_up(cols, term):
        target = moved[0, :, cols].astype(F32) + scale_ref[0] * (
            moved[1, :, cols].astype(F32) - drift_ref[:, cols].astype(F32)
        )
        rest = x_ref[:, cols].astype(F32) - target
        up_ref[p.r, :, cols] = ((rest + term) * (1024**-0.5)).astype(BF16)

    gather_up = Gather(p, up_ref, u_send, u_recv, (1,))
    for c in (0, 1):
        names = ["left", "right", "z"]
        arrived(*[(name, c) for name in names])
        out_rows(p.r, c, 0, 128, [landed[name, c] for name in names], to_up)
        gather_up.send(c, 0, 1, 2)

    pl.semaphore_signal(core_free, inc=1, device_id=partner, device_id_type=MESH)
    pl.semaphore_signal(y_free, inc=1, device_id=to_left, device_id_type=MESH)
    pl.semaphore_signal(y_free, inc=1, device_id=to_right, device_id_type=MESH)
    for copy in started + q_copies + kv_copies:
        copy.wait_send()
    mixed_t[...] = mixed_ref[...].reshape(1024, 384).T

    gm_copies, waiting = [], []

    def backward(k, owner):
        gm_copies[k].wait_recv()
        grad = (part[k, 0] + gm_in[k].astype(F32)).astype(BF16)
        tokens = rows_of(owner)
        for h in range(3):
            cols = slice(h * 128, (h + 1) * 128)
            head_grad = grad[:, cols]
            weights_low = probs[h, owner]
            weights = weights_low.astype(F32)
            value_acc[h] += jnp.dot(head_grad.T, weights_low, preferred_element_type=F32)
            grad_weights = lax.dot_general(
                head_grad, values(h), (((1,), (1,)), ((), ())), preferred_element_type=F32
            )
            inner = jnp.sum(grad_weights * weights, axis=-1, keepdims=True)
            grad_scores = (weights * (grad_weights - inner) * SCALE).astype(BF16)
            query_grad = jnp.dot(grad_scores, keys(h), preferred_element_type=F32)
            grads_ref[0, cols, tokens] = query_grad.T.astype(BF16)
            key_acc[h] += jnp.dot(
                w_ref[0, rows_of(owner), cols].T, grad_scores, preferred_element_type=F32
            )

    def visit(k, owner):
        term = lax.dot_general(
            up_ref[owner], wo_ref[...], (((1,), (1,)), ((), ())), preferred_element_type=F32
        )
        part[k, 0] = term
        rows = pl.ds(1024 + 128 * k, 128)
        w_ref[0, rows] = term.astype(BF16)
        copy = remote(w_ref.at[0, rows], gm_in.at[k], gm_send.at[k], gm_recv.at[k], p.col())
        copy.start()
        gm_copies.append(copy)
        waiting.append((k, owner))
        if 0 < k < 7:
            backward(*waiting.pop(0))

    chunks = [2 * peer + 1 - core for peer in peers] + [2 * peer + core for peer in peers]

    def unit(k, g):
        cols = pl.ds(pl.multiple_of(chunks[k] * 384, 384), 384)
        left = grads_ref[g] if g < 3 else mixed_t[...]
        right = full_ref[:, :, cols] if g < 3 else up_ref[:, :, cols]
        term = jnp.dot(left, right.reshape(1024, 384), preferred_element_type=F32)
        return term.reshape(3, 128, 384)

    core_out, core_in, core_copies = {}, {}, {}
    for i in range(4):
        for g in range(4):
            n = 4 * i + g
            slots = pl.ds(3 * (n // 8), 3)
            core_out[i, g] = outbox.at[slots, :, pl.ds(384 * (n % 8), 384)]
            core_in[i, g] = in_full.at[
                i // 2, pl.ds(3 * (i % 2), 3), :, pl.ds(384 * g, 384)
            ]
            core_copies[i, g] = remote(
                core_out[i, g], core_in[i, g], core_send.at[n], core_recv.at[n], partner
            )
    y_order = [
        (0, 3), (1, 3), (2, 3), (0, 0), (0, 1), (0, 2), (1, 0), (1, 1),
        (1, 2), (2, 0), (2, 1), (2, 2),
    ]
    y_out, y_in, y_copies = {}, {}, {}
    for n, (i, g) in enumerate(y_order):
        if n < 8:
            y_out[i, g], y_in[i, g] = out_part.at[n], in_part.at[n]
        else:
            rows = pl.ds(1024 + 384 * (n - 8), 384)
            y_out[i, g], y_in[i, g] = w_ref.at[1, rows], w_ref.at[2, rows]
        leftward = g < 2 if i == 0 else i == 1
        y_copies[i, g] = remote(
            y_out[i, g], y_in[i, g], y_send.at[n], y_recv.at[n],
            to_left if leftward else to_right,
        )

    def for_partner(i, *groups):
        for g in groups:
            core_out[i, g][...] = unit(i, g).astype(BF16)
            core_copies[i, g].start()

    def summed(i, g):
        term = unit(4 + i, g)
        core_copies[i, g].wait_recv()
        term = term + core_in[i, g][...].astype(F32)
        return term if g == 3 else term.reshape(384, 384).T.reshape(3, 128, 384)

    def landed_unit(i, g):
        return y_in[i, g][...].reshape(3, 128, 384).astype(F32)

    def onward(i, g):
        total = summed(i, g)
        if (i, g) in ((1, 0), (1, 1), (2, 2), (2, 3)):
            y_copies[0, g].wait_recv()
            total = total + landed_unit(0, g)
        y_out[i, g][...] = total.reshape(y_out[i, g].shape).astype(BF16)
        y_copies[i, g].start()

    gather_up.run(p, visit)
    pl.semaphore_wait(core_free, 1)
    for_partner(0, 3)
    for_partner(1, 3)
    for_partner(2, 3)
    pl.semaphore_wait(y_free, 2)
    onward(0, 3)
    onward(1, 3)
    for block in waiting:
        backward(*block)
    for h in range(3):
        cols = slice(h * 128, (h + 1) * 128)
        grads_ref[1, cols, :] = key_acc[h].astype(BF16)
        grads_ref[2, cols, :] = value_acc[h].astype(BF16)
    for_partner(0, 0, 2)
    onward(0, 0)
    onward(0, 2)
    for_partner(0, 1)
    for_partner(2, 0)
    onward(0, 1)
    onward(2, 3)
    for_partner(1, 2)
    onward(2, 0)
    onward(1, 2)
    for_partner(2, 1)
    for_partner(1, 0, 1)
    onward(2, 1)
    for_partner(2, 2)
    for_partner(3, 3, 0, 1, 2)
    onward(1, 0)
    onward(2, 2)
    onward(1, 1)
    for g in (3, 2, 0, 1):
        part[g] = summed(3, g)
    ends = []
    for n, g in enumerate((3, 2, 0, 1)):
        y_copies[1, g].wait_recv()
        y_copies[2, g].wait_recv()
        part[g] += landed_unit(1, g) + landed_unit(2, g)
        target = grad_in_hbm.at[g] if g < 3 else grad_out_hbm
        ends.append(pltpu.make_async_copy(part.at[g], target, end_sems.at[n]))
        ends[-1].start()
    for copy in gm_copies + list(core_copies.values()) + list(y_copies.values()):
        copy.wait_send()
    gather.finish()
    gather_up.finish()

    @pl.when(p.t < 7)
    def _():
        for move in moves:
            move.wait_send()

    for copy in ends:
        copy.wait()


def attend(scale, time, x, drift, table, w, wo, bound):
    vmem = pl.BlockSpec(memory_space=pltpu.VMEM)
    smem = pl.BlockSpec(memory_space=pltpu.SMEM)
    hbm = pl.BlockSpec(memory_space=pl.ANY)
    dma = pltpu.SemaphoreType.DMA
    return pl.pallas_call(
        attend_kernel,
        out_shape=(
            jax.ShapeDtypeStruct((3, 3, 128, 384), F32),
            jax.ShapeDtypeStruct((3, 128, 384), F32),
        ),
        in_specs=[smem, smem, vmem, vmem, hbm, hbm, hbm, hbm, hbm],
        out_specs=(hbm, hbm),
        scratch_shapes=[
            pltpu.VMEM((3, 384, 1024), BF16),
            pltpu.VMEM((8, 128, 384), BF16),
            pltpu.VMEM((384, 1024), BF16),
            pltpu.VMEM((3, 3072, 384), BF16),
            pltpu.VMEM((384, 3072), BF16),
            pltpu.VMEM((128, 3072), BF16),
            pltpu.VMEM((8, 128, 3072), BF16),
            pltpu.VMEM((8, 128, 3072), BF16),
            pltpu.VMEM((2, 128, 3072), BF16),
            pltpu.VMEM((8, 3, 128, 384), F32),
            pltpu.VMEM((8, 3, 128, 384), BF16),
            pltpu.VMEM((8, 3, 128, 384), BF16),
            pltpu.VMEM((3, 8, 128, 1024), BF16),
            pltpu.VMEM((7, 128, 3072), BF16),
            pltpu.VMEM((2, 4, 64, 1536), BF16),
            pltpu.VMEM((2, 6, 128, 1536), BF16),
            pltpu.VMEM((8, 128, 384), BF16),
            pltpu.VMEM((3, 128, 1024), F32),
            pltpu.VMEM((3, 128, 1024), F32),
            dma((3,)),
            dma((2,)),
            dma((2,)),
            dma((20,)),
            dma((20,)),
            dma((20,)),
            dma((20,)),
            dma((8,)),
            dma((8,)),
            dma((8,)),
            dma((8,)),
            dma((2,)),
            dma((2,)),
            dma((2,)),
            dma((20,)),
            dma((20,)),
            dma((8,)),
            dma((8,)),
            dma((16,)),
            dma((16,)),
            dma((12,)),
            dma((12,)),
            dma((4,)),
            pltpu.SemaphoreType.REGULAR,
            pltpu.SemaphoreType.REGULAR,
        ],
        name="attend",
        cost_estimate=pl.CostEstimate(
            flops=30_000_000_000, bytes_accessed=30_000_000, transcendentals=3 * 1024 * 1024
        ),
        compiler_params=pltpu.CompilerParams(
            collective_id=2, has_side_effects=True, vmem_limit_bytes=VMEM_LIMIT
        ),
    )(scale, time, x, table, w, wo, x, drift, bound)


def body(paths, prev_drift, boundary, step_scale, time_ids, mod_table, w_qkv, output_weight):
    w = jnp.transpose(w_qkv, (1, 0, 2))
    grad_in_sum, grad_out_sum = attend(
        step_scale, time_ids, paths[0], prev_drift[0], mod_table, w, output_weight, boundary
    )
    grad_in_sum = jnp.transpose(grad_in_sum.reshape(3, 384, 384), (1, 0, 2))
    grad_out_sum = grad_out_sum.reshape(384, 384)
    return (grad_in_sum, grad_out_sum)


def solution(mesh):
    placed = (
        P("tm", "row", "col"),
        P("tm", "row", "col"),
        P(None, "row", "col"),
        P("tm"),
        P("tm"),
        P(None, None, "col"),
        P("col", None, "row"),
        P("row", "col"),
    )
    return jax.shard_map(
        body,
        mesh=mesh,
        in_specs=placed,
        out_specs=(P(("col", "tm"), None, "row"), P("row", ("col", "tm"))),
        check_vma=False,
    )
```

```python
import jax
import jax.numpy as jnp
from jax import lax
from jax.experimental import pallas as pl
from jax.experimental.pallas import tpu as pltpu
from jax.sharding import PartitionSpec as P

D = 6144
HEAD_DIM = 128
SCALE = HEAD_DIM**-0.5
MESH = pl.DeviceIdType.MESH
VMEM_LIMIT = 63 * 1024 * 1024

norm_eps = 1e-06

BF16 = jnp.bfloat16
F32 = jnp.float32
HALVES = (pl.ds(0, 1536), pl.ds(1536, 1536))


class Place:
    def __init__(self):
        self.t = lax.axis_index("tm")
        self.r = lax.axis_index("row")
        self.c = lax.axis_index("col")
        x = lax.rem(self.r, 4)
        base = self.r - x
        other = lax.rem(base + 4, 8)
        self.left = base + lax.rem(x + 3, 4)
        self.right = base + lax.rem(x + 1, 4)
        self.far = base + lax.rem(x + 2, 4)
        self.z = other + x
        self.zleft = other + lax.rem(x + 3, 4)
        self.zright = other + lax.rem(x + 1, 4)
        self.zfar = other + lax.rem(x + 2, 4)

    def row(self, r):
        return (self.t, r, self.c)

    def col(self):
        return (self.t, self.r, 1 - self.c)


def greet(signalled, awaited):
    barrier = pltpu.get_barrier_semaphore()
    for device in signalled:
        pl.semaphore_signal(barrier, inc=1, device_id=device, device_id_type=MESH)
    pl.semaphore_wait(barrier, awaited)


def remote(src, dst, send_sem, recv_sem, device):
    return pltpu.make_async_remote_copy(
        src_ref=src,
        dst_ref=dst,
        send_sem=send_sem,
        recv_sem=recv_sem,
        device_id=device,
        device_id_type=MESH,
    )


class Gather:
    def __init__(self, place, buf, send_sems, recv_sems, over_z):
        p = place
        self.over_z = over_z
        low, high, full = pl.ds(0, 64), pl.ds(64, 64), pl.ds(0, 128)
        plan = [
            (p.r, p.left, full, p.right),
            (p.r, p.right, full, p.left),
            (p.r, p.z, full, p.z),
            (p.left, p.far, low, p.right),
            (p.right, p.far, high, p.left),
            (p.z, p.zleft, full, p.right),
            (p.z, p.zright, full, p.left),
            (p.zleft, p.zfar, low, p.right),
            (p.zright, p.zfar, high, p.left),
            (p.far, p.zfar, full, p.z),
        ]
        self.out, self.into, self.started = {}, {}, []
        for c in (0, 1):
            for m, (sent, received, rows, target) in enumerate(plan):
                i = 10 * c + m
                device = p.row(target)
                a, b = buf.at[sent, rows, HALVES[c]], buf.at[received, rows, HALVES[c]]
                self.out[m, c] = remote(a, a, send_sems.at[i], recv_sems.at[i], device)
                self.into[m, c] = remote(b, b, send_sems.at[i], recv_sems.at[i], device)

    def send(self, c, *which):
        for m in which:
            self.out[m, c].start()
            self.started.append(self.out[m, c])

    def arrived(self, c, *which):
        for m in which:
            self.into[m, c].wait_recv()

    def finish(self):
        for copy in self.started:
            copy.wait_send()

    def run(self, place, visit, spare=None):
        p = place
        visit(0, p.r)
        if self.over_z:
            self.arrived(0, 0)
            self.send(0, 3)
            self.arrived(0, 1)
            self.send(0, 4)
            self.arrived(1, 2)
            self.send(1, 5, 6)
            self.arrived(1, 0)
            self.send(1, 3)
            self.arrived(1, 1)
            self.send(1, 4)
            self.arrived(0, 2)
            self.send(0, 5, 6)
            visit(1, p.left)
            self.arrived(0, 3, 4)
            self.send(0, 9)
            visit(2, p.right)
            visit(3, p.z)
            self.arrived(1, 5)
            self.send(1, 7)
            self.arrived(1, 6)
            self.send(1, 8)
            self.arrived(1, 3, 4)
            visit(4, p.far)
            self.arrived(0, 5)
            visit(5, p.zleft)
            self.arrived(0, 6)
            visit(6, p.zright)
            self.arrived(0, 9)
            self.arrived(1, 7, 8)
            visit(7, p.zfar)
            return
        for c in (0, 1):
            self.arrived(c, 0)
            self.send(c, 3)
            self.arrived(c, 1)
            self.send(c, 4)
            self.arrived(c, 2)
            self.send(c, 5, 6)
        visit(1, p.left)
        visit(2, p.right)
        visit(3, p.z)
        self.arrived(0, 5)
        self.send(0, 7)
        self.arrived(0, 6)
        self.send(0, 8)
        for c in (0, 1):
            self.arrived(c, 3, 4)
        visit(4, p.far)
        self.arrived(1, 5)
        self.send(1, 7)
        self.arrived(1, 6)
        self.send(1, 8)
        visit(5, p.zleft)
        visit(6, p.zright)
        if spare is not None:
            spare()
        for c in (0, 1):
            self.arrived(c, 7, 8)
        visit(7, p.zfar)


def attend_kernel(
    scale_ref, time_ref, x_ref, table_ref, w_hbm, wo_hbm, paths_hbm, drift_hbm, bound_hbm,
    grad_in_hbm, grad_out_hbm,
    grads_ref, mixed_ref, mixed_t, w_ref, wo_ref, drift_ref, full_ref, up_ref, moved, part, out_part, in_part,
    probs, outbox, in_half, in_full, gm_in, key_acc, value_acc,
    w_sems, late_sems, sq_sems, n_send, n_recv, u_send, u_recv, kv_send, kv_recv, q_send, q_recv,
    tm_send, tm_recv, b_sems, rs_send, rs_recv, gm_send, gm_recv, core_send, core_recv, y_send, y_recv, end_sems,
    core_free, y_free,
):
    p = Place()
    weight_copies = [
        pltpu.make_async_copy(w_hbm.at[j], w_ref.at[j], w_sems.at[j]) for j in range(3)
    ]
    late_copies = [
        pltpu.make_async_copy(wo_hbm, wo_ref, late_sems.at[0]),
        pltpu.make_async_copy(drift_hbm, drift_ref, late_sems.at[1]),
    ]
    for copy in weight_copies + late_copies:
        copy.start()
    after = (lax.rem(p.t + 1, 8), p.r, p.c)
    before = (lax.rem(p.t + 7, 8), p.r, p.c)
    core = lax.rem(p.t, 2)
    y = p.t // 2
    peers = [lax.rem(y + by, 4) for by in (2, 3, 1, 0)]
    partner = (2 * y + 1 - core, p.r, p.c)
    to_left = (2 * peers[1] + core, p.r, p.c)
    to_right = (2 * peers[2] + core, p.r, p.c)
    row_peers = [p.row(p.right), p.row(p.left), p.row(p.z)]
    greet(row_peers + [p.col(), before, partner, to_left, to_right], 8)

    sq_out, sq_in = part.at[0, 0, :, pl.ds(0, 128)], part.at[7, 0, :, pl.ds(0, 128)]
    squares = jnp.zeros((128, 1), F32)
    for i in range(4):
        piece = x_ref[:, i * 768 : (i + 1) * 768].astype(F32)
        squares = squares + jnp.sum(piece * piece, axis=-1, keepdims=True)
    sq_out[...] = jnp.broadcast_to(squares, (128, 128))
    swap = remote(sq_out, sq_in, sq_sems.at[0], sq_sems.at[1], p.col())
    swap.start()
    swap.wait()
    total = sq_out[:, :1] + sq_in[:, :1]
    scale = lax.rsqrt(total / D + norm_eps)
    gather = Gather(p, full_ref, n_send, n_recv, False)
    modulation = table_ref[time_ref[0]].astype(F32)
    for i in range(4):
        cols = slice(i * 768, (i + 1) * 768)
        piece = x_ref[:, cols].astype(F32)
        full_ref[p.r, :, cols] = (
            piece * scale * (1.0 + modulation[0:1, cols]) + modulation[1:2, cols]
        ).astype(BF16)
        if i % 2 == 1:
            gather.send(i // 2, 0, 1, 2)

    moves = [
        remote(paths_hbm, moved.at[0], tm_send.at[0], tm_recv.at[0], after),
        remote(drift_hbm, moved.at[1], tm_send.at[1], tm_recv.at[1], after),
    ]
    bounds = [pltpu.make_async_copy(bound_hbm.at[i], moved.at[i], b_sems.at[i]) for i in (0, 1)]

    @pl.when(p.t < 7)
    def _():
        for move in moves:
            move.start()

    @pl.when(p.t == 0)
    def _():
        for copy in bounds:
            copy.start()

    kv_copies, q_copies = [], []

    def project(k, owner):
        if k == 0:
            for copy in weight_copies:
                copy.wait()

        def product(j):
            term = jnp.dot(full_ref[owner], w_ref[j], preferred_element_type=F32)
            part[k, j] = term
            out_part[k, j] = term.astype(BF16)

        @pl.loop(1, 3)
        def _(j):
            product(j)

        pair = pl.ds(1, 2)
        copy = remote(
            out_part.at[k, pair], in_part.at[k, pair], kv_send.at[k], kv_recv.at[k], p.col()
        )
        copy.start()
        kv_copies.append(copy)
        product(0)
        q_copies.append(
            remote(out_part.at[k, 0], in_part.at[k, 0], q_send.at[k], q_recv.at[k], p.col())
        )

    owners = [p.r, p.left, p.right, p.z, p.far, p.zleft, p.zright, p.zfar]

    def rows_of(owner):
        return pl.ds(pl.multiple_of(owner * 128, 128), 128)

    def join_early():
        for copy in late_copies:
            copy.wait()
        for k in range(5):
            kv_copies[k].wait_recv()
            for j in (1, 2):
                part[k, j] += in_part[k, j].astype(F32)

    gather.run(p, project, join_early)
    query_order = [7, 5, 6, 4, 1, 2, 3, 0]
    for k in query_order:
        q_copies[k].start()


    def join(k, j):
        w_ref[j, rows_of(owners[k])] = (part[k, j] + in_part[k, j].astype(F32)).astype(BF16)

    for k in range(5):
        for j in (1, 2):
            w_ref[j, rows_of(owners[k])] = part[k, j].astype(BF16)
    for k in (5, 6, 7):
        kv_copies[k].wait_recv()
        join(k, 1)
        join(k, 2)

    def keys(h):
        return w_ref[1, :1024, h * 128 : (h + 1) * 128]

    def values(h):
        return w_ref[2, :1024, h * 128 : (h + 1) * 128]

    def attend(owner):
        for h in range(3):
            cols = slice(h * 128, (h + 1) * 128)
            scores = (
                lax.dot_general(
                    w_ref[0, rows_of(owner), cols],
                    keys(h),
                    (((1,), (1,)), ((), ())),
                    preferred_element_type=F32,
                )
                * SCALE
            )
            top = jnp.max(scores, axis=-1, keepdims=True)
            weights = jnp.exp(scores - top)
            weights = weights * (1.0 / jnp.sum(weights, axis=-1, keepdims=True))
            weights_low = weights.astype(BF16)
            probs[h, owner] = weights_low
            mixed_ref[owner, :, cols] = jnp.dot(
                weights_low, values(h), preferred_element_type=F32
            ).astype(BF16)

    def ready(k):
        q_copies[k].wait_recv()
        join(k, 0)

    def out_rows(owner, c, lo, n, extra, put):
        @pl.loop(0, 2)
        def _(i):
            near = pl.ds(pl.multiple_of(i * 768, 768), 768)
            cols = pl.ds(pl.multiple_of(c * 1536 + i * 768, 768), 768)
            term = jnp.dot(
                mixed_ref[owner, lo : lo + n, :], wo_ref[:, cols], preferred_element_type=F32
            )
            for ref in extra:
                term = term + ref[:, near].astype(F32)
            put(cols, term)

    low, high, full = pl.ds(0, 64), pl.ds(64, 64), pl.ds(0, 128)
    plan = {
        "zfar low": (0, low, p.left, 0),
        "zfar high": (0, high, p.right, 1),
        "far low": (3, low, p.left, 2),
        "far high": (3, high, p.right, 3),
        "zfar": (0, full, p.z, 0),
        "zleft": (1, full, p.left, 1),
        "zright": (2, full, p.right, 2),
        "left": (4, full, p.left, 3),
        "right": (5, full, p.right, 4),
        "z": (6, full, p.z, 5),
    }
    copies, landed, started = {}, {}, []
    for c in (0, 1):
        for m, (name, (slot, rows, target, place)) in enumerate(plan.items()):
            i = 10 * c + m
            landed[name, c] = in_half.at[c, place] if m < 4 else in_full.at[c, place]
            copies[name, c] = remote(
                outbox.at[slot, rows, HALVES[c]],
                landed[name, c],
                rs_send.at[i],
                rs_recv.at[i],
                p.row(target),
            )

    def send(name, c):
        copies[name, c].start()
        started.append(copies[name, c])

    def arrived(*names_and_halves):
        for name, c in names_and_halves:
            copies[name, c].wait_recv()

    def to_slot(slot, lo, n):
        def put(cols, term):
            outbox[slot, lo : lo + n, cols] = term.astype(BF16)

        return put

    def share(slot, owner, c, lo=0, n=128, extra=()):
        out_rows(owner, c, lo, n, [landed[name, c] for name in extra], to_slot(slot, lo, n))

    ready(7)
    attend(p.zfar)
    share(0, p.zfar, 0)
    send("zfar low", 0)
    send("zfar high", 0)
    share(0, p.zfar, 1)
    send("zfar", 1)
    ready(5)
    attend(p.zleft)
    share(1, p.zleft, 1)
    send("zleft", 1)
    ready(6)
    attend(p.zright)
    share(2, p.zright, 1)
    send("zright", 1)
    share(1, p.zleft, 0, 64, 64)
    share(2, p.zright, 0, 0, 64)
    arrived(("zfar low", 0))
    share(1, p.zleft, 0, 0, 64, ["zfar low"])
    send("zleft", 0)
    arrived(("zfar high", 0))
    share(2, p.zright, 0, 64, 64, ["zfar high"])
    send("zright", 0)
    ready(4)
    attend(p.far)
    share(3, p.far, 0)
    send("far low", 0)
    send("far high", 0)
    for k in (1, 2, 3, 0):
        ready(k)

    @pl.loop(0, 4)
    def _(i):
        attend(
            jnp.where(
                i == 0, p.left, jnp.where(i == 1, p.right, jnp.where(i == 2, p.z, p.r))
            )
        )

    arrived(("zfar", 1))
    share(3, p.far, 1, extra=["zfar"])
    send("far low", 1)
    send("far high", 1)
    for c in (1, 0):
        arrived(("zleft", c), ("zright", c))
        share(6, p.z, c, extra=["zleft", "zright"])
        send("z", c)
    for c in (0, 1):
        share(4, p.left, c, 64, 64)
        share(5, p.right, c, 0, 64)
        arrived(("far low", c))
        share(4, p.left, c, 0, 64, ["far low"])
        send("left", c)
        arrived(("far high", c))
        share(5, p.right, c, 64, 64, ["far high"])
        send("right", c)

    @pl.when(p.t > 0)
    def _():
        for move in moves:
            move.wait_recv()

    @pl.when(p.t == 0)
    def _():
        for copy in bounds:
            copy.wait()

    key_acc[...] = jnp.zeros_like(key_acc)
    value_acc[...] = jnp.zeros_like(value_acc)

    def to_up(cols, term):
        target = moved[0, :, cols].astype(F32) + scale_ref[0] * (
            moved[1, :, cols].astype(F32) - drift_ref[:, cols].astype(F32)
        )
        rest = x_ref[:, cols].astype(F32) - target
        up_ref[p.r, :, cols] = ((rest + term) * (1024**-0.5)).astype(BF16)

    gather_up = Gather(p, up_ref, u_send, u_recv, True)
    for c in (0, 1):
        names = ["left", "right", "z"]
        arrived(*[(name, c) for name in names])
        out_rows(p.r, c, 0, 128, [landed[name, c] for name in names], to_up)
        gather_up.send(c, 0, 1, 2)

    pl.semaphore_signal(core_free, inc=1, device_id=partner, device_id_type=MESH)
    pl.semaphore_signal(y_free, inc=1, device_id=to_left, device_id_type=MESH)
    pl.semaphore_signal(y_free, inc=1, device_id=to_right, device_id_type=MESH)
    for copy in started + q_copies + kv_copies:
        copy.wait_send()
    mixed_t[...] = mixed_ref[...].reshape(1024, 384).T

    gm_copies, waiting = [], []

    def backward(k, owner):
        gm_copies[k].wait_recv()
        grad = (part[k, 0] + gm_in[k].astype(F32)).astype(BF16)
        tokens = rows_of(owner)
        for h in range(3):
            cols = slice(h * 128, (h + 1) * 128)
            head_grad = grad[:, cols]
            weights_low = probs[h, owner]
            weights = weights_low.astype(F32)
            value_acc[h] += jnp.dot(head_grad.T, weights_low, preferred_element_type=F32)
            grad_weights = lax.dot_general(
                head_grad, values(h), (((1,), (1,)), ((), ())), preferred_element_type=F32
            )
            inner = jnp.sum(grad_weights * weights, axis=-1, keepdims=True)
            grad_scores = (weights * (grad_weights - inner) * SCALE).astype(BF16)
            query_grad = jnp.dot(grad_scores, keys(h), preferred_element_type=F32)
            grads_ref[0, cols, tokens] = query_grad.T.astype(BF16)
            key_acc[h] += jnp.dot(
                w_ref[0, rows_of(owner), cols].T, grad_scores, preferred_element_type=F32
            )

    def visit(k, owner):
        term = lax.dot_general(
            up_ref[owner], wo_ref[...], (((1,), (1,)), ((), ())), preferred_element_type=F32
        )
        part[k, 0] = term
        rows = pl.ds(1024 + 128 * k, 128)
        w_ref[0, rows] = term.astype(BF16)
        copy = remote(w_ref.at[0, rows], gm_in.at[k], gm_send.at[k], gm_recv.at[k], p.col())
        copy.start()
        gm_copies.append(copy)
        waiting.append((k, owner))
        if 0 < k < 7:
            backward(*waiting.pop(0))

    chunks = [2 * peer + 1 - core for peer in peers] + [2 * peer + core for peer in peers]

    def unit(k, g):
        cols = pl.ds(pl.multiple_of(chunks[k] * 384, 384), 384)
        left = grads_ref[g] if g < 3 else mixed_t[...]
        right = full_ref[:, :, cols] if g < 3 else up_ref[:, :, cols]
        term = jnp.dot(left, right.reshape(1024, 384), preferred_element_type=F32)
        return term.reshape(3, 128, 384)

    core_out, core_in, core_copies = {}, {}, {}
    for i in range(4):
        for g in range(4):
            n = 4 * i + g
            slots = pl.ds(3 * (n // 8), 3)
            core_out[i, g] = outbox.at[slots, :, pl.ds(384 * (n % 8), 384)]
            core_in[i, g] = in_full.at[
                i // 2, pl.ds(3 * (i % 2), 3), :, pl.ds(384 * g, 384)
            ]
            core_copies[i, g] = remote(
                core_out[i, g], core_in[i, g], core_send.at[n], core_recv.at[n], partner
            )
    y_order = [
        (0, 3), (1, 3), (2, 3), (0, 0), (0, 1), (0, 2), (1, 0), (1, 1),
        (1, 2), (2, 0), (2, 1), (2, 2),
    ]
    y_out, y_in, y_copies = {}, {}, {}
    for n, (i, g) in enumerate(y_order):
        if n < 8:
            y_out[i, g], y_in[i, g] = out_part.at[n], in_part.at[n]
        else:
            rows = pl.ds(1024 + 384 * (n - 8), 384)
            y_out[i, g], y_in[i, g] = w_ref.at[1, rows], w_ref.at[2, rows]
        leftward = g < 2 if i == 0 else i == 1
        y_copies[i, g] = remote(
            y_out[i, g], y_in[i, g], y_send.at[n], y_recv.at[n],
            to_left if leftward else to_right,
        )

    def for_partner(i, *groups):
        for g in groups:
            core_out[i, g][...] = unit(i, g).astype(BF16)
            core_copies[i, g].start()

    def summed(i, g):
        term = unit(4 + i, g)
        core_copies[i, g].wait_recv()
        term = term + core_in[i, g][...].astype(F32)
        return term if g == 3 else term.reshape(384, 384).T.reshape(3, 128, 384)

    def landed_unit(i, g):
        return y_in[i, g][...].reshape(3, 128, 384).astype(F32)

    def onward(i, g):
        total = summed(i, g)
        if (i, g) in ((1, 0), (1, 1), (2, 2), (2, 3)):
            y_copies[0, g].wait_recv()
            total = total + landed_unit(0, g)
        y_out[i, g][...] = total.reshape(y_out[i, g].shape).astype(BF16)
        y_copies[i, g].start()

    gather_up.run(p, visit)
    pl.semaphore_wait(core_free, 1)
    for_partner(0, 3)
    for_partner(1, 3)
    for_partner(2, 3)
    pl.semaphore_wait(y_free, 2)
    onward(0, 3)
    onward(1, 3)
    for block in waiting:
        backward(*block)
    for h in range(3):
        cols = slice(h * 128, (h + 1) * 128)
        grads_ref[1, cols, :] = key_acc[h].astype(BF16)
        grads_ref[2, cols, :] = value_acc[h].astype(BF16)
    for_partner(0, 0, 2)
    onward(0, 0)
    onward(0, 2)
    for_partner(0, 1)
    for_partner(2, 0)
    onward(0, 1)
    onward(2, 3)
    for_partner(1, 2)
    onward(2, 0)
    onward(1, 2)
    for_partner(2, 1)
    for_partner(1, 0, 1)
    onward(2, 1)
    for_partner(2, 2)
    for_partner(3, 3, 0, 1, 2)
    onward(1, 0)
    onward(2, 2)
    onward(1, 1)
    for g in (3, 2, 0, 1):
        part[g] = summed(3, g)
    ends = []
    for n, g in enumerate((3, 2, 0, 1)):
        y_copies[1, g].wait_recv()
        y_copies[2, g].wait_recv()
        part[g] += landed_unit(1, g) + landed_unit(2, g)
        target = grad_in_hbm.at[g] if g < 3 else grad_out_hbm
        ends.append(pltpu.make_async_copy(part.at[g], target, end_sems.at[n]))
        ends[-1].start()
    for copy in gm_copies + list(core_copies.values()) + list(y_copies.values()):
        copy.wait_send()
    gather.finish()
    gather_up.finish()

    @pl.when(p.t < 7)
    def _():
        for move in moves:
            move.wait_send()

    for copy in ends:
        copy.wait()


def attend(scale, time, x, drift, table, w, wo, bound):
    vmem = pl.BlockSpec(memory_space=pltpu.VMEM)
    smem = pl.BlockSpec(memory_space=pltpu.SMEM)
    hbm = pl.BlockSpec(memory_space=pl.ANY)
    dma = pltpu.SemaphoreType.DMA
    return pl.pallas_call(
        attend_kernel,
        out_shape=(
            jax.ShapeDtypeStruct((3, 3, 128, 384), F32),
            jax.ShapeDtypeStruct((3, 128, 384), F32),
        ),
        in_specs=[smem, smem, vmem, vmem, hbm, hbm, hbm, hbm, hbm],
        out_specs=(hbm, hbm),
        scratch_shapes=[
            pltpu.VMEM((3, 384, 1024), BF16),
            pltpu.VMEM((8, 128, 384), BF16),
            pltpu.VMEM((384, 1024), BF16),
            pltpu.VMEM((3, 3072, 384), BF16),
            pltpu.VMEM((384, 3072), BF16),
            pltpu.VMEM((128, 3072), BF16),
            pltpu.VMEM((8, 128, 3072), BF16),
            pltpu.VMEM((8, 128, 3072), BF16),
            pltpu.VMEM((2, 128, 3072), BF16),
            pltpu.VMEM((8, 3, 128, 384), F32),
            pltpu.VMEM((8, 3, 128, 384), BF16),
            pltpu.VMEM((8, 3, 128, 384), BF16),
            pltpu.VMEM((3, 8, 128, 1024), BF16),
            pltpu.VMEM((7, 128, 3072), BF16),
            pltpu.VMEM((2, 4, 64, 1536), BF16),
            pltpu.VMEM((2, 6, 128, 1536), BF16),
            pltpu.VMEM((8, 128, 384), BF16),
            pltpu.VMEM((3, 128, 1024), F32),
            pltpu.VMEM((3, 128, 1024), F32),
            dma((3,)),
            dma((2,)),
            dma((2,)),
            dma((20,)),
            dma((20,)),
            dma((20,)),
            dma((20,)),
            dma((8,)),
            dma((8,)),
            dma((8,)),
            dma((8,)),
            dma((2,)),
            dma((2,)),
            dma((2,)),
            dma((20,)),
            dma((20,)),
            dma((8,)),
            dma((8,)),
            dma((16,)),
            dma((16,)),
            dma((12,)),
            dma((12,)),
            dma((4,)),
            pltpu.SemaphoreType.REGULAR,
            pltpu.SemaphoreType.REGULAR,
        ],
        name="attend",
        cost_estimate=pl.CostEstimate(
            flops=30_000_000_000, bytes_accessed=30_000_000, transcendentals=3 * 1024 * 1024
        ),
        compiler_params=pltpu.CompilerParams(
            collective_id=2, has_side_effects=True, vmem_limit_bytes=VMEM_LIMIT
        ),
    )(scale, time, x, table, w, wo, x, drift, bound)


def body(paths, prev_drift, boundary, step_scale, time_ids, mod_table, w_qkv, output_weight):
    w = jnp.transpose(w_qkv, (1, 0, 2))
    grad_in_sum, grad_out_sum = attend(
        step_scale, time_ids, paths[0], prev_drift[0], mod_table, w, output_weight, boundary
    )
    grad_in_sum = jnp.transpose(grad_in_sum.reshape(3, 384, 384), (1, 0, 2))
    grad_out_sum = grad_out_sum.reshape(384, 384)
    return (grad_in_sum, grad_out_sum)


def solution(mesh):
    placed = (
        P("tm", "row", "col"),
        P("tm", "row", "col"),
        P(None, "row", "col"),
        P("tm"),
        P("tm"),
        P(None, None, "col"),
        P("col", None, "row"),
        P("row", "col"),
    )
    return jax.shard_map(
        body,
        mesh=mesh,
        in_specs=placed,
        out_specs=(P(("col", "tm"), None, "row"), P("row", ("col", "tm"))),
        check_vma=False,
    )
```

```python
import jax
import jax.numpy as jnp
from jax import lax
from jax.experimental import pallas as pl
from jax.experimental.pallas import tpu as pltpu
from jax.sharding import PartitionSpec as P

D = 6144
HEAD_DIM = 128
SCALE = HEAD_DIM**-0.5
MESH = pl.DeviceIdType.MESH
VMEM_LIMIT = 63 * 1024 * 1024

norm_eps = 1e-06

BF16 = jnp.bfloat16
F32 = jnp.float32
HALVES = (pl.ds(0, 1536), pl.ds(1536, 1536))


class Place:
    def __init__(self):
        self.t = lax.axis_index("tm")
        self.r = lax.axis_index("row")
        self.c = lax.axis_index("col")
        x = lax.rem(self.r, 4)
        base = self.r - x
        other = lax.rem(base + 4, 8)
        self.left = base + lax.rem(x + 3, 4)
        self.right = base + lax.rem(x + 1, 4)
        self.far = base + lax.rem(x + 2, 4)
        self.z = other + x
        self.zleft = other + lax.rem(x + 3, 4)
        self.zright = other + lax.rem(x + 1, 4)
        self.zfar = other + lax.rem(x + 2, 4)

    def row(self, r):
        return (self.t, r, self.c)

    def col(self):
        return (self.t, self.r, 1 - self.c)


def greet(signalled, awaited):
    barrier = pltpu.get_barrier_semaphore()
    for device in signalled:
        pl.semaphore_signal(barrier, inc=1, device_id=device, device_id_type=MESH)
    pl.semaphore_wait(barrier, awaited)


def remote(src, dst, send_sem, recv_sem, device):
    return pltpu.make_async_remote_copy(
        src_ref=src,
        dst_ref=dst,
        send_sem=send_sem,
        recv_sem=recv_sem,
        device_id=device,
        device_id_type=MESH,
    )


class Gather:
    def __init__(self, place, buf, send_sems, recv_sems, over_z):
        p = place
        self.over_z = over_z
        low, high, full = pl.ds(0, 64), pl.ds(64, 64), pl.ds(0, 128)
        plan = [
            (p.r, p.left, full, p.right),
            (p.r, p.right, full, p.left),
            (p.r, p.z, full, p.z),
            (p.left, p.far, low, p.right),
            (p.right, p.far, high, p.left),
            (p.z, p.zleft, full, p.right),
            (p.z, p.zright, full, p.left),
            (p.zleft, p.zfar, low, p.right),
            (p.zright, p.zfar, high, p.left),
            (p.far, p.zfar, full, p.z),
        ]
        self.out, self.into, self.started = {}, {}, []
        for c in (0, 1):
            for m, (sent, received, rows, target) in enumerate(plan):
                i = 10 * c + m
                device = p.row(target)
                a, b = buf.at[sent, rows, HALVES[c]], buf.at[received, rows, HALVES[c]]
                self.out[m, c] = remote(a, a, send_sems.at[i], recv_sems.at[i], device)
                self.into[m, c] = remote(b, b, send_sems.at[i], recv_sems.at[i], device)

    def send(self, c, *which):
        for m in which:
            self.out[m, c].start()
            self.started.append(self.out[m, c])

    def arrived(self, c, *which):
        for m in which:
            self.into[m, c].wait_recv()

    def finish(self):
        for copy in self.started:
            copy.wait_send()

    def run(self, place, visit, spare=None):
        p = place
        visit(0, p.r)
        if self.over_z:
            self.arrived(0, 0)
            self.send(0, 3)
            self.arrived(0, 1)
            self.send(0, 4)
            self.arrived(1, 2)
            self.send(1, 5, 6)
            self.arrived(1, 0)
            self.send(1, 3)
            self.arrived(1, 1)
            self.send(1, 4)
            self.arrived(0, 2)
            self.send(0, 5, 6)
            visit(1, p.left)
            self.arrived(0, 3, 4)
            self.send(0, 9)
            visit(2, p.right)
            visit(3, p.z)
            self.arrived(1, 5)
            self.send(1, 7)
            self.arrived(1, 6)
            self.send(1, 8)
            self.arrived(1, 3, 4)
            visit(4, p.far)
            self.arrived(0, 5)
            visit(5, p.zleft)
            self.arrived(0, 6)
            visit(6, p.zright)
            self.arrived(0, 9)
            self.arrived(1, 7, 8)
            visit(7, p.zfar)
            return
        for c in (0, 1):
            self.arrived(c, 0)
            self.send(c, 3)
            self.arrived(c, 1)
            self.send(c, 4)
            self.arrived(c, 2)
            self.send(c, 5, 6)
        visit(1, p.left)
        visit(2, p.right)
        visit(3, p.z)
        self.arrived(0, 5)
        self.send(0, 7)
        self.arrived(0, 6)
        self.send(0, 8)
        for c in (0, 1):
            self.arrived(c, 3, 4)
        visit(4, p.far)
        self.arrived(1, 5)
        self.send(1, 7)
        self.arrived(1, 6)
        self.send(1, 8)
        visit(5, p.zleft)
        visit(6, p.zright)
        if spare is not None:
            spare()
        for c in (0, 1):
            self.arrived(c, 7, 8)
        visit(7, p.zfar)


def attend_kernel(
    scale_ref, time_ref, x_ref, table_ref, w_hbm, wo_hbm, paths_hbm, drift_hbm, bound_hbm,
    grad_in_hbm, grad_out_hbm,
    grads_ref, mixed_ref, mixed_t, w_ref, wo_ref, drift_ref, full_ref, up_ref, moved, part, out_part, in_part,
    probs, outbox, in_half, in_full, gm_in, key_acc, value_acc,
    w_sems, late_sems, sq_sems, n_send, n_recv, u_send, u_recv, kv_send, kv_recv, q_send, q_recv,
    tm_send, tm_recv, b_sems, rs_send, rs_recv, gm_send, gm_recv, core_send, core_recv, y_send, y_recv, end_sems,
    core_free, y_free,
):
    p = Place()
    weight_copies = [
        pltpu.make_async_copy(w_hbm.at[j], w_ref.at[j], w_sems.at[j]) for j in range(3)
    ]
    late_copies = [
        pltpu.make_async_copy(wo_hbm, wo_ref, late_sems.at[0]),
        pltpu.make_async_copy(drift_hbm, drift_ref, late_sems.at[1]),
    ]
    for copy in weight_copies + late_copies:
        copy.start()
    after = (lax.rem(p.t + 1, 8), p.r, p.c)
    before = (lax.rem(p.t + 7, 8), p.r, p.c)
    core = lax.rem(p.t, 2)
    y = p.t // 2
    peers = [lax.rem(y + by, 4) for by in (2, 3, 1, 0)]
    partner = (2 * y + 1 - core, p.r, p.c)
    to_left = (2 * peers[1] + core, p.r, p.c)
    to_right = (2 * peers[2] + core, p.r, p.c)
    row_peers = [p.row(p.right), p.row(p.left), p.row(p.z)]
    greet(row_peers + [p.col(), before, partner, to_left, to_right], 8)

    sq_out, sq_in = part.at[0, 0, :, pl.ds(0, 128)], part.at[7, 0, :, pl.ds(0, 128)]
    squares = jnp.zeros((128, 1), F32)
    for i in range(4):
        piece = x_ref[:, i * 768 : (i + 1) * 768].astype(F32)
        squares = squares + jnp.sum(piece * piece, axis=-1, keepdims=True)
    sq_out[...] = jnp.broadcast_to(squares, (128, 128))
    swap = remote(sq_out, sq_in, sq_sems.at[0], sq_sems.at[1], p.col())
    swap.start()
    swap.wait()
    total = sq_out[:, :1] + sq_in[:, :1]
    scale = lax.rsqrt(total / D + norm_eps)
    gather = Gather(p, full_ref, n_send, n_recv, False)
    modulation = table_ref[time_ref[0]].astype(F32)
    for i in range(4):
        cols = slice(i * 768, (i + 1) * 768)
        piece = x_ref[:, cols].astype(F32)
        full_ref[p.r, :, cols] = (
            piece * scale * (1.0 + modulation[0:1, cols]) + modulation[1:2, cols]
        ).astype(BF16)
        if i % 2 == 1:
            gather.send(i // 2, 0, 1, 2)

    moves = [
        remote(paths_hbm, moved.at[0], tm_send.at[0], tm_recv.at[0], after),
        remote(drift_hbm, moved.at[1], tm_send.at[1], tm_recv.at[1], after),
    ]
    bounds = [pltpu.make_async_copy(bound_hbm.at[i], moved.at[i], b_sems.at[i]) for i in (0, 1)]

    @pl.when(p.t < 7)
    def _():
        for move in moves:
            move.start()

    @pl.when(p.t == 0)
    def _():
        for copy in bounds:
            copy.start()

    kv_copies, q_copies = [], []

    def project(k, owner):
        if k == 0:
            for copy in weight_copies:
                copy.wait()

        def product(j):
            term = jnp.dot(full_ref[owner], w_ref[j], preferred_element_type=F32)
            part[k, j] = term
            out_part[k, j] = term.astype(BF16)

        @pl.loop(1, 3)
        def _(j):
            product(j)

        pair = pl.ds(1, 2)
        copy = remote(
            out_part.at[k, pair], in_part.at[k, pair], kv_send.at[k], kv_recv.at[k], p.col()
        )
        copy.start()
        kv_copies.append(copy)
        product(0)
        q_copies.append(
            remote(out_part.at[k, 0], in_part.at[k, 0], q_send.at[k], q_recv.at[k], p.col())
        )

    owners = [p.r, p.left, p.right, p.z, p.far, p.zleft, p.zright, p.zfar]

    def rows_of(owner):
        return pl.ds(pl.multiple_of(owner * 128, 128), 128)

    def join_early():
        for copy in late_copies:
            copy.wait()
        for k in range(5):
            kv_copies[k].wait_recv()
            for j in (1, 2):
                part[k, j] += in_part[k, j].astype(F32)

    gather.run(p, project, join_early)
    query_order = [7, 5, 6, 4, 1, 2, 3, 0]
    for k in query_order:
        q_copies[k].start()


    def join(k, j):
        w_ref[j, rows_of(owners[k])] = (part[k, j] + in_part[k, j].astype(F32)).astype(BF16)

    for k in range(5):
        for j in (1, 2):
            w_ref[j, rows_of(owners[k])] = part[k, j].astype(BF16)
    for k in (5, 6, 7):
        kv_copies[k].wait_recv()
        join(k, 1)
        join(k, 2)

    def keys(h):
        return w_ref[1, :1024, h * 128 : (h + 1) * 128]

    def values(h):
        return w_ref[2, :1024, h * 128 : (h + 1) * 128]

    def attend(owner):
        for h in range(3):
            cols = slice(h * 128, (h + 1) * 128)
            scores = (
                lax.dot_general(
                    w_ref[0, rows_of(owner), cols],
                    keys(h),
                    (((1,), (1,)), ((), ())),
                    preferred_element_type=F32,
                )
                * SCALE
            )
            top = jnp.max(scores, axis=-1, keepdims=True)
            weights = jnp.exp(scores - top)
            weights = weights * (1.0 / jnp.sum(weights, axis=-1, keepdims=True))
            weights_low = weights.astype(BF16)
            probs[h, owner] = weights_low
            mixed_ref[owner, :, cols] = jnp.dot(
                weights_low, values(h), preferred_element_type=F32
            ).astype(BF16)

    def ready(k):
        q_copies[k].wait_recv()
        join(k, 0)

    def out_rows(owner, c, lo, n, extra, put):
        @pl.loop(0, 2)
        def _(i):
            near = pl.ds(pl.multiple_of(i * 768, 768), 768)
            cols = pl.ds(pl.multiple_of(c * 1536 + i * 768, 768), 768)
            term = jnp.dot(
                mixed_ref[owner, lo : lo + n, :], wo_ref[:, cols], preferred_element_type=F32
            )
            for ref in extra:
                term = term + ref[:, near].astype(F32)
            put(cols, term)

    low, high, full = pl.ds(0, 64), pl.ds(64, 64), pl.ds(0, 128)
    plan = {
        "zfar low": (0, low, p.left, 0),
        "zfar high": (0, high, p.right, 1),
        "far low": (3, low, p.left, 2),
        "far high": (3, high, p.right, 3),
        "zfar": (0, full, p.z, 0),
        "zleft": (1, full, p.left, 1),
        "zright": (2, full, p.right, 2),
        "left": (4, full, p.left, 3),
        "right": (5, full, p.right, 4),
        "z": (6, full, p.z, 5),
    }
    copies, landed, started = {}, {}, []
    for c in (0, 1):
        for m, (name, (slot, rows, target, place)) in enumerate(plan.items()):
            i = 10 * c + m
            landed[name, c] = in_half.at[c, place] if m < 4 else in_full.at[c, place]
            copies[name, c] = remote(
                outbox.at[slot, rows, HALVES[c]],
                landed[name, c],
                rs_send.at[i],
                rs_recv.at[i],
                p.row(target),
            )

    def send(name, c):
        copies[name, c].start()
        started.append(copies[name, c])

    def arrived(*names_and_halves):
        for name, c in names_and_halves:
            copies[name, c].wait_recv()

    def to_slot(slot, lo, n):
        def put(cols, term):
            outbox[slot, lo : lo + n, cols] = term.astype(BF16)

        return put

    def share(slot, owner, c, lo=0, n=128, extra=()):
        out_rows(owner, c, lo, n, [landed[name, c] for name in extra], to_slot(slot, lo, n))

    ready(7)
    attend(p.zfar)
    share(0, p.zfar, 0)
    send("zfar low", 0)
    send("zfar high", 0)
    share(0, p.zfar, 1)
    send("zfar", 1)
    ready(5)
    attend(p.zleft)
    share(1, p.zleft, 1)
    send("zleft", 1)
    ready(6)
    attend(p.zright)
    share(2, p.zright, 1)
    send("zright", 1)
    share(1, p.zleft, 0, 64, 64)
    share(2, p.zright, 0, 0, 64)
    arrived(("zfar low", 0))
    share(1, p.zleft, 0, 0, 64, ["zfar low"])
    send("zleft", 0)
    arrived(("zfar high", 0))
    share(2, p.zright, 0, 64, 64, ["zfar high"])
    send("zright", 0)
    ready(4)
    attend(p.far)
    share(3, p.far, 0)
    send("far low", 0)
    send("far high", 0)
    for k in (1, 2, 3, 0):
        ready(k)

    @pl.loop(0, 4)
    def _(i):
        attend(
            jnp.where(
                i == 0, p.left, jnp.where(i == 1, p.right, jnp.where(i == 2, p.z, p.r))
            )
        )

    arrived(("zfar", 1))
    share(3, p.far, 1, extra=["zfar"])
    send("far low", 1)
    send("far high", 1)
    for c in (1, 0):
        arrived(("zleft", c), ("zright", c))
        share(6, p.z, c, extra=["zleft", "zright"])
        send("z", c)
    for c in (0, 1):
        share(4, p.left, c, 64, 64)
        share(5, p.right, c, 0, 64)
        arrived(("far low", c))
        share(4, p.left, c, 0, 64, ["far low"])
        send("left", c)
        arrived(("far high", c))
        share(5, p.right, c, 64, 64, ["far high"])
        send("right", c)

    @pl.when(p.t > 0)
    def _():
        for move in moves:
            move.wait_recv()

    @pl.when(p.t == 0)
    def _():
        for copy in bounds:
            copy.wait()

    key_acc[...] = jnp.zeros_like(key_acc)
    value_acc[...] = jnp.zeros_like(value_acc)

    def to_up(cols, term):
        target = moved[0, :, cols].astype(F32) + scale_ref[0] * (
            moved[1, :, cols].astype(F32) - drift_ref[:, cols].astype(F32)
        )
        rest = x_ref[:, cols].astype(F32) - target
        up_ref[p.r, :, cols] = ((rest + term) * (1024**-0.5)).astype(BF16)

    gather_up = Gather(p, up_ref, u_send, u_recv, True)
    for c in (0, 1):
        names = ["left", "right", "z"]
        arrived(*[(name, c) for name in names])
        out_rows(p.r, c, 0, 128, [landed[name, c] for name in names], to_up)
        gather_up.send(c, 0, 1, 2)

    pl.semaphore_signal(core_free, inc=1, device_id=partner, device_id_type=MESH)
    pl.semaphore_signal(y_free, inc=1, device_id=to_left, device_id_type=MESH)
    pl.semaphore_signal(y_free, inc=1, device_id=to_right, device_id_type=MESH)
    for copy in started + q_copies + kv_copies:
        copy.wait_send()
    mixed_t[...] = mixed_ref[...].reshape(1024, 384).T

    gm_copies, waiting = [], []

    def backward(k, owner):
        gm_copies[k].wait_recv()
        grad = (part[k, 0] + gm_in[k].astype(F32)).astype(BF16)
        tokens = rows_of(owner)
        for h in range(3):
            cols = slice(h * 128, (h + 1) * 128)
            head_grad = grad[:, cols]
            weights_low = probs[h, owner]
            weights = weights_low.astype(F32)
            value_acc[h] += jnp.dot(head_grad.T, weights_low, preferred_element_type=F32)
            grad_weights = lax.dot_general(
                head_grad, values(h), (((1,), (1,)), ((), ())), preferred_element_type=F32
            )
            inner = jnp.sum(grad_weights * weights, axis=-1, keepdims=True)
            grad_scores = (weights * (grad_weights - inner) * SCALE).astype(BF16)
            query_grad = jnp.dot(grad_scores, keys(h), preferred_element_type=F32)
            grads_ref[0, cols, tokens] = query_grad.T.astype(BF16)
            key_acc[h] += jnp.dot(
                w_ref[0, rows_of(owner), cols].T, grad_scores, preferred_element_type=F32
            )

    def visit(k, owner):
        term = lax.dot_general(
            up_ref[owner], wo_ref[...], (((1,), (1,)), ((), ())), preferred_element_type=F32
        )
        part[k, 0] = term
        rows = pl.ds(1024 + 128 * k, 128)
        w_ref[0, rows] = term.astype(BF16)
        copy = remote(w_ref.at[0, rows], gm_in.at[k], gm_send.at[k], gm_recv.at[k], p.col())
        copy.start()
        gm_copies.append(copy)
        waiting.append((k, owner))
        if 0 < k < 7:
            backward(*waiting.pop(0))

    chunks = [2 * peer + 1 - core for peer in peers] + [2 * peer + core for peer in peers]

    def unit(k, g):
        cols = pl.ds(pl.multiple_of(chunks[k] * 384, 384), 384)
        left = grads_ref[g] if g < 3 else mixed_t[...]
        right = full_ref[:, :, cols] if g < 3 else up_ref[:, :, cols]
        term = jnp.dot(left, right.reshape(1024, 384), preferred_element_type=F32)
        return term.reshape(3, 128, 384)

    core_out, core_in, core_copies = {}, {}, {}
    for i in range(4):
        for g in range(4):
            n = 4 * i + g
            slots = pl.ds(3 * (n // 8), 3)
            core_out[i, g] = outbox.at[slots, :, pl.ds(384 * (n % 8), 384)]
            core_in[i, g] = in_full.at[
                i // 2, pl.ds(3 * (i % 2), 3), :, pl.ds(384 * g, 384)
            ]
            core_copies[i, g] = remote(
                core_out[i, g], core_in[i, g], core_send.at[n], core_recv.at[n], partner
            )
    y_order = [
        (0, 3), (1, 3), (2, 3), (0, 0), (0, 1), (0, 2), (1, 0), (1, 1),
        (1, 2), (2, 0), (2, 1), (2, 2),
    ]
    y_out, y_in, y_copies = {}, {}, {}
    for n, (i, g) in enumerate(y_order):
        if n < 8:
            y_out[i, g], y_in[i, g] = out_part.at[n], in_part.at[n]
        else:
            rows = pl.ds(1024 + 384 * (n - 8), 384)
            y_out[i, g], y_in[i, g] = w_ref.at[1, rows], w_ref.at[2, rows]
        leftward = g < 2 if i == 0 else i == 1
        y_copies[i, g] = remote(
            y_out[i, g], y_in[i, g], y_send.at[n], y_recv.at[n],
            to_left if leftward else to_right,
        )

    def for_partner(i, *groups):
        for g in groups:
            core_out[i, g][...] = unit(i, g).astype(BF16)
            core_copies[i, g].start()

    def summed(i, g):
        term = unit(4 + i, g)
        core_copies[i, g].wait_recv()
        term = term + core_in[i, g][...].astype(F32)
        return term if g == 3 else term.reshape(384, 384).T.reshape(3, 128, 384)

    def landed_unit(i, g):
        return y_in[i, g][...].reshape(3, 128, 384).astype(F32)

    def onward(i, g):
        total = summed(i, g)
        if (i, g) in ((1, 0), (1, 1), (2, 2), (2, 3)):
            y_copies[0, g].wait_recv()
            total = total + landed_unit(0, g)
        y_out[i, g][...] = total.reshape(y_out[i, g].shape).astype(BF16)
        y_copies[i, g].start()

    gather_up.run(p, visit)
    pl.semaphore_wait(core_free, 1)
    for_partner(0, 3)
    pl.semaphore_wait(y_free, 2)
    onward(0, 3)
    for_partner(1, 3)
    onward(1, 3)
    for_partner(2, 3)
    for block in waiting:
        backward(*block)
    for h in range(3):
        cols = slice(h * 128, (h + 1) * 128)
        grads_ref[1, cols, :] = key_acc[h].astype(BF16)
        grads_ref[2, cols, :] = value_acc[h].astype(BF16)
    for_partner(0, 0, 2)
    onward(0, 0)
    onward(0, 2)
    for_partner(0, 1)
    for_partner(2, 0)
    onward(0, 1)
    onward(2, 3)
    for_partner(1, 2)
    onward(2, 0)
    onward(1, 2)
    for_partner(2, 1)
    for_partner(1, 0, 1)
    onward(2, 1)
    for_partner(2, 2)
    for_partner(3, 3, 0, 1, 2)
    onward(1, 0)
    onward(2, 2)
    onward(1, 1)
    for g in (3, 2, 0, 1):
        part[g] = summed(3, g)
    ends = []
    for n, g in enumerate((3, 2, 0, 1)):
        y_copies[1, g].wait_recv()
        y_copies[2, g].wait_recv()
        part[g] += landed_unit(1, g) + landed_unit(2, g)
        target = grad_in_hbm.at[g] if g < 3 else grad_out_hbm
        ends.append(pltpu.make_async_copy(part.at[g], target, end_sems.at[n]))
        ends[-1].start()
    for copy in gm_copies + list(core_copies.values()) + list(y_copies.values()):
        copy.wait_send()
    gather.finish()
    gather_up.finish()

    @pl.when(p.t < 7)
    def _():
        for move in moves:
            move.wait_send()

    for copy in ends:
        copy.wait()


def attend(scale, time, x, drift, table, w, wo, bound):
    vmem = pl.BlockSpec(memory_space=pltpu.VMEM)
    smem = pl.BlockSpec(memory_space=pltpu.SMEM)
    hbm = pl.BlockSpec(memory_space=pl.ANY)
    dma = pltpu.SemaphoreType.DMA
    return pl.pallas_call(
        attend_kernel,
        out_shape=(
            jax.ShapeDtypeStruct((3, 3, 128, 384), F32),
            jax.ShapeDtypeStruct((3, 128, 384), F32),
        ),
        in_specs=[smem, smem, vmem, vmem, hbm, hbm, hbm, hbm, hbm],
        out_specs=(hbm, hbm),
        scratch_shapes=[
            pltpu.VMEM((3, 384, 1024), BF16),
            pltpu.VMEM((8, 128, 384), BF16),
            pltpu.VMEM((384, 1024), BF16),
            pltpu.VMEM((3, 3072, 384), BF16),
            pltpu.VMEM((384, 3072), BF16),
            pltpu.VMEM((128, 3072), BF16),
            pltpu.VMEM((8, 128, 3072), BF16),
            pltpu.VMEM((8, 128, 3072), BF16),
            pltpu.VMEM((2, 128, 3072), BF16),
            pltpu.VMEM((8, 3, 128, 384), F32),
            pltpu.VMEM((8, 3, 128, 384), BF16),
            pltpu.VMEM((8, 3, 128, 384), BF16),
            pltpu.VMEM((3, 8, 128, 1024), BF16),
            pltpu.VMEM((7, 128, 3072), BF16),
            pltpu.VMEM((2, 4, 64, 1536), BF16),
            pltpu.VMEM((2, 6, 128, 1536), BF16),
            pltpu.VMEM((8, 128, 384), BF16),
            pltpu.VMEM((3, 128, 1024), F32),
            pltpu.VMEM((3, 128, 1024), F32),
            dma((3,)),
            dma((2,)),
            dma((2,)),
            dma((20,)),
            dma((20,)),
            dma((20,)),
            dma((20,)),
            dma((8,)),
            dma((8,)),
            dma((8,)),
            dma((8,)),
            dma((2,)),
            dma((2,)),
            dma((2,)),
            dma((20,)),
            dma((20,)),
            dma((8,)),
            dma((8,)),
            dma((16,)),
            dma((16,)),
            dma((12,)),
            dma((12,)),
            dma((4,)),
            pltpu.SemaphoreType.REGULAR,
            pltpu.SemaphoreType.REGULAR,
        ],
        name="attend",
        cost_estimate=pl.CostEstimate(
            flops=30_000_000_000, bytes_accessed=30_000_000, transcendentals=3 * 1024 * 1024
        ),
        compiler_params=pltpu.CompilerParams(
            collective_id=2, has_side_effects=True, vmem_limit_bytes=VMEM_LIMIT
        ),
    )(scale, time, x, table, w, wo, x, drift, bound)


def body(paths, prev_drift, boundary, step_scale, time_ids, mod_table, w_qkv, output_weight):
    w = jnp.transpose(w_qkv, (1, 0, 2))
    grad_in_sum, grad_out_sum = attend(
        step_scale, time_ids, paths[0], prev_drift[0], mod_table, w, output_weight, boundary
    )
    grad_in_sum = jnp.transpose(grad_in_sum.reshape(3, 384, 384), (1, 0, 2))
    grad_out_sum = grad_out_sum.reshape(384, 384)
    return (grad_in_sum, grad_out_sum)


def solution(mesh):
    placed = (
        P("tm", "row", "col"),
        P("tm", "row", "col"),
        P(None, "row", "col"),
        P("tm"),
        P("tm"),
        P(None, None, "col"),
        P("col", None, "row"),
        P("row", "col"),
    )
    return jax.shard_map(
        body,
        mesh=mesh,
        in_specs=placed,
        out_specs=(P(("col", "tm"), None, "row"), P("row", ("col", "tm"))),
        check_vma=False,
    )
```
